32 devices in a mesh: img: 16 (over z, x, core), seq: 2 (over y).
Axes of the slice: x: 2, y: 2, z: 4, core: 2. Of those that a mesh axis runs over, the one named last changes fastest.
Arguments:
- patches: bfloat16 [64, 1024, 768], P('img', 'seq'), may hold values from -6 to 6
- lengths: int32 [64], P('img'), may hold values from 192 to 1024, as said below
- pooled_cot: float32 [64, 768], P('img'), may hold values from -6 to 6
- norm1_gain: bfloat16 [768], P(('img', 'seq')), may hold values from 0.5 to 1.5
- norm1_bias: bfloat16 [768], P(('img', 'seq')), may hold values from -1.75 to 1.75
- qkv_weight: bfloat16 [768, 2304], P(('img', 'seq')), may hold values from -0.21875 to 0.21875
- query_bias: bfloat16 [768], P(('img', 'seq')), may hold values from -1.75 to 1.75
- value_bias: bfloat16 [768], P(('img', 'seq')), may hold values from -1.75 to 1.75
- attn_weight: bfloat16 [768, 768], P(('img', 'seq')), may hold values from -1.25 to 1.25
- attn_bias: bfloat16 [768], P(('img', 'seq')), may hold values from -1.75 to 1.75
- norm2_gain: bfloat16 [768], P(('img', 'seq')), may hold values from 0.5 to 1.5
- norm2_bias: bfloat16 [768], P(('img', 'seq')), may hold values from -1.75 to 1.75
- fc1_weight: bfloat16 [768, 3072], P(('img', 'seq')), may hold values from -0.21875 to 0.21875
- fc1_bias: bfloat16 [3072], P(('img', 'seq')), may hold values from -1.75 to 1.75
- fc2_weight: bfloat16 [3072, 768], P(('img', 'seq')), may hold values from -0.109375 to 0.109375
- fc2_bias: bfloat16 [768], P(('img', 'seq')), may hold values from -1.75 to 1.75
- final_gain: bfloat16 [768], P(('img', 'seq')), may hold values from 0.5 to 1.5
- final_bias: bfloat16 [768], P(('img', 'seq')), may hold values from -1.75 to 1.75
- probe_vector: bfloat16 [768], P(('img', 'seq')), may hold values from -6 to 6
- pool_query_weight: bfloat16 [768, 768], P(('img', 'seq')), may hold values from -0.21875 to 0.21875
- pool_query_bias: bfloat16 [768], P(('img', 'seq')), may hold values from -1.75 to 1.75
- pool_kv_weight: bfloat16 [768, 1536], P(('img', 'seq')), may hold values from -0.21875 to 0.21875
- pool_value_bias: bfloat16 [768], P(('img', 'seq')), may hold values from -1.75 to 1.75
- pool_out_weight: bfloat16 [768, 768], P(('img', 'seq')), may hold values from -1.25 to 1.25
- pool_out_bias: bfloat16 [768], P(('img', 'seq')), may hold values from -1.75 to 1.75
- head_gain: bfloat16 [768], P(('img', 'seq')), may hold values from 0.5 to 1.5
- head_bias: bfloat16 [768], P(('img', 'seq')), may hold values from -1.75 to 1.75
- head_fc1_weight: bfloat16 [768, 3072], P(('img', 'seq')), may hold values from -0.21875 to 0.21875
- head_fc1_bias: bfloat16 [3072], P(('img', 'seq')), may hold values from -1.75 to 1.75
- head_fc2_weight: bfloat16 [3072, 768], P(('img', 'seq')), may hold values from -0.109375 to 0.109375
- head_fc2_bias: bfloat16 [768], P(('img', 'seq')), may hold values from -1.75 to 1.75
Outputs:
- pooled: float32 [64, 768], P('img')
- patch_grad: float32 [64, 1024, 768], P('img', 'seq')
- grad_norm1_gain: float32 [768], P(('img', 'seq'))
- grad_norm1_bias: float32 [768], P(('img', 'seq'))
- grad_qkv_weight: float32 [768, 2304], P(('img', 'seq'))
- grad_query_bias: float32 [768], P(('img', 'seq'))
- grad_value_bias: float32 [768], P(('img', 'seq'))
- grad_attn_weight: float32 [768, 768], P(('img', 'seq'))
- grad_attn_bias: float32 [768], P(('img', 'seq'))
- grad_norm2_gain: float32 [768], P(('img', 'seq'))
- grad_norm2_bias: float32 [768], P(('img', 'seq'))
- grad_fc1_weight: float32 [768, 3072], P(('img', 'seq'))
- grad_fc1_bias: float32 [3072], P(('img', 'seq'))
- grad_fc2_weight: float32 [3072, 768], P(('img', 'seq'))
- grad_fc2_bias: float32 [768], P(('img', 'seq'))
- grad_final_gain: float32 [768], P(('img', 'seq'))
- grad_final_bias: float32 [768], P(('img', 'seq'))
- grad_probe_vector: float32 [768], P(('img', 'seq'))
- grad_pool_query_weight: float32 [768, 768], P(('img', 'seq'))
- grad_pool_query_bias: float32 [768], P(('img', 'seq'))
- grad_pool_kv_weight: float32 [768, 1536], P(('img', 'seq'))
- grad_pool_value_bias: float32 [768], P(('img', 'seq'))
- grad_pool_out_weight: float32 [768, 768], P(('img', 'seq'))
- grad_pool_out_bias: float32 [768], P(('img', 'seq'))
- grad_head_gain: float32 [768], P(('img', 'seq'))
- grad_head_bias: float32 [768], P(('img', 'seq'))
- grad_head_fc1_weight: float32 [768, 3072], P(('img', 'seq'))
- grad_head_fc1_bias: float32 [3072], P(('img', 'seq'))
- grad_head_fc2_weight: float32 [3072, 768], P(('img', 'seq'))
- grad_head_fc2_bias: float32 [768], P(('img', 'seq'))
The draws below stay inside these ranges and needn't reach their ends.
Inputs may be any that keep to these rules, and one draw needn't show every extreme that they name: `lengths`: valid patches of each image; positions from the count on are padding.
All inputs are finite; a program needn't handle non-finite values.
Results may differ from the reference program's by a relative error of at most 0.024.
Values may be sent and summed in bfloat16 or wider, within the bound.
No kernel may reach another device: no remote copies, remote signals or barrier semaphores. Data moves between devices by JAX's collectives and lax.ppermute only.
A program may use at most 320 MiB of HBM per device.

```python
import jax
import jax.numpy as jnp
from jax import lax

D = 768
FF = 3072
HEADS = 12
LEN = 1024
IMAGES = 64


def draw_lengths(key, part):
    shortest = LEN * 3 // 16
    spread_key, other_key, third_key, long_key, short_key = jax.random.split(key, 5)
    first = jax.random.randint(spread_key, (IMAGES,), 0, LEN - shortest + 1)
    second = jax.random.randint(other_key, (IMAGES,), 0, LEN - shortest + 1)
    third = jax.random.randint(third_key, (IMAGES,), 0, LEN - shortest + 1)
    counts = shortest + (first + jnp.minimum(second, third)) // 2
    long_index = jax.random.randint(long_key, (), 0, IMAGES)
    short_index = (long_index + 1 + jax.random.randint(short_key, (), 0, IMAGES - 1)) % IMAGES
    counts = counts.at[long_index].set(LEN)
    counts = counts.at[short_index].set(shortest)
    return counts.astype(jnp.int32)


def level_of(own_key, extent, cuts, low, largest):
    def one(axis_at, blocks):
        steps = jax.random.uniform(jax.random.fold_in(jax.random.fold_in(own_key, 6), axis_at), (blocks,), jnp.float32, low / len(cuts), largest / len(cuts))
        return jnp.repeat(jnp.exp(steps), extent[axis_at] // blocks).reshape((-1,) + (1,) * (len(extent) - axis_at - 1))

    factor_of = one(*cuts[0])
    for cut in cuts[1:]:
        factor_of = factor_of * one(*cut)
    return factor_of


def noise(rng, dims, deviation, most, cuts=(), dtype=jnp.bfloat16):
    values = jax.random.normal(rng, dims, jnp.float32) * deviation
    if len(cuts) > 0:
        values = level_of(rng, dims, cuts, -0.22, 0.18) * values
    return jnp.clip(values, min=-most, max=most).astype(dtype)


def setup_inputs(seed: int = 0) -> dict:
    arg_keys = jax.random.split(jax.random.key(seed), 32)
    patches = noise(arg_keys[0], (IMAGES, LEN, D), 1.0, 6.0, ((0, 16), (1, 2)))
    lengths = draw_lengths(jax.random.fold_in(arg_keys[31], 71), 0)
    pooled_cot = noise(arg_keys[2], (IMAGES, D), 1.0, 6.0, ((0, 16),), jnp.float32)
    norm1_gain = jnp.clip(1.0 + 0.1 * jax.random.normal(arg_keys[3], (D,), jnp.float32), 0.5, 1.5).astype(jnp.bfloat16)
    norm1_bias = noise(arg_keys[4], (D,), 0.3, 1.75, ((0, 32),))
    qkv_weight = noise(arg_keys[5], (D, 3 * D), D ** -0.5, 0.21875, ((0, 32),))
    query_bias = noise(arg_keys[6], (D,), 0.3, 1.75, ((0, 32),))
    value_bias = noise(arg_keys[7], (D,), 0.3, 1.75, ((0, 32),))
    attn_weight = noise(arg_keys[8], (D, D), (D // 32) ** -0.5, 1.25, ((0, 32),))
    attn_bias = noise(arg_keys[9], (D,), 0.3, 1.75, ((0, 32),))
    norm2_gain = jnp.clip(1.0 + 0.1 * jax.random.normal(arg_keys[10], (D,), jnp.float32), 0.5, 1.5).astype(jnp.bfloat16)
    norm2_bias = noise(arg_keys[11], (D,), 0.3, 1.75, ((0, 32),))
    fc1_weight = noise(arg_keys[12], (D, FF), D ** -0.5, 0.21875, ((0, 32),))
    fc1_bias = noise(arg_keys[13], (FF,), 0.3, 1.75, ((0, 32),))
    fc2_weight = noise(arg_keys[14], (FF, D), FF ** -0.5, 0.109375, ((0, 32),))
    fc2_bias = noise(arg_keys[15], (D,), 0.3, 1.75, ((0, 32),))
    final_gain = jnp.clip(1.0 + 0.1 * jax.random.normal(arg_keys[16], (D,), jnp.float32), 0.5, 1.5).astype(jnp.bfloat16)
    final_bias = noise(arg_keys[17], (D,), 0.3, 1.75, ((0, 32),))
    probe_vector = noise(arg_keys[18], (D,), 1.0, 6.0, ((0, 32),))
    pool_query_weight = noise(arg_keys[19], (D, D), D ** -0.5, 0.21875, ((0, 32),))
    pool_query_bias = noise(arg_keys[20], (D,), 0.3, 1.75, ((0, 32),))
    pool_kv_weight = noise(arg_keys[21], (D, 2 * D), D ** -0.5, 0.21875, ((0, 32),))
    pool_value_bias = noise(arg_keys[22], (D,), 0.3, 1.75, ((0, 32),))
    pool_out_weight = noise(arg_keys[23], (D, D), (D // 32) ** -0.5, 1.25, ((0, 32),))
    pool_out_bias = noise(arg_keys[24], (D,), 0.3, 1.75, ((0, 32),))
    head_gain = jnp.clip(1.0 + 0.1 * jax.random.normal(arg_keys[25], (D,), jnp.float32), 0.5, 1.5).astype(jnp.bfloat16)
    head_bias = noise(arg_keys[26], (D,), 0.3, 1.75, ((0, 32),))
    head_fc1_weight = noise(arg_keys[27], (D, FF), D ** -0.5, 0.21875, ((0, 32),))
    head_fc1_bias = noise(arg_keys[28], (FF,), 0.3, 1.75, ((0, 32),))
    head_fc2_weight = noise(arg_keys[29], (FF, D), FF ** -0.5, 0.109375, ((0, 32),))
    head_fc2_bias = noise(arg_keys[30], (D,), 0.3, 1.75, ((0, 32),))
    return dict(patches=patches, lengths=lengths, pooled_cot=pooled_cot, norm1_gain=norm1_gain, norm1_bias=norm1_bias, qkv_weight=qkv_weight, query_bias=query_bias, value_bias=value_bias, attn_weight=attn_weight, attn_bias=attn_bias, norm2_gain=norm2_gain, norm2_bias=norm2_bias, fc1_weight=fc1_weight, fc1_bias=fc1_bias, fc2_weight=fc2_weight, fc2_bias=fc2_bias, final_gain=final_gain, final_bias=final_bias, probe_vector=probe_vector, pool_query_weight=pool_query_weight, pool_query_bias=pool_query_bias, pool_kv_weight=pool_kv_weight, pool_value_bias=pool_value_bias, pool_out_weight=pool_out_weight, pool_out_bias=pool_out_bias, head_gain=head_gain, head_bias=head_bias, head_fc1_weight=head_fc1_weight, head_fc1_bias=head_fc1_bias, head_fc2_weight=head_fc2_weight, head_fc2_bias=head_fc2_bias)


@jax.custom_vjp
def low(v):
    return lax.optimization_barrier(v.astype(jnp.bfloat16)).astype(jnp.float32)

@jax.custom_vjp
def low_back(v):
    return v

def low_keep(v):
    return (low(v), None)

def low_pass(kept, grad):
    return (grad,)

def back_keep(v):
    return (v, None)

def back_low(kept, grad):
    return (low(grad),)
low.defvjp(low_keep, low_pass)
low_back.defvjp(back_keep, back_low)
highest = lax.Precision.HIGHEST
masked_score = -1e+30
norm_epsilon = 1e-06

def layer_norm(source, norm_gain, norm_bias):
    centre = lax.optimization_barrier(jnp.mean(source, axis=-1, keepdims=True))
    centred = source - centre
    spread = lax.optimization_barrier(jnp.mean(centred * centred, axis=-1, keepdims=True))
    return centred * lax.rsqrt(spread + norm_epsilon) * norm_gain + norm_bias

def gelu_tanh(source):
    return jax.nn.gelu(source, approximate=True)

def project(source, matrix):
    return jnp.einsum('...d,de->...e', source, matrix, precision=highest)

def forward(weights, images, counts):
    norm1_gain, norm1_bias, qkv_weight, query_bias, value_bias, attn_weight, attn_bias, norm2_gain, norm2_bias, fc1_weight, fc1_bias, fc2_weight, fc2_bias, final_gain, final_bias, probe_vector, pool_query_weight, pool_query_bias, pool_kv_weight, pool_value_bias, pool_out_weight, pool_out_bias, head_gain, head_bias, head_fc1_weight, head_fc1_bias, head_fc2_weight, head_fc2_bias = weights
    pair_count = images.shape[0]
    head_dim = D // HEADS
    positions = jnp.arange(LEN)
    key_valid = positions[None, :] < counts[:, None]
    normed1 = low(layer_norm(images, norm1_gain, norm1_bias))
    qkv_rows = project(normed1, qkv_weight)
    queries = low_back(low(qkv_rows[..., :D] + query_bias))
    key_rows = low_back(low(qkv_rows[..., D:2 * D]))
    values = low_back(low(qkv_rows[..., 2 * D:] + value_bias))
    query_heads = queries.reshape(pair_count, LEN, HEADS, head_dim)
    key_heads = key_rows.reshape(pair_count, LEN, HEADS, head_dim)
    value_heads = values.reshape(pair_count, LEN, HEADS, head_dim)
    scores = low_back(jnp.einsum('pqhd,pkhd->phqk', query_heads, key_heads, precision=highest) * 0.125)
    scores = jnp.where(key_valid[:, None, None, :], scores, masked_score)
    shares = jax.nn.softmax(scores, axis=-1)
    attended = jnp.einsum('phqk,pkhd->pqhd', low(shares), value_heads, precision=highest)
    attended = low_back(low(attended.reshape(pair_count, LEN, D)))
    branch = low_back(project(attended, attn_weight) + attn_bias)
    residual = images + branch
    normed2 = low(layer_norm(residual, norm2_gain, norm2_bias))
    hidden_pre = low_back(project(normed2, fc1_weight) + fc1_bias)
    hidden_act = low(gelu_tanh(hidden_pre))
    encoded = residual + low_back(project(hidden_act, fc2_weight) + fc2_bias)
    final_rows = low(layer_norm(encoded, final_gain, final_bias))
    pool_query = low(project(probe_vector, pool_query_weight) + pool_query_bias)
    pool_kv = project(final_rows, pool_kv_weight)
    pool_keys = low_back(low(pool_kv[..., :D])).reshape(pair_count, LEN, HEADS, head_dim)
    pool_values = low_back(low(pool_kv[..., D:] + pool_value_bias)).reshape(pair_count, LEN, HEADS, head_dim)
    pool_scores = jnp.einsum('hd,plhd->phl', pool_query.reshape(HEADS, head_dim), pool_keys, precision=highest) * 0.125
    pool_scores = jnp.where(key_valid[:, None, :], pool_scores, masked_score)
    pool_shares = jax.nn.softmax(pool_scores, axis=-1)
    pooled_heads = jnp.einsum('phl,plhd->phd', pool_shares, pool_values, precision=highest).reshape(pair_count, D)
    pool_branch = low_back(project(low(pooled_heads), pool_out_weight) + pool_out_bias)
    head_normed = low(layer_norm(pool_branch, head_gain, head_bias))
    head_pre = low_back(project(head_normed, head_fc1_weight) + head_fc1_bias)
    head_act = low(gelu_tanh(head_pre))
    return pool_branch + low_back(project(head_act, head_fc2_weight) + head_fc2_bias)

def reference(patches, lengths, pooled_cot, norm1_gain, norm1_bias, qkv_weight, query_bias, value_bias, attn_weight, attn_bias, norm2_gain, norm2_bias, fc1_weight, fc1_bias, fc2_weight, fc2_bias, final_gain, final_bias, probe_vector, pool_query_weight, pool_query_bias, pool_kv_weight, pool_value_bias, pool_out_weight, pool_out_bias, head_gain, head_bias, head_fc1_weight, head_fc1_bias, head_fc2_weight, head_fc2_bias):
    weights = tuple((matrix.astype(jnp.float32) for matrix in (norm1_gain, norm1_bias, qkv_weight, query_bias, value_bias, attn_weight, attn_bias, norm2_gain, norm2_bias, fc1_weight, fc1_bias, fc2_weight, fc2_bias, final_gain, final_bias, probe_vector, pool_query_weight, pool_query_bias, pool_kv_weight, pool_value_bias, pool_out_weight, pool_out_bias, head_gain, head_bias, head_fc1_weight, head_fc1_bias, head_fc2_weight, head_fc2_bias)))
    images = patches.astype(jnp.float32).reshape(IMAGES // 2, 2, LEN, D)
    counts = lengths.reshape(IMAGES // 2, 2)
    cotangent = pooled_cot.astype(jnp.float32).reshape(IMAGES // 2, 2, D)

    def scan_step(totals, inputs):
        pair_images, pair_counts, pair_cot = inputs

        def bound_forward(weight_set, image_set):
            return forward(weight_set, image_set, pair_counts)
        result, pullback = jax.vjp(bound_forward, weights, pair_images)
        weight_grads, image_grads = pullback(pair_cot)
        totals = jax.tree.map(jnp.add, totals, weight_grads)
        return (totals, (result, image_grads))
    zero_grads = jax.tree.map(jnp.zeros_like, weights)
    totals, (pooled, patch_grad) = lax.scan(scan_step, zero_grads, (images, counts, cotangent))
    return (pooled.reshape(IMAGES, D), patch_grad.reshape(IMAGES, LEN, D), totals[0], totals[1], totals[2], totals[3], totals[4], totals[5], totals[6], totals[7], totals[8], totals[9], totals[10], totals[11], totals[12], totals[13], totals[14], totals[15], totals[16], totals[17], totals[18], totals[19], totals[20], totals[21], totals[22], totals[23], totals[24], totals[25], totals[26], totals[27])
```

```python
import functools

import jax
import jax.numpy as jnp
from jax import lax
from jax.experimental import pallas as pl
from jax.experimental.pallas import tpu as pltpu
from jax.sharding import PartitionSpec as P

HEADS = 12
HEAD_DIM = 64
BLOCK = 256
PAIR = 128
wide = jnp.float32
low = jnp.bfloat16
masked_score = -1e30
norm_epsilon = 1e-06
root_two_pi = 0.7978845608028654
vmem_bytes = 60 * 1024 * 1024


def dot_nn(a, b):
    return jnp.dot(a, b, preferred_element_type=wide)


def dot_nt(a, b):
    return lax.dot_general(a, b, (((1,), (1,)), ((), ())), preferred_element_type=wide)


def dot_tn(a, b):
    return lax.dot_general(a, b, (((0,), (0,)), ((), ())), preferred_element_type=wide)


def halves(v):
    top = v.astype(low)
    return top, (v - top.astype(wide)).astype(low)


def normalise(v):
    centred = v - jnp.mean(v, axis=-1, keepdims=True)
    spread = jnp.mean(centred * centred, axis=-1, keepdims=True)
    scale = lax.rsqrt(spread + norm_epsilon)
    return centred * scale, scale


def norm_back(grad, gain, normal, scale):
    gn = grad * gain
    return (
        gn
        - jnp.mean(gn, axis=-1, keepdims=True)
        - normal * jnp.mean(gn * normal, axis=-1, keepdims=True)
    ) * scale


def column_sum(v):
    return jnp.sum(v, axis=0, keepdims=True)


def params(rank):
    return pltpu.CompilerParams(
        dimension_semantics=("arbitrary",) * rank, vmem_limit_bytes=vmem_bytes
    )


def whole(shape):
    return pl.BlockSpec(
        shape, lambda *_: (0,) * len(shape), pipeline_mode=pl.Buffered(1)
    )


def cost(flops, nbytes, exps=0):
    return pl.CostEstimate(flops=int(flops), bytes_accessed=int(nbytes), transcendentals=int(exps))


class Sizes:
    def __init__(self, images, length, width, hidden):
        self.images, self.length, self.width, self.hidden = images, length, width, hidden
        self.rows = images * length
        self.blocks = length // BLOCK
        self.pairs = width // PAIR

    def row_spec(self, cols):
        blocks = self.blocks

        def index(i, b, meta):
            return i * blocks + jnp.clip(b, 0, jnp.maximum(meta[i] - 1, 0)), 0

        return pl.BlockSpec((BLOCK, cols), index)

    def lane_spec(self, rows):
        def index(i, b, meta):
            return i, 0, jnp.clip(b, 0, jnp.maximum(meta[i] - 1, 0))

        return pl.BlockSpec((1, rows, BLOCK), index)

    def image_spec(self, rows, cols):
        return pl.BlockSpec((1, rows, cols), lambda i, b, meta: (i, 0, 0))


(
    NORM1_GAIN,
    NORM1_BIAS,
    QUERY_BIAS,
    VALUE_BIAS,
    ATTN_BIAS,
    NORM2_GAIN,
    NORM2_BIAS,
    FC2_BIAS,
    FINAL_GAIN,
    FINAL_BIAS,
    POOL_QUERY_BIAS,
    POOL_VALUE_BIAS,
    POOL_OUT_BIAS,
    HEAD_GAIN,
    HEAD_BIAS,
    HEAD_FC2_BIAS,
) = range(16)


def row_of(ref, at):
    return ref[at : at + 1, :]


def qkv_body(meta, x, vec, weight, qkv, normed):
    @pl.when(pl.program_id(1) < meta[pl.program_id(0)])
    def _():
        width = x.shape[1]
        normal, _ = normalise(x[...].astype(wide))
        rows = (normal * row_of(vec, NORM1_GAIN) + row_of(vec, NORM1_BIAS)).astype(low)
        normed[...] = rows
        for part, bias in enumerate((QUERY_BIAS, None, VALUE_BIAS)):
            cols = slice(part * width, (part + 1) * width)
            out = dot_nn(rows, weight[:, cols])
            if bias is not None:
                out = out + row_of(vec, bias)
            qkv[:, cols] = out.astype(low)


def qkv_call(sz, meta, x, vec, weight):
    w = sz.width
    return pl.pallas_call(
        qkv_body,
        grid_spec=pltpu.PrefetchScalarGridSpec(
            num_scalar_prefetch=1,
            grid=(sz.images, sz.blocks),
            in_specs=[sz.row_spec(w), whole(vec.shape), whole(weight.shape)],
            out_specs=[sz.row_spec(3 * w), sz.row_spec(w)],
        ),
        out_shape=[
            jax.ShapeDtypeStruct((sz.rows, 3 * w), low),
            jax.ShapeDtypeStruct((sz.rows, w), low),
        ],
        compiler_params=params(2),
        cost_estimate=cost(6 * sz.rows * w * w, sz.rows * w * 10 + 6 * w * w),
        name="qkv",
    )(meta, x, vec, weight)


def attend_body(images, blocks, meta, q_ref, k_ref, v_ref, out_ref, lse_ref):
    at = pl.program_id(0)
    count, length = meta[at], meta[images + at]
    lane = lax.broadcasted_iota(jnp.int32, (BLOCK, PAIR), 1)
    first = lane < HEAD_DIM

    def variant(keys_in):
        near = keys_in - BLOCK
        column = lax.broadcasted_iota(jnp.int32, (BLOCK, BLOCK), 1) + near

        @pl.loop(0, count)
        def _(step):
            rows = pl.ds(pl.multiple_of(step * BLOCK, BLOCK), BLOCK)
            q = q_ref[rows, :]
            outs, logs = [], []
            for head in range(2):
                own = first if head == 0 else jnp.logical_not(first)
                qh = jnp.where(own, q, jnp.zeros_like(q))
                last = dot_nt(qh, k_ref[near:keys_in, :]) * 0.125
                last = jnp.where(column < length, last, masked_score)
                top = jnp.max(last, axis=1, keepdims=True)
                if near:
                    body = dot_nt(qh, k_ref[:near, :]) * 0.125
                    top = jnp.maximum(top, jnp.max(body, axis=1, keepdims=True))
                p_last = jnp.exp(last - top)
                total = jnp.sum(p_last, axis=1, keepdims=True)
                acc = dot_nn(p_last.astype(low), v_ref[near:keys_in, :])
                if near:
                    p_body = jnp.exp(body - top)
                    total = total + jnp.sum(p_body, axis=1, keepdims=True)
                    acc = acc + dot_nn(p_body.astype(low), v_ref[:near, :])
                outs.append(acc / total)
                logs.append(top + jnp.log(total))
            out_ref[rows, :] = jnp.where(first, outs[0], outs[1]).astype(low)
            both = jnp.where(lane == 0, logs[0], logs[1])
            lse_ref[0, :, rows] = both.T[:8, :]

    for keys in range(1, blocks + 1):
        pl.when(count == keys)(functools.partial(variant, keys * BLOCK))


def attend_call(sz, meta, qkv):
    pairs = sz.pairs

    def spec(part):
        return pl.BlockSpec((sz.length, PAIR), lambda i, p, m: (i, part * pairs + p))

    return pl.pallas_call(
        functools.partial(attend_body, sz.images, sz.blocks),
        grid_spec=pltpu.PrefetchScalarGridSpec(
            num_scalar_prefetch=1,
            grid=(sz.images, pairs),
            in_specs=[spec(0), spec(1), spec(2)],
            out_specs=[
                pl.BlockSpec((sz.length, PAIR), lambda i, p, m: (i, p)),
                pl.BlockSpec((1, 8, sz.length), lambda i, p, m: (i, p, 0)),
            ],
        ),
        out_shape=[
            jax.ShapeDtypeStruct((sz.rows, sz.width), low),
            jax.ShapeDtypeStruct((sz.images, 8 * pairs, sz.length), wide),
        ],
        compiler_params=params(2),
        cost_estimate=cost(
            4 * sz.rows * sz.length * sz.width,
            8 * sz.rows * sz.width,
            sz.rows * sz.length * HEADS,
        ),
        name="attend",
    )(meta, qkv, qkv, qkv)


def mlp_body(meta, x, att, vec, fcb, attn_w, fc1, fc2, res, n2, slope, act, enc, fin):
    @pl.when(pl.program_id(1) < meta[pl.program_id(0)])
    def _():
        width = x.shape[1]
        branch = dot_nn(att[...], attn_w[...]) + row_of(vec, ATTN_BIAS)
        rows = x[...].astype(wide) + branch
        res[...] = rows
        normal, _ = normalise(rows)
        normed = (normal * row_of(vec, NORM2_GAIN) + row_of(vec, NORM2_BIAS)).astype(low)
        n2[...] = normed
        total = rows + row_of(vec, FC2_BIAS)
        for part in range(fc1.shape[1] // width):
            cols = slice(part * width, (part + 1) * width)
            u = dot_nn(normed, fc1[:, cols]) + fcb[0:1, cols]
            square = u * u
            bend = jnp.tanh(root_two_pi * u * (1.0 + 0.044715 * square))
            half = 0.5 * (1.0 + bend)
            hidden = (u * half).astype(low)
            slope[:, cols] = (
                half
                + (0.5 * root_two_pi) * u * (1.0 - bend * bend) * (1.0 + 0.134145 * square)
            ).astype(low)
            act[:, cols] = hidden
            total = total + dot_nn(hidden, fc2[cols, :])
        enc[...] = total
        normal, _ = normalise(total)
        fin[...] = (normal * row_of(vec, FINAL_GAIN) + row_of(vec, FINAL_BIAS)).astype(low)


def mlp_call(sz, meta, x, att, vec, fcb, attn_w, fc1, fc2):
    w, f = sz.width, sz.hidden
    return pl.pallas_call(
        mlp_body,
        grid_spec=pltpu.PrefetchScalarGridSpec(
            num_scalar_prefetch=1,
            grid=(sz.images, sz.blocks),
            in_specs=[sz.row_spec(w), sz.row_spec(w)]
            + [whole(v.shape) for v in (vec, fcb, attn_w, fc1, fc2)],
            out_specs=[sz.row_spec(c) for c in (w, w, f, f, w, w)],
        ),
        out_shape=[
            jax.ShapeDtypeStruct((sz.rows, w), wide),
            jax.ShapeDtypeStruct((sz.rows, w), low),
            jax.ShapeDtypeStruct((sz.rows, f), low),
            jax.ShapeDtypeStruct((sz.rows, f), low),
            jax.ShapeDtypeStruct((sz.rows, w), wide),
            jax.ShapeDtypeStruct((sz.rows, w), low),
        ],
        compiler_params=params(2),
        cost_estimate=cost(
            sz.rows * w * (2 * w + 4 * f), sz.rows * (14 * w + 4 * f) + 4 * w * f, sz.rows * f
        ),
        name="mlp",
    )(meta, x, att, vec, fcb, attn_w, fc1, fc2)


HEAD_ROWS = 16


def head_body(
    images, blocks, meta, fin, probe_w, cot_ref, vec, fcb, pool_v, pool_out, fc1, fc2,
    pooled_ref, shares, lift, drop, outer, wide_rows, narrow_rows, sums, score,
):
    width, hidden = pool_out.shape[0], fc1.shape[1]
    head_row = lax.broadcasted_iota(jnp.int32, (HEAD_ROWS, width), 0)
    head_col = lax.broadcasted_iota(jnp.int32, (HEAD_ROWS, width), 1) // HEAD_DIM
    own = head_row == head_col
    row_id = lax.broadcasted_iota(jnp.int32, (HEAD_ROWS, 1), 0)
    probe_top, probe_rest = halves(probe_w[...])
    pooled_heads = jnp.zeros((HEAD_ROWS, width), wide)
    for i in range(images):
        count, length = meta[i], meta[images + i]
        base = i * blocks * BLOCK
        for b in range(blocks):
            cols = slice(b * BLOCK, (b + 1) * BLOCK)
            score[:, cols] = jnp.full((HEAD_ROWS, BLOCK), masked_score, wide)

            @pl.when(b < count)
            def _(b=b, cols=cols, base=base, length=length):
                rows = fin[base + b * BLOCK : base + (b + 1) * BLOCK, :]
                value = dot_nt(probe_top, rows) + dot_nt(probe_rest, rows)
                column = lax.broadcasted_iota(jnp.int32, (HEAD_ROWS, BLOCK), 1) + b * BLOCK
                score[:, cols] = jnp.where(column < length, value, masked_score)

        raised = jnp.exp(score[...] - jnp.max(score[...], axis=1, keepdims=True))
        share = raised / jnp.sum(raised, axis=1, keepdims=True)
        shares[i] = share
        lift[i] = jnp.zeros((HEAD_ROWS, width), wide)
        for b in range(blocks):
            cols = slice(b * BLOCK, (b + 1) * BLOCK)

            @pl.when(b < count)
            def _(b=b, cols=cols, base=base, i=i):
                rows = fin[base + b * BLOCK : base + (b + 1) * BLOCK, :]
                top, rest = halves(shares[i, :, cols])
                lift[i] += dot_nn(top, rows) + dot_nn(rest, rows)

        mixed = lift[i]
        outer[i] = mixed.astype(low)
        top, rest = halves(mixed)
        heads = dot_nn(top, pool_v[...]) + dot_nn(rest, pool_v[...])
        row = column_sum(jnp.where(own, heads, 0.0)) + row_of(vec, POOL_VALUE_BIAS)
        pooled_heads = jnp.where(row_id == i, row, pooled_heads)
    real = row_id < jnp.where(meta[0] > 0, images, 0)
    cot = jnp.where(real, cot_ref[...], 0.0)
    pooled_low = pooled_heads.astype(low)
    branch = dot_nn(pooled_low, pool_out[...]) + row_of(vec, POOL_OUT_BIAS)
    normal, scale = normalise(branch)
    gain = row_of(vec, HEAD_GAIN)
    normed = (normal * gain + row_of(vec, HEAD_BIAS)).astype(low)
    cot_low = cot.astype(low)
    total = branch + row_of(vec, HEAD_FC2_BIAS)
    back = jnp.zeros((HEAD_ROWS, width), wide)
    for part in range(hidden // width):
        cols = slice(part * width, (part + 1) * width)
        u = dot_nn(normed, fc1[:, cols]) + fcb[1:2, cols]
        square = u * u
        bend = jnp.tanh(root_two_pi * u * (1.0 + 0.044715 * square))
        half = 0.5 * (1.0 + bend)
        act = (u * half).astype(low)
        slope = half + (0.5 * root_two_pi) * u * (1.0 - bend * bend) * (1.0 + 0.134145 * square)
        total = total + dot_nn(act, fc2[cols, :])
        grad = jnp.where(real, dot_nt(cot_low, fc2[cols, :]) * slope, 0.0).astype(low)
        back = back + dot_nt(grad, fc1[:, cols])
        narrow_rows[:, cols] = act
        wide_rows[:, cols] = grad
    pooled_ref[...] = total
    sums[0:1, :] = column_sum(jnp.where(real, back * normal, 0.0))
    sums[1:2, :] = column_sum(jnp.where(real, back, 0.0))
    branch_grad = jnp.where(real, cot + norm_back(back, gain, normal, scale), 0.0).astype(low)
    pooled_grad = dot_nt(branch_grad, pool_out[...])
    narrow_rows[:, hidden : hidden + width] = normed
    narrow_rows[:, hidden + width : hidden + 2 * width] = pooled_low
    wide_rows[:, hidden : hidden + width] = branch_grad
    wide_rows[:, hidden + width : hidden + 2 * width] = pooled_grad.astype(low)
    wide_rows[:, hidden + 2 * width : hidden + 3 * width] = cot_low
    for i in range(images):
        spread = jnp.where(own, pooled_grad[i : i + 1, :], 0.0)
        top, rest = halves(spread)
        raised = dot_nt(top, pool_v[...]) + dot_nt(rest, pool_v[...])
        both = jnp.sum(raised * lift[i], axis=1, keepdims=True)
        drop[i] = jnp.broadcast_to(both, (HEAD_ROWS, PAIR))
        lift[i] = raised


def head_call(sz, meta, fin, probe_w, cot, vec, fcb, pool_v, pool_out, fc1, fc2):
    w, f, n = sz.width, sz.hidden, sz.images

    def out(shape, dtype):
        return jax.ShapeDtypeStruct(shape, dtype)

    shapes = [
        out((HEAD_ROWS, w), wide),
        out((n, HEAD_ROWS, sz.length), wide),
        out((n, HEAD_ROWS, w), wide),
        out((n, HEAD_ROWS, PAIR), wide),
        out((n, HEAD_ROWS, w), low),
        out((HEAD_ROWS, f + 3 * w), low),
        out((HEAD_ROWS, f + 2 * w), low),
        out((8, w), wide),
    ]
    ins = (fin, probe_w, cot, vec, fcb, pool_v, pool_out, fc1, fc2)
    return pl.pallas_call(
        functools.partial(head_body, sz.images, sz.blocks),
        grid_spec=pltpu.PrefetchScalarGridSpec(
            num_scalar_prefetch=1,
            grid=(1,),
            in_specs=[whole(v.shape) for v in ins],
            out_specs=[pl.BlockSpec(s.shape, lambda *_, r=len(s.shape): (0,) * r) for s in shapes],
            scratch_shapes=[pltpu.VMEM((HEAD_ROWS, sz.length), wide)],
        ),
        out_shape=shapes,
        compiler_params=params(1),
        cost_estimate=cost(16 * 8 * w * f, sz.rows * w * 2 + 4 * w * f + 4 * w * w),
        name="head",
    )(meta, *ins)


def back_body(
    meta, fin, enc, res, att, slope, shares, lift, drop, probe_w, spread, vec, attn_w, fc1, fc2,
    g_mlp, g_hidden, g_res, g_branch, g_att, delta, mix, sums, fc1_sum,
):
    @pl.when((pl.program_id(0) == 0) & (pl.program_id(1) == 0))
    def _():
        mix[...] = jnp.zeros_like(mix)
        sums[...] = jnp.zeros_like(sums)
        fc1_sum[...] = jnp.zeros_like(fc1_sum)

    @pl.when(pl.program_id(1) < meta[pl.program_id(0)])
    def _():
        width = fin.shape[1]
        rows = fin[...]
        share = shares[0]
        lift_top, lift_rest = halves(lift[0])
        probe_top, probe_rest = halves(probe_w[...])
        reach = dot_nt(lift_top, rows) + dot_nt(lift_rest, rows)
        g_score = share * (reach - drop[0][:, :1])
        top, rest = halves(g_score)
        mix[...] += dot_nn(top, rows) + dot_nn(rest, rows)
        share_top, share_rest = halves(share)
        left = jnp.concatenate([top, share_top, rest, share_rest, top, share_top], axis=0)
        right = jnp.concatenate(
            [probe_top, lift_top, probe_top, lift_top, probe_rest, lift_rest], axis=0
        )
        g_fin = dot_tn(left, right)
        normal, scale = normalise(enc[...])
        sums[0:1, :] += column_sum(g_fin * normal)
        sums[1:2, :] += column_sum(g_fin)
        g_enc = norm_back(g_fin, row_of(vec, FINAL_GAIN), normal, scale)
        low_enc = g_enc.astype(low)
        g_mlp[...] = low_enc
        sums[2:3, :] += column_sum(low_enc.astype(wide))
        back = jnp.zeros_like(g_enc)
        for part in range(fc1.shape[1] // width):
            cols = slice(part * width, (part + 1) * width)
            grad = (dot_nt(low_enc, fc2[cols, :]) * slope[:, cols].astype(wide)).astype(low)
            g_hidden[:, cols] = grad
            fc1_sum[0:1, cols] += column_sum(grad.astype(wide))
            back = back + dot_nt(grad, fc1[:, cols])
        normal, scale = normalise(res[...])
        sums[3:4, :] += column_sum(back * normal)
        sums[4:5, :] += column_sum(back)
        total = g_enc + norm_back(back, row_of(vec, NORM2_GAIN), normal, scale)
        g_res[...] = total
        low_res = total.astype(low)
        g_branch[...] = low_res
        sums[5:6, :] += column_sum(low_res.astype(wide))
        grad = dot_nt(low_res, attn_w[...]).astype(low)
        g_att[...] = grad
        top, rest = halves(grad.astype(wide) * att[...].astype(wide))
        delta[0] = dot_nt(spread[...], top) + dot_nt(spread[...], rest)


def back_call(
    sz, meta, fin, enc, res, att, slope, shares, lift, drop, probe_w, vec, attn_w, fc1, fc2
):
    w, f, n = sz.width, sz.hidden, sz.images
    lines = 8 * sz.pairs
    line = lax.broadcasted_iota(jnp.int32, (lines, w), 0)
    head = lax.broadcasted_iota(jnp.int32, (lines, w), 1) // HEAD_DIM
    spread = (head == 2 * (line // 8) + line % 8).astype(low)
    fixed = (probe_w, spread, vec, attn_w, fc1, fc2)

    def out(shape, dtype):
        return jax.ShapeDtypeStruct(shape, dtype)

    def kept(shape):
        return pl.BlockSpec(shape, lambda i, b, m: (0, 0))

    return pl.pallas_call(
        back_body,
        grid_spec=pltpu.PrefetchScalarGridSpec(
            num_scalar_prefetch=1,
            grid=(n, sz.blocks),
            in_specs=[
                sz.row_spec(w), sz.row_spec(w), sz.row_spec(w), sz.row_spec(w), sz.row_spec(f),
                sz.lane_spec(HEAD_ROWS), sz.image_spec(HEAD_ROWS, w), sz.image_spec(HEAD_ROWS, PAIR),
            ]
            + [whole(v.shape) for v in fixed],
            out_specs=[
                sz.row_spec(w), sz.row_spec(f), sz.row_spec(w), sz.row_spec(w), sz.row_spec(w),
                sz.lane_spec(lines), kept((HEAD_ROWS, w)), kept((8, w)), kept((8, f)),
            ],
        ),
        out_shape=[
            out((sz.rows, w), low), out((sz.rows, f), low), out((sz.rows, w), wide),
            out((sz.rows, w), low), out((sz.rows, w), low), out((n, lines, sz.length), wide),
            out((HEAD_ROWS, w), wide), out((8, w), wide), out((8, f), wide),
        ],
        compiler_params=params(2),
        cost_estimate=cost(
            sz.rows * w * (2 * w + 4 * f), sz.rows * (22 * w + 4 * f) + 4 * w * f
        ),
        name="mlp_back",
    )(meta, fin, enc, res, att, slope, shares, lift, drop, *fixed)


def outer_body(images, blocks, meta, a_ref, b_ref, out_ref, acc):
    span = blocks * BLOCK
    for i in range(images):
        for keys in range(blocks + 1):

            @pl.when(meta[i] == keys)
            def _(i=i, keys=keys):
                if keys:
                    rows = slice(i * span, i * span + keys * BLOCK)
                    term = dot_tn(a_ref[rows, :], b_ref[rows, :])
                else:
                    term = jnp.zeros(acc.shape, wide)
                if i > 0:
                    term = term + acc[...]
                if i < images - 1:
                    acc[...] = term
                else:
                    out_ref[...] = term.astype(out_ref.dtype)


def outer_call(sz, meta, a, b, tile_m, tile_n, name):
    m, n = a.shape[1], b.shape[1]
    return pl.pallas_call(
        functools.partial(outer_body, sz.images, sz.blocks),
        grid_spec=pltpu.PrefetchScalarGridSpec(
            num_scalar_prefetch=1,
            grid=(m // tile_m, n // tile_n),
            in_specs=[
                pl.BlockSpec((sz.rows, tile_m), lambda i, j, c: (0, i)),
                pl.BlockSpec((sz.rows, tile_n), lambda i, j, c: (0, j)),
            ],
            out_specs=pl.BlockSpec((tile_m, tile_n), lambda i, j, c: (i, j)),
            scratch_shapes=[pltpu.VMEM((tile_m, tile_n), wide)],
        ),
        out_shape=jax.ShapeDtypeStruct((m, n), low),
        compiler_params=params(2),
        cost_estimate=cost(2 * sz.rows * m * n, 2 * sz.rows * (m + n) + 2 * m * n),
        name=name,
    )(meta, a, b)


def attend_back_body(
    images, blocks, meta, q_ref, k_ref, v_ref, g_ref, lse_ref, delta_ref, dq_ref, dk_ref, dv_ref,
    dk_acc, dv_acc,
):
    at = pl.program_id(0)
    count, length = meta[at], meta[images + at]
    lane = lax.broadcasted_iota(jnp.int32, (BLOCK, PAIR), 1)
    first = lane < HEAD_DIM

    def keep(value, head):
        own = first if head == 0 else jnp.logical_not(first)
        zero = jnp.zeros_like(value[:BLOCK])
        return jnp.concatenate(
            [
                jnp.where(own, value[r : r + BLOCK], zero)
                for r in range(0, value.shape[0], BLOCK)
            ],
            axis=0,
        )

    def variant(keys_in):
        near = keys_in - BLOCK
        valid = lax.broadcasted_iota(jnp.int32, (BLOCK, BLOCK), 0) + near < length
        keys = k_ref[:keys_in, :]
        kept_keys = [keep(keys, head) for head in range(2)]
        values = v_ref[:keys_in, :]
        kept_values = [keep(values, head) for head in range(2)]
        dk_acc[:keys_in, :] = jnp.zeros((keys_in, PAIR), wide)
        dv_acc[:keys_in, :] = jnp.zeros((keys_in, PAIR), wide)

        @pl.loop(0, count)
        def _(step):
            rows = pl.ds(pl.multiple_of(step * BLOCK, BLOCK), BLOCK)
            q, g = q_ref[rows, :], g_ref[rows, :]
            dq = None
            for head in range(2):
                log = lse_ref[0, head : head + 1, rows]
                drop = delta_ref[0, head : head + 1, rows]
                score = dot_nt(kept_keys[head], q) * 0.125
                share = jnp.exp(score - log)
                if near:
                    share = jnp.concatenate(
                        [share[:near], jnp.where(valid, share[near:], 0.0)], axis=0
                    )
                else:
                    share = jnp.where(valid, share, 0.0)
                reach = dot_nt(kept_values[head], g)
                grad = (share * (reach - drop)).astype(low)
                dv_acc[:keys_in, :] += dot_nn(share.astype(low), keep(g, head))
                dk_acc[:keys_in, :] += dot_nn(grad, keep(q, head))
                term = dot_tn(grad, kept_keys[head])
                dq = term if dq is None else dq + term
            dq_ref[rows, :] = (dq * 0.125).astype(low)

        dk_ref[:keys_in, :] = (dk_acc[:keys_in, :] * 0.125).astype(low)
        dv_ref[:keys_in, :] = dv_acc[:keys_in, :].astype(low)

    for keys in range(1, blocks + 1):
        pl.when(count == keys)(functools.partial(variant, keys * BLOCK))


def attend_back_call(sz, meta, qkv, g_att, lse, delta):
    pairs = sz.pairs

    def spec(part):
        return pl.BlockSpec((sz.length, PAIR), lambda i, p, m: (i, part * pairs + p))

    line = pl.BlockSpec((1, 8, sz.length), lambda i, p, m: (i, p, 0))
    out = jax.ShapeDtypeStruct((sz.rows, sz.width), low)
    return pl.pallas_call(
        functools.partial(attend_back_body, sz.images, sz.blocks),
        grid_spec=pltpu.PrefetchScalarGridSpec(
            num_scalar_prefetch=1,
            grid=(sz.images, pairs),
            in_specs=[spec(0), spec(1), spec(2), spec(0), line, line],
            out_specs=[spec(0), spec(0), spec(0)],
            scratch_shapes=[pltpu.VMEM((sz.length, PAIR), wide)] * 2,
        ),
        out_shape=[out, out, out],
        compiler_params=params(2),
        cost_estimate=cost(
            10 * sz.rows * sz.length * sz.width,
            14 * sz.rows * sz.width,
            sz.rows * sz.length * HEADS,
        ),
        name="attend_back",
    )(meta, qkv, qkv, qkv, g_att, lse, delta)


def qkv_back_body(meta, x, g_res, dq, dk, dv, vec, weight, grad_ref, sums):
    @pl.when((pl.program_id(0) == 0) & (pl.program_id(1) == 0))
    def _():
        sums[...] = jnp.zeros_like(sums)

    live = pl.program_id(1) < meta[pl.program_id(0)]

    @pl.when(live)
    def _():
        width = x.shape[1]
        normal, scale = normalise(x[...].astype(wide))
        back = None
        for part, ref in enumerate((dq, dk, dv)):
            term = dot_nt(ref[...], weight[:, part * width : (part + 1) * width])
            back = term if back is None else back + term
        sums[0:1, :] += column_sum(back * normal)
        sums[1:2, :] += column_sum(back)
        sums[2:3, :] += column_sum(dq[...].astype(wide))
        sums[3:4, :] += column_sum(dv[...].astype(wide))
        grad_ref[...] = g_res[...] + norm_back(back, row_of(vec, NORM1_GAIN), normal, scale)

    @pl.when(jnp.logical_not(live))
    def _():
        grad_ref[...] = jnp.zeros_like(grad_ref)


def qkv_back_call(sz, meta, x, g_res, dq, dk, dv, vec, weight):
    w, blocks = sz.width, sz.blocks
    return pl.pallas_call(
        qkv_back_body,
        grid_spec=pltpu.PrefetchScalarGridSpec(
            num_scalar_prefetch=1,
            grid=(sz.images, blocks),
            in_specs=[sz.row_spec(w)] * 5 + [whole(vec.shape), whole(weight.shape)],
            out_specs=[
                pl.BlockSpec((BLOCK, w), lambda i, b, m: (i * blocks + b, 0)),
                pl.BlockSpec((8, w), lambda i, b, m: (0, 0)),
            ],
        ),
        out_shape=[
            jax.ShapeDtypeStruct((sz.rows, w), wide),
            jax.ShapeDtypeStruct((8, w), wide),
        ],
        compiler_params=params(2),
        cost_estimate=cost(6 * sz.rows * w * w, sz.rows * w * 16 + 6 * w * w),
        name="qkv_back",
    )(meta, x, g_res, dq, dk, dv, vec, weight)


axes = ("img", "seq")


def swap(value, bit, count):
    return lax.ppermute(value, axes, [(i, i ^ bit) for i in range(count)])


def bits_of(count):
    return [1 << k for k in range(count.bit_length() - 1)]


def small_gather(value, me, count):
    value = value[None]
    for bit in bits_of(count):
        other = swap(value, bit, count)
        value = jnp.where(
            (me & bit) > 0,
            jnp.concatenate([other, value], axis=0),
            jnp.concatenate([value, other], axis=0),
        )
    return value


def small_sum(value, count):
    for bit in bits_of(count):
        value = value + swap(value, bit, count)
    return value


def small_scatter(value, me, count):
    for bit in reversed(bits_of(count)):
        pair = value.reshape((2, value.shape[0] // 2) + value.shape[1:])
        up = (me & bit) > 0
        value = jnp.where(up, pair[1], pair[0]) + swap(
            jnp.where(up, pair[0], pair[1]), bit, count
        )
    return value[0]


def gathered(value):
    return lax.all_gather(value, axes, axis=0, tiled=True)


def scattered(value):
    return lax.psum_scatter(value, axes, scatter_dimension=0, tiled=True).astype(wide)


def local(img_count, seq_count, *args):
    (
        patches, lengths, pooled_cot, norm1_gain, norm1_bias, qkv_weight, query_bias, value_bias,
        attn_weight, attn_bias, norm2_gain, norm2_bias, fc1_weight, fc1_bias, fc2_weight, fc2_bias,
        final_gain, final_bias, probe_vector, pool_query_weight, pool_query_bias, pool_kv_weight,
        pool_value_bias, pool_out_weight, pool_out_bias, head_gain, head_bias, head_fc1_weight,
        head_fc1_bias, head_fc2_weight, head_fc2_bias,
    ) = args
    count = img_count * seq_count
    groups, part_rows, width = patches.shape
    length = part_rows * seq_count
    hidden = fc1_weight.shape[1]
    images = max(1, groups // seq_count)
    share = max(1, seq_count // groups)
    own = width // count
    fold = hidden // width
    sz = Sizes(images, length, width, hidden)
    me = lax.axis_index(axes)
    seq_at = lax.axis_index("seq")

    vectors = jnp.stack(
        [
            norm1_gain, norm1_bias, query_bias, value_bias, attn_bias, norm2_gain, norm2_bias,
            fc2_bias, final_gain, final_bias, pool_query_bias, pool_value_bias, pool_out_bias,
            head_gain, head_bias, head_fc2_bias,
        ]
        + [v for b in (fc1_bias, head_fc1_bias) for v in b.reshape(fold, own)]
    )
    vectors = small_gather(vectors, me, count).astype(wide)
    vec = vectors[:, :16].transpose(1, 0, 2).reshape(16, width)
    fcb = vectors[:, 16:].reshape(count, 2, fold * own).transpose(1, 0, 2).reshape(2, hidden)

    if seq_count > 1:
        x = lax.all_to_all(
            jnp.repeat(patches, share, axis=0), "seq", split_axis=0, concat_axis=1, tiled=True
        )
    else:
        x = patches
    x = x.reshape(sz.rows, width)
    first_image = (seq_at // share) * images
    own_lengths = lax.dynamic_slice_in_dim(lengths, first_image, images)
    own_lengths = jnp.where(seq_at % share == 0, own_lengths, 0)
    own_cot = lax.dynamic_slice_in_dim(pooled_cot, first_image, images)
    meta = jnp.concatenate([(own_lengths + BLOCK - 1) // BLOCK, own_lengths]).astype(jnp.int32)

    qkv_full = gathered(qkv_weight)
    attn_full = gathered(attn_weight)
    fc1_full = gathered(fc1_weight)
    fc2_full = gathered(fc2_weight)
    pool_k, pool_v = pool_kv_weight[:, :width], pool_kv_weight[:, width:]
    pool_v_full = gathered(pool_v)
    pool_out_full = gathered(pool_out_weight)
    head_fc1_full = gathered(head_fc1_weight)
    head_fc2_full = gathered(head_fc2_weight)

    query_part = jnp.sum(
        probe_vector.astype(wide)[:, None] * pool_query_weight.astype(wide), axis=0, keepdims=True
    )
    pool_query = (small_sum(query_part, count) + vec[POOL_QUERY_BIAS:][:1]).astype(low)
    pool_query = pool_query.astype(wide)
    probe_own = (pool_k.astype(wide) * pool_query).reshape(own, HEADS, HEAD_DIM).sum(-1) * 0.125
    probe_own = jnp.pad(probe_own, ((0, 0), (0, HEAD_ROWS - HEADS)))
    probe_w = small_gather(probe_own.T, me, count).transpose(1, 0, 2).reshape(HEAD_ROWS, width)

    qkv, n1 = qkv_call(sz, meta, x, vec, qkv_full)
    att, lse = attend_call(sz, meta, qkv)
    res, n2, slope, act, enc, fin = mlp_call(
        sz, meta, x, att, vec, fcb, attn_full, fc1_full, fc2_full
    )
    cot_rows = jnp.pad(own_cot, ((0, HEAD_ROWS - images), (0, 0)))
    pooled, shares, lift, drop, mixed, wide_rows, narrow_rows, head_sums = head_call(
        sz, meta, fin, probe_w, cot_rows, vec, fcb, pool_v_full, pool_out_full, head_fc1_full,
        head_fc2_full,
    )
    pooled = lax.all_gather(pooled[:images], "seq", axis=0, tiled=True)[::share]

    g_mlp, g_hidden, g_res, g_branch, g_att, delta, mix, back_sums, fc1_sum = back_call(
        sz, meta, fin, enc, res, att, slope, shares, lift, drop, probe_w, vec, attn_full,
        fc1_full, fc2_full,
    )
    grad_fc2 = scattered(outer_call(sz, meta, act, g_mlp, 768, width, "grad_fc2"))
    grad_fc1 = scattered(outer_call(sz, meta, n2, g_hidden, width, 768, "grad_fc1"))
    grad_attn = scattered(outer_call(sz, meta, att, g_branch, width, 768, "grad_attn"))
    dq, dk, dv = attend_back_call(sz, meta, qkv, g_att, lse, delta)
    patch_grad, qkv_sums = qkv_back_call(sz, meta, x, g_res, dq, dk, dv, vec, qkv_full)
    grad_qkv = jnp.concatenate(
        [
            outer_call(sz, meta, n1, d, width, 768, "grad_" + name)
            for d, name in ((dq, "q"), (dk, "k"), (dv, "v"))
        ],
        axis=1,
    )
    grad_qkv = scattered(grad_qkv)

    def chunks(v, per):
        return v.reshape(v.shape[0], count, per).transpose(1, 0, 2)

    sent = jnp.concatenate(
        [
            chunks(narrow_rows[:images, :hidden], hidden // count),
            chunks(narrow_rows[:images, hidden : hidden + width], own),
            chunks(narrow_rows[:images, hidden + width :], own),
            mixed[:, :HEADS].reshape(images, HEADS, count, own).transpose(2, 0, 1, 3).reshape(
                count, images, HEADS * own
            ),
        ],
        axis=2,
    )
    mine = lax.all_to_all(sent, axes, split_axis=0, concat_axis=0, tiled=True)
    mine = mine.reshape(count * images, -1)
    rows = small_gather(wide_rows[:images], me, count).reshape(count * images, -1)
    per = hidden // count
    act_own, normed_own = mine[:, :per], mine[:, per : per + own]
    pooled_own, mixed_own = mine[:, per + own : per + 2 * own], mine[:, per + 2 * own :]
    head_grad, branch_rows = rows[:, :hidden], rows[:, hidden : hidden + width]
    pooled_rows, cot_all = rows[:, hidden + width : hidden + 2 * width], rows[:, hidden + 2 * width :]
    grad_head_fc2 = dot_tn(act_own, cot_all)
    grad_head_fc1 = dot_tn(normed_own, head_grad)
    grad_pool_out = dot_tn(pooled_own, branch_rows)
    grad_pool_v = jnp.einsum(
        "ihr,ihd->rhd",
        mixed_own.reshape(-1, HEADS, own),
        pooled_rows.reshape(-1, HEADS, HEAD_DIM),
        preferred_element_type=wide,
    ).reshape(own, width)
    row_sums = jnp.sum(rows.astype(wide), axis=0)
    mix_own = small_scatter(
        mix[:HEADS].reshape(HEADS, count, own).transpose(1, 0, 2), me, count
    )
    grad_pool_k = (
        0.125 * mix_own.T[:, :, None] * pool_query.reshape(1, HEADS, HEAD_DIM)
    ).reshape(own, width)
    query_grad = 0.125 * jnp.sum(
        mix_own.T[:, :, None] * pool_k.astype(wide).reshape(own, HEADS, HEAD_DIM), axis=0
    )
    query_grad = small_sum(query_grad.reshape(1, width), count)
    grad_pool_query_weight = probe_vector.astype(wide)[:, None] * query_grad
    grad_probe = jnp.sum(pool_query_weight.astype(wide) * query_grad, axis=1)
    grad_pool_kv = jnp.concatenate([grad_pool_k, grad_pool_v], axis=1)

    sums = jnp.concatenate([back_sums[:6], head_sums[:2], qkv_sums[:4]], axis=0)
    sums = jnp.concatenate(
        [
            sums.reshape(12, count, own).transpose(1, 0, 2).reshape(count, 12 * own),
            fc1_sum[0].reshape(count, per),
        ],
        axis=1,
    )
    sums = small_scatter(sums, me, count)
    (
        g_final_gain, g_final_bias, g_fc2_bias, g_norm2_gain, g_norm2_bias, g_attn_bias,
        g_head_gain, g_head_bias, g_norm1_gain, g_norm1_bias, g_query_bias, g_value_bias,
    ) = sums[: 12 * own].reshape(12, own)
    g_fc1_bias = sums[12 * own :]

    def own_part(v, size):
        return lax.dynamic_slice_in_dim(v, me * size, size)

    g_head_fc1_bias = own_part(row_sums[:hidden], per)
    g_pool_out_bias = own_part(row_sums[hidden : hidden + width], own)
    g_pool_value_bias = own_part(row_sums[hidden + width : hidden + 2 * width], own)
    g_head_fc2_bias = own_part(row_sums[hidden + 2 * width :], own)
    g_pool_query_bias = own_part(query_grad[0], own)

    patch_grad = patch_grad.reshape(images, length, width)
    if seq_count > 1:
        back = lax.all_to_all(
            patch_grad.astype(low), "seq", split_axis=1, concat_axis=0, tiled=True
        )[::share].astype(wide)
        if share == 1:
            kept = lax.dynamic_slice_in_dim(patch_grad, seq_at * part_rows, part_rows, axis=1)
            back = lax.dynamic_update_slice_in_dim(back, kept, first_image, axis=0)
        patch_grad = back
    return (
        pooled, patch_grad, g_norm1_gain, g_norm1_bias, grad_qkv, g_query_bias, g_value_bias,
        grad_attn, g_attn_bias, g_norm2_gain, g_norm2_bias, grad_fc1, g_fc1_bias, grad_fc2,
        g_fc2_bias, g_final_gain, g_final_bias, grad_probe, grad_pool_query_weight,
        g_pool_query_bias, grad_pool_kv, g_pool_value_bias, grad_pool_out, g_pool_out_bias,
        g_head_gain, g_head_bias, grad_head_fc1, g_head_fc1_bias, grad_head_fc2, g_head_fc2_bias,
    )


def solution(mesh):
    rows, vector = P(axes, None), P(axes)
    body = functools.partial(local, mesh.shape["img"], mesh.shape["seq"])
    vector_weights = (3, 4, 6, 7, 9, 10, 11, 13, 15, 16, 17, 18, 20, 22, 24, 25, 26, 28, 30)
    in_specs = (P("img", "seq", None), P("img"), P("img", None)) + tuple(
        vector if at in vector_weights else rows for at in range(3, 31)
    )
    out_specs = (P("img", None), P("img", "seq", None)) + in_specs[3:]
    return jax.shard_map(body, mesh=mesh, in_specs=in_specs, out_specs=out_specs, check_vma=False)
```

```python
import functools

import jax
import jax.numpy as jnp
from jax import lax
from jax.experimental import pallas as pl
from jax.experimental.pallas import tpu as pltpu
from jax.sharding import PartitionSpec as P

HEADS = 12
HEAD_DIM = 64
BLOCK = 256
PAIR = 128
wide = jnp.float32
low = jnp.bfloat16
masked_score = -1e30
norm_epsilon = 1e-06
root_two_pi = 0.7978845608028654
vmem_bytes = 60 * 1024 * 1024


def dot_nn(a, b):
    return jnp.dot(a, b, preferred_element_type=wide)


def dot_nt(a, b):
    return lax.dot_general(a, b, (((1,), (1,)), ((), ())), preferred_element_type=wide)


def dot_tn(a, b):
    return lax.dot_general(a, b, (((0,), (0,)), ((), ())), preferred_element_type=wide)


def halves(v):
    top = v.astype(low)
    return top, (v - top.astype(wide)).astype(low)


def normalise(v):
    centred = v - jnp.mean(v, axis=-1, keepdims=True)
    spread = jnp.mean(centred * centred, axis=-1, keepdims=True)
    scale = lax.rsqrt(spread + norm_epsilon)
    return centred * scale, scale


def norm_back(grad, gain, normal, scale):
    gn = grad * gain
    return (
        gn
        - jnp.mean(gn, axis=-1, keepdims=True)
        - normal * jnp.mean(gn * normal, axis=-1, keepdims=True)
    ) * scale


def column_sum(v):
    return jnp.sum(v, axis=0, keepdims=True)


def params(rank):
    return pltpu.CompilerParams(
        dimension_semantics=("arbitrary",) * rank, vmem_limit_bytes=vmem_bytes
    )


def whole(shape):
    return pl.BlockSpec(
        shape, lambda *_: (0,) * len(shape), pipeline_mode=pl.Buffered(1)
    )


def cost(flops, nbytes, exps=0):
    return pl.CostEstimate(flops=int(flops), bytes_accessed=int(nbytes), transcendentals=int(exps))


class Sizes:
    def __init__(self, images, length, width, hidden):
        self.images, self.length, self.width, self.hidden = images, length, width, hidden
        self.rows = images * length
        self.blocks = length // BLOCK
        self.pairs = width // PAIR

        self.units = 0

    def row_spec(self, cols):
        blocks = self.blocks

        def index(i, b, meta):
            return i * blocks + jnp.clip(b, 0, jnp.maximum(meta[i] - 1, 0)), 0

        return pl.BlockSpec((BLOCK, cols), index)

    def lane_spec(self, rows):
        def index(i, b, meta):
            return i, 0, jnp.clip(b, 0, jnp.maximum(meta[i] - 1, 0))

        return pl.BlockSpec((1, rows, BLOCK), index)

    def image_spec(self, rows, cols):
        return pl.BlockSpec((1, rows, cols), lambda i, b, meta: (i, 0, 0))


(
    NORM1_GAIN,
    NORM1_BIAS,
    QUERY_BIAS,
    VALUE_BIAS,
    ATTN_BIAS,
    NORM2_GAIN,
    NORM2_BIAS,
    FC2_BIAS,
    FINAL_GAIN,
    FINAL_BIAS,
    POOL_QUERY_BIAS,
    POOL_VALUE_BIAS,
    POOL_OUT_BIAS,
    HEAD_GAIN,
    HEAD_BIAS,
    HEAD_FC2_BIAS,
) = range(16)


PROBE = 16
FC1_BIAS = 17
VECTORS = 32


def row_of(ref, at):
    return ref[at : at + 1, :]


anywhere = pl.BlockSpec(memory_space=pl.ANY)


def fetch_all(meta, base, parts, held, sems):
    copies, place = [], 0
    for part in parts:
        for k in range(part.shape[0]):
            copies.append(
                pltpu.make_async_copy(part.at[k], held.at[meta[base + place]], sems.at[place])
            )
            place += 1
    for copy in copies:
        copy.start()
    for copy in copies:
        copy.wait()


def held_scratch(parts):
    units = sum(part.shape[0] for part in parts)
    return [
        pltpu.VMEM((units,) + parts[0].shape[1:], parts[0].dtype),
        pltpu.SemaphoreType.DMA((units,)),
    ]


def columns(held, start, size):
    units, rows, _ = held.shape
    return held[:, :, start : start + size].reshape(units * rows, size)


def is_first():
    return (pl.program_id(0) == 0) & (pl.program_id(1) == 0)


def vectors_body(*refs):
    rows, weight, (out, lines) = refs[:-3], refs[-3], refs[-2:]
    own, cols = weight.shape
    lines[...] = jnp.zeros_like(lines)
    at = 0
    for ref in rows:
        lines[at : at + ref.shape[0], :own] = ref[...].astype(wide)
        at += ref.shape[0]
    out[:, :cols] = weight[...]
    out[:, cols:] = lines[...].T[:own].astype(low)


def vectors_call(rows, weight):
    own, cols = weight.shape
    ins = (*rows, weight)
    return pl.pallas_call(
        vectors_body,
        in_specs=[pl.BlockSpec(memory_space=pltpu.VMEM)] * len(ins),
        out_specs=pl.BlockSpec(memory_space=pltpu.VMEM),
        out_shape=jax.ShapeDtypeStruct((own, cols + PAIR), low),
        scratch_shapes=[pltpu.VMEM((PAIR, PAIR), wide)],
        compiler_params=params(0),
        cost_estimate=cost(0, 4 * own * cols),
        name="vectors",
    )(*ins)


def qkv_body(base, meta, x, mine, theirs, qkv, normed, vec, held, sems):
    width = x.shape[1]

    @pl.when(is_first())
    def _():
        fetch_all(meta, base, (mine, theirs), held, sems)
        vec[...] = columns(held, 3 * width, PAIR).astype(wide).T[:VECTORS]

    @pl.when(pl.program_id(1) < meta[pl.program_id(0)])
    def _():
        normal, _ = normalise(x[...].astype(wide))
        rows = (normal * row_of(vec, NORM1_GAIN) + row_of(vec, NORM1_BIAS)).astype(low)
        normed[...] = rows
        for part, bias in enumerate((QUERY_BIAS, None, VALUE_BIAS)):
            out = dot_nn(rows, columns(held, part * width, width))
            if bias is not None:
                out = out + row_of(vec, bias)
            qkv[:, part * width : (part + 1) * width] = out.astype(low)


def qkv_call(sz, meta, x, weight):
    w = sz.width
    return pl.pallas_call(
        functools.partial(qkv_body, 2 * sz.images),
        grid_spec=pltpu.PrefetchScalarGridSpec(
            num_scalar_prefetch=1,
            grid=(sz.images, sz.blocks),
            in_specs=[sz.row_spec(w), anywhere, anywhere],
            out_specs=[
                sz.row_spec(3 * w),
                sz.row_spec(w),
                pl.BlockSpec((VECTORS, w), lambda i, b, m: (0, 0)),
            ],
            scratch_shapes=held_scratch(weight),
        ),
        out_shape=[
            jax.ShapeDtypeStruct((sz.rows, 3 * w), low),
            jax.ShapeDtypeStruct((sz.rows, w), low),
            jax.ShapeDtypeStruct((VECTORS, w), wide),
        ],
        compiler_params=params(2),
        cost_estimate=cost(6 * sz.rows * w * w, sz.rows * w * 10 + 6 * w * w),
        name="qkv",
    )(meta, x, *weight)


def attend_body(images, blocks, meta, q_ref, k_ref, v_ref, out_ref, lse_ref):
    at = pl.program_id(0)
    count, length = meta[at], meta[images + at]
    lane = lax.broadcasted_iota(jnp.int32, (BLOCK, PAIR), 1)
    first = lane < HEAD_DIM

    def variant(keys_in):
        near = keys_in - BLOCK
        column = lax.broadcasted_iota(jnp.int32, (BLOCK, BLOCK), 1) + near

        @pl.loop(0, count)
        def _(step):
            rows = pl.ds(pl.multiple_of(step * BLOCK, BLOCK), BLOCK)
            q = q_ref[rows, :]
            outs, logs = [], []
            for head in range(2):
                own = first if head == 0 else jnp.logical_not(first)
                qh = jnp.where(own, q, jnp.zeros_like(q))
                last = dot_nt(qh, k_ref[near:keys_in, :]) * 0.125
                last = jnp.where(column < length, last, masked_score)
                top = jnp.max(last, axis=1, keepdims=True)
                if near:
                    body = dot_nt(qh, k_ref[:near, :]) * 0.125
                    top = jnp.maximum(top, jnp.max(body, axis=1, keepdims=True))
                p_last = jnp.exp(last - top)
                total = jnp.sum(p_last, axis=1, keepdims=True)
                acc = dot_nn(p_last.astype(low), v_ref[near:keys_in, :])
                if near:
                    p_body = jnp.exp(body - top)
                    total = total + jnp.sum(p_body, axis=1, keepdims=True)
                    acc = acc + dot_nn(p_body.astype(low), v_ref[:near, :])
                outs.append(acc / total)
                logs.append(top + jnp.log(total))
            out_ref[rows, :] = jnp.where(first, outs[0], outs[1]).astype(low)
            both = jnp.where(lane == 0, logs[0], logs[1])
            lse_ref[0, :, rows] = both.T[:8, :]

    for keys in range(1, blocks + 1):
        pl.when(count == keys)(functools.partial(variant, keys * BLOCK))


def attend_call(sz, meta, qkv):
    pairs = sz.pairs

    def spec(part):
        return pl.BlockSpec((sz.length, PAIR), lambda i, p, m: (i, part * pairs + p))

    return pl.pallas_call(
        functools.partial(attend_body, sz.images, sz.blocks),
        grid_spec=pltpu.PrefetchScalarGridSpec(
            num_scalar_prefetch=1,
            grid=(sz.images, pairs),
            in_specs=[spec(0), spec(1), spec(2)],
            out_specs=[
                pl.BlockSpec((sz.length, PAIR), lambda i, p, m: (i, p)),
                pl.BlockSpec((1, 8, sz.length), lambda i, p, m: (i, p, 0)),
            ],
        ),
        out_shape=[
            jax.ShapeDtypeStruct((sz.rows, sz.width), low),
            jax.ShapeDtypeStruct((sz.images, 8 * pairs, sz.length), wide),
        ],
        compiler_params=params(2),
        cost_estimate=cost(
            4 * sz.rows * sz.length * sz.width,
            8 * sz.rows * sz.width,
            sz.rows * sz.length * HEADS,
        ),
        name="attend",
    )(meta, qkv, qkv, qkv)


def mlp_body(meta, x, att, vec, weight, res, n2, slope, act, enc, fin):
    @pl.when(pl.program_id(1) < meta[pl.program_id(0)])
    def _():
        width = x.shape[1]
        fold = slope.shape[1] // width

        def part_of(k):
            return weight[:, k * width : (k + 1) * width]

        branch = dot_nn(att[...], part_of(0)) + row_of(vec, ATTN_BIAS)
        rows = x[...].astype(wide) + branch
        res[...] = rows
        normal, _ = normalise(rows)
        normed = (normal * row_of(vec, NORM2_GAIN) + row_of(vec, NORM2_BIAS)).astype(low)
        n2[...] = normed
        total = rows + row_of(vec, FC2_BIAS)
        for part in range(fold):
            cols = slice(part * width, (part + 1) * width)
            u = dot_nn(normed, part_of(1 + part)) + row_of(vec, FC1_BIAS + part)
            square = u * u
            bend = jnp.tanh(root_two_pi * u * (1.0 + 0.044715 * square))
            half = 0.5 * (1.0 + bend)
            hidden = (u * half).astype(low)
            slope[:, cols] = (
                half
                + (0.5 * root_two_pi) * u * (1.0 - bend * bend) * (1.0 + 0.134145 * square)
            ).astype(low)
            act[:, cols] = hidden
            total = total + dot_nn(hidden, part_of(1 + fold + part))
        enc[...] = total
        normal, _ = normalise(total)
        fin[...] = (normal * row_of(vec, FINAL_GAIN) + row_of(vec, FINAL_BIAS)).astype(low)


def mlp_call(sz, meta, x, att, vec, weight):
    w, f = sz.width, sz.hidden
    return pl.pallas_call(
        mlp_body,
        grid_spec=pltpu.PrefetchScalarGridSpec(
            num_scalar_prefetch=1,
            grid=(sz.images, sz.blocks),
            in_specs=[sz.row_spec(w), sz.row_spec(w), whole(vec.shape), whole(weight.shape)],
            out_specs=[sz.row_spec(c) for c in (w, w, f, f, w, w)],
        ),
        out_shape=[
            jax.ShapeDtypeStruct((sz.rows, w), wide),
            jax.ShapeDtypeStruct((sz.rows, w), low),
            jax.ShapeDtypeStruct((sz.rows, f), low),
            jax.ShapeDtypeStruct((sz.rows, f), low),
            jax.ShapeDtypeStruct((sz.rows, w), wide),
            jax.ShapeDtypeStruct((sz.rows, w), low),
        ],
        compiler_params=params(2),
        cost_estimate=cost(
            sz.rows * w * (2 * w + 4 * f), sz.rows * (14 * w + 4 * f) + 4 * w * f, sz.rows * f
        ),
        name="mlp",
    )(meta, x, att, vec, weight)


HEAD_ROWS = 16


SENT_ROWS = 48
SENT_MIX, SENT_ACT, SENT_GRAD, SENT_NORMED, SENT_POOLED = 16, 32, 36, 40, 41
SENT_BRANCH, SENT_PULL, SENT_COT, SENT_OUT, SENT_OUT_REST = 42, 43, 44, 45, 46
SENT_QUERY, SENT_QUERY_REST = 47, 31


def head_body(
    images, blocks, fold, meta, fin, cot_ref, vec, mine, theirs, rest,
    shares, g_score, lift, probe_out, sent, sums, score, mixed, line, held, sems,
):
    width = fin.shape[1]
    fetch_all(meta, 2 * images, (mine, theirs, rest), held, sems)
    at_out, at_v, at_k, at_q = (2 * fold + k for k in range(4))

    def part_of(k):
        return columns(held, k * width, width)

    head_row = lax.broadcasted_iota(jnp.int32, (HEAD_ROWS, width), 0)
    head_col = lax.broadcasted_iota(jnp.int32, (HEAD_ROWS, width), 1) // HEAD_DIM
    own = head_row == head_col
    row_id = lax.broadcasted_iota(jnp.int32, (HEAD_ROWS, 1), 0)
    probe = jnp.broadcast_to(row_of(vec, PROBE), (HEAD_ROWS, width)).astype(low)
    query = (dot_nn(probe, part_of(at_q)) + row_of(vec, POOL_QUERY_BIAS)).astype(low)
    probe_w = 0.125 * dot_nt(jnp.where(own, query, jnp.zeros_like(query)), part_of(at_k))
    probe_out[...] = jnp.where(row_id == HEADS, query.astype(wide), probe_w)
    probe_top, probe_rest = halves(probe_w)
    pooled_heads = jnp.zeros((HEAD_ROWS, width), wide)

    def block_rows(i, b):
        start = (i * blocks + b) * BLOCK
        return fin[start : start + BLOCK, :]

    for i in range(images):
        count, length = meta[i], meta[images + i]
        for b in range(blocks):
            cols = slice(b * BLOCK, (b + 1) * BLOCK)
            score[:, cols] = jnp.full((HEAD_ROWS, BLOCK), masked_score, wide)

            @pl.when(b < count)
            def _(i=i, b=b, cols=cols, length=length):
                rows = block_rows(i, b)
                value = dot_nt(probe_top, rows) + dot_nt(probe_rest, rows)
                column = lax.broadcasted_iota(jnp.int32, (HEAD_ROWS, BLOCK), 1) + b * BLOCK
                score[:, cols] = jnp.where(column < length, value, masked_score)

        raised = jnp.exp(score[...] - jnp.max(score[...], axis=1, keepdims=True))
        shares[i] = raised / jnp.sum(raised, axis=1, keepdims=True)
        mixed[i] = jnp.zeros((HEAD_ROWS, width), wide)
        for b in range(blocks):
            cols = slice(b * BLOCK, (b + 1) * BLOCK)

            @pl.when(b < count)
            def _(i=i, b=b, cols=cols):
                rows = block_rows(i, b)
                top, rest = halves(shares[i, :, cols])
                mixed[i] += dot_nn(top, rows) + dot_nn(rest, rows)

        top, rest = halves(mixed[i])
        sent[i * SENT_ROWS : i * SENT_ROWS + HEAD_ROWS, :] = top
        heads = dot_nn(top, part_of(at_v)) + dot_nn(rest, part_of(at_v))
        row = column_sum(jnp.where(own, heads, 0.0)) + row_of(vec, POOL_VALUE_BIAS)
        pooled_heads = jnp.where(row_id == i, row, pooled_heads)
    real = row_id < jnp.where(meta[0] > 0, images, 0)
    cot = jnp.where(real, cot_ref[...], 0.0)
    pooled_low = pooled_heads.astype(low)
    branch = dot_nn(pooled_low, part_of(at_out)) + row_of(vec, POOL_OUT_BIAS)
    normal, scale = normalise(branch)
    gain = row_of(vec, HEAD_GAIN)
    normed = (normal * gain + row_of(vec, HEAD_BIAS)).astype(low)
    cot_low = cot.astype(low)
    total = branch + row_of(vec, HEAD_FC2_BIAS)
    back = jnp.zeros((HEAD_ROWS, width), wide)

    def keep(at, value):
        for i in range(images):
            line[i, at - 2 * HEAD_ROWS : at + 1 - 2 * HEAD_ROWS, :] = value[i : i + 1, :].astype(wide)

    for part in range(fold):
        u = dot_nn(normed, part_of(part)) + row_of(vec, FC1_BIAS + fold + part)
        square = u * u
        bend = jnp.tanh(root_two_pi * u * (1.0 + 0.044715 * square))
        half = 0.5 * (1.0 + bend)
        act = (u * half).astype(low)
        slope = half + (0.5 * root_two_pi) * u * (1.0 - bend * bend) * (1.0 + 0.134145 * square)
        second = part_of(fold + part)
        total = total + dot_nn(act, second)
        grad = jnp.where(real, dot_nt(cot_low, second) * slope, 0.0).astype(low)
        back = back + dot_nt(grad, part_of(part))
        keep(SENT_ACT + part, act)
        keep(SENT_GRAD + part, grad)
    sums[...] = jnp.zeros_like(sums)
    sums[0:1, :] = column_sum(jnp.where(real, back * normal, 0.0))
    sums[1:2, :] = column_sum(jnp.where(real, back, 0.0))
    branch_grad = jnp.where(real, cot + norm_back(back, gain, normal, scale), 0.0).astype(low)
    pull = dot_nt(branch_grad, part_of(at_out))
    keep(SENT_NORMED, normed)
    keep(SENT_POOLED, pooled_low)
    keep(SENT_BRANCH, branch_grad)
    keep(SENT_PULL, pull)
    keep(SENT_COT, cot_low)
    top, rest = halves(total)
    keep(SENT_OUT, top)
    keep(SENT_OUT_REST, rest)
    for i in range(images):
        top, rest = halves(jnp.where(own, pull[i : i + 1, :], 0.0))
        raised = dot_nt(top, part_of(at_v)) + dot_nt(rest, part_of(at_v))
        drop = jnp.sum(raised * mixed[i], axis=1, keepdims=True)
        lift[i] = raised
        lift_top, lift_rest = halves(raised)
        mixed[i] = jnp.zeros((HEAD_ROWS, width), wide)
        for b in range(blocks):
            cols = slice(b * BLOCK, (b + 1) * BLOCK)

            @pl.when(b < meta[i])
            def _(i=i, b=b, cols=cols):
                rows = block_rows(i, b)
                reach = dot_nt(lift_top, rows) + dot_nt(lift_rest, rows)
                grad = shares[i, :, cols] * (reach - drop)
                g_score[i, :, cols] = grad
                top, rest = halves(grad)
                mixed[i] += dot_nn(top, rows) + dot_nn(rest, rows)

        top, rest = halves(mixed[i])
        pulled = dot_nn(top, part_of(at_k)) + dot_nn(rest, part_of(at_k))
        query_grad = 0.125 * column_sum(jnp.where(own, pulled, 0.0))
        query_top, query_rest = halves(query_grad)
        line[i, HEAD_ROWS - 1 : HEAD_ROWS, :] = query_top.astype(wide)
        both = jnp.where(row_id == HEAD_ROWS - 1, query_rest.astype(wide), mixed[i])
        start = i * SENT_ROWS + HEAD_ROWS
        sent[start : start + HEAD_ROWS, :] = both.astype(low)
        sent[start + HEAD_ROWS : start + 2 * HEAD_ROWS, :] = line[i].astype(low)


def head_call(sz, meta, fin, cot, vec, weight):
    w, f, n = sz.width, sz.hidden, sz.images

    def out(shape, dtype):
        return jax.ShapeDtypeStruct(shape, dtype)

    shapes = [
        out((n, HEAD_ROWS, sz.length), wide),
        out((n, HEAD_ROWS, sz.length), wide),
        out((n, HEAD_ROWS, w), wide),
        out((HEAD_ROWS, w), wide),
        out((n * SENT_ROWS, w), low),
        out((8, w), wide),
    ]
    ins = (fin, cot, vec)
    return pl.pallas_call(
        functools.partial(head_body, sz.images, sz.blocks, f // w),
        grid_spec=pltpu.PrefetchScalarGridSpec(
            num_scalar_prefetch=1,
            grid=(1,),
            in_specs=[whole(v.shape) for v in ins] + [anywhere] * 3,
            out_specs=[pl.BlockSpec(s.shape, lambda *_, r=len(s.shape): (0,) * r) for s in shapes],
            scratch_shapes=[
                pltpu.VMEM((HEAD_ROWS, sz.length), wide),
                pltpu.VMEM((n, HEAD_ROWS, w), wide),
                pltpu.VMEM((n, HEAD_ROWS, w), wide),
            ]
            + held_scratch(weight),
        ),
        out_shape=shapes,
        compiler_params=params(1),
        cost_estimate=cost(16 * 8 * w * f, sz.rows * w * 2 + 4 * w * f + 8 * w * w),
        name="head",
    )(meta, *ins, *weight)


def back_body(
    meta, fin, enc, res, att, slope, g_score, shares, lift, probe_w, spread, vec, weight,
    g_mlp, g_hidden, g_res, g_branch, g_att, delta, sums,
):
    @pl.when(is_first())
    def _():
        sums[...] = jnp.zeros_like(sums)

    @pl.when(pl.program_id(1) < meta[pl.program_id(0)])
    def _():
        width = fin.shape[1]
        fold = slope.shape[1] // width

        def part_of(k):
            return weight[:, k * width : (k + 1) * width]

        lift_top, lift_rest = halves(lift[0])
        probe_top, probe_rest = halves(probe_w[...])
        top, rest = halves(g_score[0])
        share_top, share_rest = halves(shares[0])
        left = jnp.concatenate([top, share_top, rest, share_rest, top, share_top], axis=0)
        right = jnp.concatenate(
            [probe_top, lift_top, probe_top, lift_top, probe_rest, lift_rest], axis=0
        )
        g_fin = dot_tn(left, right)
        normal, scale = normalise(enc[...])
        sums[0:1, :] += column_sum(g_fin * normal)
        sums[1:2, :] += column_sum(g_fin)
        g_enc = norm_back(g_fin, row_of(vec, FINAL_GAIN), normal, scale)
        low_enc = g_enc.astype(low)
        g_mlp[...] = low_enc
        sums[2:3, :] += column_sum(low_enc.astype(wide))
        back = jnp.zeros_like(g_enc)
        for part in range(fold):
            cols = slice(part * width, (part + 1) * width)
            grad = dot_nt(low_enc, part_of(1 + fold + part))
            grad = (grad * slope[:, cols].astype(wide)).astype(low)
            g_hidden[:, cols] = grad
            sums[8 + part : 9 + part, :] += column_sum(grad.astype(wide))
            back = back + dot_nt(grad, part_of(1 + part))
        normal, scale = normalise(res[...])
        sums[3:4, :] += column_sum(back * normal)
        sums[4:5, :] += column_sum(back)
        total = g_enc + norm_back(back, row_of(vec, NORM2_GAIN), normal, scale)
        g_res[...] = total
        low_res = total.astype(low)
        g_branch[...] = low_res
        sums[5:6, :] += column_sum(low_res.astype(wide))
        grad = dot_nt(low_res, part_of(0)).astype(low)
        g_att[...] = grad
        top, rest = halves(grad.astype(wide) * att[...].astype(wide))
        delta[0] = dot_nt(spread[...], top) + dot_nt(spread[...], rest)


def back_call(
    sz, meta, fin, enc, res, att, slope, g_score, shares, lift, probe_w, vec, weight
):
    w, f, n = sz.width, sz.hidden, sz.images
    lines = 8 * sz.pairs
    line = lax.broadcasted_iota(jnp.int32, (lines, w), 0)
    head = lax.broadcasted_iota(jnp.int32, (lines, w), 1) // HEAD_DIM
    spread = (head == 2 * (line // 8) + line % 8).astype(low)
    fixed = (probe_w, spread, vec, weight)

    def out(shape, dtype):
        return jax.ShapeDtypeStruct(shape, dtype)

    def kept(shape):
        return pl.BlockSpec(shape, lambda i, b, m: (0, 0))

    return pl.pallas_call(
        back_body,
        grid_spec=pltpu.PrefetchScalarGridSpec(
            num_scalar_prefetch=1,
            grid=(n, sz.blocks),
            in_specs=[
                sz.row_spec(w), sz.row_spec(w), sz.row_spec(w), sz.row_spec(w), sz.row_spec(f),
                sz.lane_spec(HEAD_ROWS), sz.lane_spec(HEAD_ROWS), sz.image_spec(HEAD_ROWS, w),
            ]
            + [whole(v.shape) for v in fixed],
            out_specs=[
                sz.row_spec(w), sz.row_spec(f), sz.row_spec(w), sz.row_spec(w), sz.row_spec(w),
                sz.lane_spec(lines), kept((16, w)),
            ],
        ),
        out_shape=[
            out((sz.rows, w), low), out((sz.rows, f), low), out((sz.rows, w), wide),
            out((sz.rows, w), low), out((sz.rows, w), low), out((n, lines, sz.length), wide),
            out((16, w), wide),
        ],
        compiler_params=params(2),
        cost_estimate=cost(
            sz.rows * w * (2 * w + 4 * f), sz.rows * (22 * w + 4 * f) + 4 * w * f
        ),
        name="mlp_back",
    )(meta, fin, enc, res, att, slope, g_score, shares, lift, *fixed)


def outer_body(images, blocks, units, meta, a_ref, b_ref, out_ref, acc):
    span = blocks * BLOCK

    def finish(term):
        if units == 0:
            out_ref[...] = term.astype(out_ref.dtype)
            return
        rows = term.shape[0] // units
        for u in range(units):
            out_ref[meta[2 * images + units + u]] = term[u * rows : (u + 1) * rows].astype(low)

    for i in range(images):
        for keys in range(blocks + 1):

            @pl.when(meta[i] == keys)
            def _(i=i, keys=keys):
                if keys:
                    rows = slice(i * span, i * span + keys * BLOCK)
                    term = dot_tn(a_ref[rows, :], b_ref[rows, :])
                else:
                    term = jnp.zeros(acc.shape, wide)
                if i > 0:
                    term = term + acc[...]
                if i < images - 1:
                    acc[...] = term
                else:
                    finish(term)


def outer_block_body(
    images, blocks, fold, meta, att_ref, g_att_ref, n2_ref, g_hidden_ref, act_ref, g_mlp_ref, out_ref, acc
):
    step = pl.program_id(0)
    for live, a_ref, b_ref in (
        (step == 0, att_ref, g_att_ref),
        ((step > 0) & (step <= fold), n2_ref, g_hidden_ref),
        (step > fold, act_ref, g_mlp_ref),
    ):
        pl.when(live)(
            functools.partial(outer_body, images, blocks, 0, meta, a_ref, b_ref, out_ref, acc)
        )


def outer_block_call(sz, meta, att, g_branch, n2, g_hidden, act, g_mlp):
    w, fold = sz.width, sz.hidden // sz.width
    one = whole((sz.rows, w))

    def part(first):
        return pl.BlockSpec((sz.rows, w), lambda j, c: (0, jnp.clip(j - first, 0, fold - 1)))

    return pl.pallas_call(
        functools.partial(outer_block_body, sz.images, sz.blocks, fold),
        grid_spec=pltpu.PrefetchScalarGridSpec(
            num_scalar_prefetch=1,
            grid=(1 + 2 * fold,),
            in_specs=[one, one, one, part(1), part(1 + fold), one],
            out_specs=pl.BlockSpec((w, w), lambda j, c: (0, j)),
            scratch_shapes=[pltpu.VMEM((w, w), wide)],
        ),
        out_shape=jax.ShapeDtypeStruct((w, (1 + 2 * fold) * w), low),
        compiler_params=params(1),
        cost_estimate=cost(2 * sz.rows * w * w * (1 + 2 * fold), 2 * sz.rows * w * (2 * fold + 4)),
        name="grad_block",
    )(meta, att, g_branch, n2, g_hidden, act, g_mlp)


def outer_qkv_body(images, blocks, units, meta, n1_ref, dq_ref, dk_ref, dv_ref, out_ref, acc):
    for k, b_ref in enumerate((dq_ref, dk_ref, dv_ref)):
        pl.when(pl.program_id(0) == k)(
            functools.partial(outer_body, images, blocks, units, meta, n1_ref, b_ref, out_ref, acc)
        )


def outer_qkv_call(sz, meta, n1, dq, dk, dv, units):
    w = sz.width
    return pl.pallas_call(
        functools.partial(outer_qkv_body, sz.images, sz.blocks, units),
        grid_spec=pltpu.PrefetchScalarGridSpec(
            num_scalar_prefetch=1,
            grid=(3,),
            in_specs=[whole((sz.rows, w))] * 4,
            out_specs=pl.BlockSpec((units, w // units, w), lambda j, c: (0, 0, j)),
            scratch_shapes=[pltpu.VMEM((w, w), wide)],
        ),
        out_shape=jax.ShapeDtypeStruct((units, w // units, 3 * w), low),
        compiler_params=params(1),
        cost_estimate=cost(6 * sz.rows * w * w, 8 * sz.rows * w),
        name="grad_qkv",
    )(meta, n1, dq, dk, dv)


def place_body(at, kept, taken, out):
    i = pl.program_id(0)

    @pl.when(at[2 * i] == 1)
    def _():
        out[...] = kept[...]

    @pl.when(at[2 * i] == 0)
    def _():
        out[...] = taken[...].astype(wide)


def place_call(at, kept, taken, groups, rows):
    width = kept.shape[-1]
    spec = pl.BlockSpec((1, rows, width), lambda i, at: (at[2 * i + 1], 0, 0))
    return pl.pallas_call(
        place_body,
        grid_spec=pltpu.PrefetchScalarGridSpec(
            num_scalar_prefetch=1,
            grid=(groups,),
            in_specs=[spec, spec],
            out_specs=pl.BlockSpec((1, rows, width), lambda i, at: (i, 0, 0)),
        ),
        out_shape=jax.ShapeDtypeStruct((groups, rows, width), wide),
        compiler_params=params(1),
        cost_estimate=cost(0, groups * rows * width * 10),
        name="place",
    )(at, kept, taken)


def attend_back_body(
    images, blocks, meta, q_ref, k_ref, v_ref, g_ref, lse_ref, delta_ref, dq_ref, dk_ref, dv_ref,
    dk_acc, dv_acc,
):
    at = pl.program_id(0)
    count, length = meta[at], meta[images + at]
    lane = lax.broadcasted_iota(jnp.int32, (BLOCK, PAIR), 1)
    first = lane < HEAD_DIM

    def keep(value, head):
        own = first if head == 0 else jnp.logical_not(first)
        zero = jnp.zeros_like(value[:BLOCK])
        return jnp.concatenate(
            [
                jnp.where(own, value[r : r + BLOCK], zero)
                for r in range(0, value.shape[0], BLOCK)
            ],
            axis=0,
        )

    def variant(keys_in):
        near = keys_in - BLOCK
        valid = lax.broadcasted_iota(jnp.int32, (BLOCK, BLOCK), 0) + near < length
        keys = k_ref[:keys_in, :]
        kept_keys = [keep(keys, head) for head in range(2)]
        values = v_ref[:keys_in, :]
        kept_values = [keep(values, head) for head in range(2)]
        dk_acc[:keys_in, :] = jnp.zeros((keys_in, PAIR), wide)
        dv_acc[:keys_in, :] = jnp.zeros((keys_in, PAIR), wide)

        @pl.loop(0, count)
        def _(step):
            rows = pl.ds(pl.multiple_of(step * BLOCK, BLOCK), BLOCK)
            q, g = q_ref[rows, :], g_ref[rows, :]
            dq = None
            for head in range(2):
                log = lse_ref[0, head : head + 1, rows]
                drop = delta_ref[0, head : head + 1, rows]
                score = dot_nt(kept_keys[head], q) * 0.125
                share = jnp.exp(score - log)
                if near:
                    share = jnp.concatenate(
                        [share[:near], jnp.where(valid, share[near:], 0.0)], axis=0
                    )
                else:
                    share = jnp.where(valid, share, 0.0)
                reach = dot_nt(kept_values[head], g)
                grad = (share * (reach - drop)).astype(low)
                dv_acc[:keys_in, :] += dot_nn(share.astype(low), keep(g, head))
                dk_acc[:keys_in, :] += dot_nn(grad, keep(q, head))
                term = dot_tn(grad, kept_keys[head])
                dq = term if dq is None else dq + term
            dq_ref[rows, :] = (dq * 0.125).astype(low)

        dk_ref[:keys_in, :] = (dk_acc[:keys_in, :] * 0.125).astype(low)
        dv_ref[:keys_in, :] = dv_acc[:keys_in, :].astype(low)

    for keys in range(1, blocks + 1):
        pl.when(count == keys)(functools.partial(variant, keys * BLOCK))


def attend_back_call(sz, meta, qkv, g_att, lse, delta):
    pairs = sz.pairs

    def spec(part):
        return pl.BlockSpec((sz.length, PAIR), lambda i, p, m: (i, part * pairs + p))

    line = pl.BlockSpec((1, 8, sz.length), lambda i, p, m: (i, p, 0))
    out = jax.ShapeDtypeStruct((sz.rows, sz.width), low)
    return pl.pallas_call(
        functools.partial(attend_back_body, sz.images, sz.blocks),
        grid_spec=pltpu.PrefetchScalarGridSpec(
            num_scalar_prefetch=1,
            grid=(sz.images, pairs),
            in_specs=[spec(0), spec(1), spec(2), spec(0), line, line],
            out_specs=[spec(0), spec(0), spec(0)],
            scratch_shapes=[pltpu.VMEM((sz.length, PAIR), wide)] * 2,
        ),
        out_shape=[out, out, out],
        compiler_params=params(2),
        cost_estimate=cost(
            10 * sz.rows * sz.length * sz.width,
            14 * sz.rows * sz.width,
            sz.rows * sz.length * HEADS,
        ),
        name="attend_back",
    )(meta, qkv, qkv, qkv, g_att, lse, delta)


def qkv_back_body(
    base, meta, x, g_res, dq, dk, dv, vec, mine, theirs, grad_ref, low_ref, sums, held, sems
):
    @pl.when(is_first())
    def _():
        fetch_all(meta, base, (mine, theirs), held, sems)
        sums[...] = jnp.zeros_like(sums)

    live = pl.program_id(1) < meta[pl.program_id(0)]

    @pl.when(live)
    def _():
        width = x.shape[1]
        normal, scale = normalise(x[...].astype(wide))
        back = None
        for part, ref in enumerate((dq, dk, dv)):
            term = dot_nt(ref[...], columns(held, part * width, width))
            back = term if back is None else back + term
        sums[0:1, :] += column_sum(back * normal)
        sums[1:2, :] += column_sum(back)
        sums[2:3, :] += column_sum(dq[...].astype(wide))
        sums[3:4, :] += column_sum(dv[...].astype(wide))
        grad = g_res[...] + norm_back(back, row_of(vec, NORM1_GAIN), normal, scale)
        grad_ref[...] = grad
        low_ref[...] = grad.astype(low)

    @pl.when(jnp.logical_not(live))
    def _():
        grad_ref[...] = jnp.zeros_like(grad_ref)
        low_ref[...] = jnp.zeros_like(low_ref)


def qkv_back_call(sz, meta, x, g_res, dq, dk, dv, vec, weight):
    w, blocks = sz.width, sz.blocks
    plain = pl.BlockSpec((BLOCK, w), lambda i, b, m: (i * blocks + b, 0))
    return pl.pallas_call(
        functools.partial(qkv_back_body, 2 * sz.images),
        grid_spec=pltpu.PrefetchScalarGridSpec(
            num_scalar_prefetch=1,
            grid=(sz.images, blocks),
            in_specs=[sz.row_spec(w)] * 5 + [whole(vec.shape), anywhere, anywhere],
            out_specs=[plain, plain, pl.BlockSpec((8, w), lambda i, b, m: (0, 0))],
            scratch_shapes=held_scratch(weight),
        ),
        out_shape=[
            jax.ShapeDtypeStruct((sz.rows, w), wide),
            jax.ShapeDtypeStruct((sz.rows, w), low),
            jax.ShapeDtypeStruct((8, w), wide),
        ],
        compiler_params=params(2),
        cost_estimate=cost(6 * sz.rows * w * w, sz.rows * w * 18 + 6 * w * w),
        name="qkv_back",
    )(meta, x, g_res, dq, dk, dv, vec, *weight)


axes = ("img", "seq")


def bits_of(count):
    return [1 << k for k in range(count.bit_length() - 1)]


def tied(value, *after):
    return lax.optimization_barrier((value, *after))[0]


def together(*values):
    return lax.optimization_barrier(values)


def cut(size, shares):
    edges = [round(size * sum(shares[:k]) / sum(shares) / 16) * 16 for k in range(len(shares) + 1)]
    return [slice(p, q) for p, q in zip(edges[:-1], edges[1:], strict=True)]


class Wires:
    def __init__(self, img_count, seq_count):
        self.count, self.seq_count = img_count * seq_count, seq_count
        self.core = seq_count
        self.units = img_count
        self.seq_bits = bits_of(seq_count)
        inner = [bit for bit in bits_of(self.count) if bit > self.core]
        inner = inner[:1] + inner[:0:-1]
        self.orders = (inner, inner[1:] + inner[:1])

    def swap(self, value, bit):
        return lax.ppermute(value, axes, [(i, i ^ bit) for i in range(self.count)])

    def step(self, value, at):
        pairs = [(i, i ^ self.orders[1 if i & self.core else 0][at]) for i in range(self.count)]
        return lax.ppermute(value, axes, pairs)

    def tables(self, me):
        img = me // self.seq_count
        core = img % 2

        def at(place, side):
            by_core = []
            for order in self.orders:
                unit = 0
                for k, bit in enumerate(order):
                    unit |= ((place >> k) & 1) * (bit // self.seq_count)
                by_core.append(unit)
            which = core if side == 0 else 1 - core
            return (img ^ side) ^ jnp.where(which == 0, by_core[0], by_core[1])

        def place(unit):
            side = (unit ^ img) & 1
            delta = unit ^ img
            by_core = []
            for order in self.orders:
                total = jnp.zeros((), jnp.int32)
                for k, bit in enumerate(order):
                    shift = (bit // self.seq_count).bit_length() - 1
                    total = total | (((delta >> shift) & 1) << k)
                by_core.append(total)
            which = core ^ side
            return side * (self.units // 2) + jnp.where(which == 0, by_core[0], by_core[1])

        half = self.units // 2
        order = [at(k, side) for side in range(2) for k in range(half)]
        inverse = [place(unit) for unit in range(self.units)]
        return jnp.stack(order + inverse)

    def join_seq(self, value, me):
        for bit in self.seq_bits:
            other = self.swap(value, bit)
            value = jnp.where(
                (me & bit) > 0,
                jnp.concatenate([other, value], axis=0),
                jnp.concatenate([value, other], axis=0),
            )
        return value

    def joined(self, value, at):
        return jnp.concatenate([value, self.step(value, at)], axis=0)

    def halved(self, value, at):
        half = value.shape[0] // 2
        return value[:half] + self.step(value[half:], at)

    def small_scatter(self, value, me, bits):
        for bit in reversed(bits):
            value = self.small_half(value, me, bit)
        return value[0]

    def small_half(self, value, me, bit):
        pair = value.reshape((2, value.shape[0] // 2) + value.shape[1:])
        up = (me & bit) > 0
        return jnp.where(up, pair[1], pair[0]) + self.swap(jnp.where(up, pair[0], pair[1]), bit)


def local(img_count, seq_count, *args):
    (
        patches, lengths, pooled_cot, norm1_gain, norm1_bias, qkv_weight, query_bias, value_bias,
        attn_weight, attn_bias, norm2_gain, norm2_bias, fc1_weight, fc1_bias, fc2_weight, fc2_bias,
        final_gain, final_bias, probe_vector, pool_query_weight, pool_query_bias, pool_kv_weight,
        pool_value_bias, pool_out_weight, pool_out_bias, head_gain, head_bias, head_fc1_weight,
        head_fc1_bias, head_fc2_weight, head_fc2_bias,
    ) = args
    count = img_count * seq_count
    groups, part_rows, width = patches.shape
    length = part_rows * seq_count
    hidden = fc1_weight.shape[1]
    images = max(1, groups // seq_count)
    share = max(1, seq_count // groups)
    own = width // count
    per = hidden // count
    fold = hidden // width
    sz = Sizes(images, length, width, hidden)
    wires = Wires(img_count, seq_count)
    me = lax.axis_index(axes)
    seq_at = lax.axis_index("seq")
    first_image = (seq_at // share) * images

    slots = list(range(groups))
    if share == 1:
        turn = [r % seq_count if (r // seq_count) % 2 == 0 else -1 - r % seq_count for r in slots]
        slots = [(t % seq_count) * images + r // seq_count for r, t in zip(slots, turn, strict=True)]
        ahead = (lengths[None, :] > lengths[:, None]) | (
            (lengths[None, :] == lengths[:, None])
            & (jnp.arange(groups)[None, :] < jnp.arange(groups)[:, None])
        )
        rank = jnp.sum(ahead, axis=1)
        slot_of = sum(jnp.where(rank == r, slot, 0) for r, slot in enumerate(slots))
    else:
        slot_of = jnp.arange(groups)
    order = jnp.sum(
        jnp.where(slot_of[None, :] == jnp.arange(groups)[:, None], jnp.arange(groups)[None, :], 0),
        axis=1,
    )

    def of_slots(value, first):
        at = lax.dynamic_slice_in_dim(order, first, images)
        return jnp.concatenate(
            [lax.dynamic_slice_in_dim(value, at[k], 1) for k in range(images)], axis=0
        )

    own_lengths = of_slots(lengths, first_image)
    own_lengths = jnp.where(seq_at % share == 0, own_lengths, 0)
    own_cot = of_slots(pooled_cot, first_image)
    meta = jnp.concatenate(
        [(own_lengths + BLOCK - 1) // BLOCK, own_lengths, wires.tables(me)]
    ).astype(jnp.int32)

    def by_unit(bias):
        return bias.reshape(own, fold).T

    vectors = [
        v.reshape(1, own)
        for v in (
            norm1_gain, norm1_bias, query_bias, value_bias, attn_bias, norm2_gain, norm2_bias,
            fc2_bias, final_gain, final_bias, pool_query_bias, pool_value_bias, pool_out_bias,
            head_gain, head_bias, head_fc2_bias, probe_vector,
        )
    ]
    vectors += [by_unit(fc1_bias), by_unit(head_fc1_bias)]
    unit_a = vectors_call(vectors, qkv_weight)
    unit_a, fc1_weight, head_fc1_weight = together(unit_a, fc1_weight, head_fc1_weight)

    def by_part(weight):
        return weight.reshape(own, width, fold).transpose(0, 2, 1).reshape(own, hidden)

    block = jnp.concatenate(
        [attn_weight, by_part(fc1_weight), fc2_weight.reshape(own, hidden)], axis=1
    )
    block = lax.all_gather(block, axes, axis=0, tiled=True)

    pack = jnp.concatenate(
        [
            by_part(head_fc1_weight), head_fc2_weight.reshape(own, hidden), pool_out_weight,
            pool_kv_weight[:, width:], pool_kv_weight[:, :width], pool_query_weight,
        ],
        axis=1,
    )

    pairwise = seq_count == 2 and share == 1
    steps = len(wires.orders[0])
    if pairwise:
        kept = of_slots(patches, first_image)
        given = of_slots(patches, (1 - seq_at) * images)
        parts = cut(part_rows, list(range(2, steps + 2)))
    else:
        ordered = jnp.concatenate(
            [lax.dynamic_slice_in_dim(patches, order[k], 1) for k in range(groups)], axis=0
        )
        given = jnp.repeat(ordered, share, axis=0)
    mine = wires.join_seq(unit_a, me)[None]
    mine, given = together(mine, given)
    taken = []
    for at in range(steps):
        mine = wires.joined(mine, at)
        if pairwise:
            mine, one, meta = together(mine, wires.swap(given[:, parts[at]], 1), meta)
            taken.append(one)
        if at == steps - 2:
            mine, pack = together(mine, pack)
    theirs = wires.swap(mine, wires.core)
    theirs, pack = together(theirs, wires.join_seq(pack, me)[None])
    qkv_full = (mine, theirs)
    if pairwise:
        taken = jnp.concatenate(taken, axis=1)
        x = jnp.where(
            seq_at == 0,
            jnp.concatenate([kept, taken], axis=1),
            jnp.concatenate([taken, kept], axis=1),
        )
    else:
        x = lax.all_to_all(given, "seq", split_axis=0, concat_axis=1, tiled=True)
    x = x.reshape(sz.rows, width)

    qkv, n1, vec = qkv_call(sz, meta, x, qkv_full)
    for at in range(steps - 2):
        pack = wires.joined(pack, at)
    qkv, pack = together(qkv, pack)
    att, lse = attend_call(sz, meta, qkv)
    pack = wires.joined(pack, steps - 2)
    att, pack = together(att, pack)
    res, n2, slope, act, enc, fin = mlp_call(sz, meta, x, att, vec, block)
    other = wires.swap(pack, wires.core)
    pack_rest = wires.step(pack, steps - 1)
    fin, other, pack_rest = together(fin, other, pack_rest)
    other_rest = wires.swap(pack_rest, wires.core)
    head_full = (jnp.concatenate([pack, pack_rest], axis=0), other, other_rest)
    cot_rows = jnp.pad(own_cot, ((0, HEAD_ROWS - images), (0, 0)))
    shares, g_score, lift, probe_w, sent, head_sums = head_call(
        sz, meta, fin, cot_rows, vec, head_full
    )
    rows = lax.all_gather(sent, axes, axis=0, tiled=True)

    g_mlp, g_hidden, g_res, g_branch, g_att, delta, back_sums = back_call(
        sz, meta, fin, enc, res, att, slope, g_score, shares, lift, probe_w, vec, block
    )
    terms = outer_block_call(sz, meta, att, g_branch, n2, g_hidden, act, g_mlp)
    terms, g_att, rows = together(terms, g_att, rows)
    totals = lax.psum_scatter(terms, axes, scatter_dimension=0, tiled=True).astype(wide)
    grad_attn = totals[:, :width]

    def by_column(grad):
        return grad.reshape(own, fold, width).transpose(0, 2, 1).reshape(own, hidden)

    grad_fc1 = by_column(totals[:, width : width + hidden])
    grad_fc2 = totals[:, width + hidden :].reshape(per, width)
    dq, dk, dv = attend_back_call(sz, meta, qkv, g_att, lse, delta)
    last = outer_qkv_call(sz, meta, n1, dq, dk, dv, wires.units)
    half = wires.units // 2
    g_res, last = together(g_res, last)
    last = last[:half] + wires.swap(last[half:], wires.core)
    patch_grad, patch_low, qkv_sums = qkv_back_call(sz, meta, x, g_res, dq, dk, dv, vec, qkv_full)
    patch_grad = patch_grad.reshape(images, length, width)
    patch_low = patch_low.reshape(images, length, width)
    sums = jnp.concatenate(
        [back_sums[:6], head_sums[:2], qkv_sums[:4], back_sums[8 : 8 + fold]], axis=0
    )
    sums = sums.reshape(-1, count, own).transpose(1, 0, 2)
    if pairwise:
        kept = lax.dynamic_slice_in_dim(patch_grad, seq_at * part_rows, part_rows, axis=1)
        given = lax.dynamic_slice_in_dim(patch_low, (1 - seq_at) * part_rows, part_rows, axis=1)
    else:
        back = lax.all_to_all(patch_low, "seq", split_axis=1, concat_axis=0, tiled=True)[::share]
        patch_grad = jnp.concatenate(
            [lax.dynamic_slice_in_dim(back, slot_of[k], 1) for k in range(groups)], axis=0
        ).astype(wide)

    rows = rows.reshape(count * images, SENT_ROWS, width)

    def own_part(v, axis=-1):
        return lax.dynamic_slice_in_dim(v, me * own, own, axis=axis)

    narrow = own_part(rows)
    head_grad = rows[:, SENT_GRAD : SENT_GRAD + fold].reshape(count * images, hidden)
    branch_rows, pull_rows, cot_all = rows[:, SENT_BRANCH], rows[:, SENT_PULL], rows[:, SENT_COT]
    act_own = narrow[:, SENT_ACT : SENT_ACT + fold].transpose(0, 2, 1).reshape(-1, per)
    grad_head_fc2 = dot_tn(act_own, cot_all)
    grad_head_fc1 = by_column(dot_tn(narrow[:, SENT_NORMED], head_grad))
    grad_pool_out = dot_tn(narrow[:, SENT_POOLED], branch_rows)
    grad_pool_v = jnp.einsum(
        "ihr,ihd->rhd",
        narrow[:, :HEADS],
        pull_rows.reshape(-1, HEADS, HEAD_DIM),
        preferred_element_type=wide,
    ).reshape(own, width)
    row_sums = jnp.sum(rows[:, 2 * HEAD_ROWS - 1 :].astype(wide), axis=0)

    def row_sum(at):
        return row_sums[at - 2 * HEAD_ROWS + 1]

    mix_own = jnp.sum(narrow[:, SENT_MIX : SENT_MIX + HEADS].astype(wide), axis=0)
    pool_query = probe_w[HEADS]
    query_grad = row_sum(SENT_QUERY) + row_sum(SENT_QUERY_REST)
    grad_pool_query_weight = probe_vector.astype(wide)[:, None] * query_grad[None, :]
    grad_probe = jnp.sum(pool_query_weight.astype(wide) * query_grad[None, :], axis=1)
    own_sums = own_part(row_sums)
    g_head_fc1_bias = own_sums[SENT_GRAD - 2 * HEAD_ROWS + 1 :][:fold].T.reshape(per)
    pooled = rows[:, SENT_OUT].astype(wide) + rows[:, SENT_OUT_REST].astype(wide)
    pooled = pooled.reshape(img_count, seq_count, images, width)[:, ::share]
    pooled = lax.dynamic_index_in_dim(pooled, me // seq_count, 0, keepdims=False)
    pooled = pooled.reshape(groups, width)
    pooled = jnp.concatenate(
        [lax.dynamic_slice_in_dim(pooled, slot_of[k], 1) for k in range(groups)], axis=0
    )
    grad_pool_k = (
        0.125 * mix_own.T[:, :, None] * pool_query.reshape(1, HEADS, HEAD_DIM)
    ).reshape(own, width)
    grad_pool_kv = jnp.concatenate([grad_pool_k, grad_pool_v], axis=1)

    head_grads = (grad_head_fc2, grad_head_fc1, grad_pool_out, grad_pool_kv, row_sums, grad_probe)
    if pairwise:
        parts, taken = cut(part_rows, (1,) * steps), []
        last, given = together(last, given)
    bits = list(reversed(bits_of(count)))
    for at in reversed(range(steps)):
        last = wires.halved(last, at)
        if bits:
            sums = wires.small_half(sums, me, bits.pop(0))
        if pairwise:
            taken.append(wires.swap(given[:, parts[steps - 1 - at]], 1))
            last, sums, taken[-1] = together(last, sums, taken[-1])
        if at == steps - 2:
            last, head_grads = together(last, head_grads)
    if pairwise:
        at_slot = jnp.stack(
            [(slot_of // images == seq_at).astype(jnp.int32), slot_of % images], axis=1
        )
        patch_grad = place_call(
            at_slot.reshape(-1).astype(jnp.int32),
            kept,
            jnp.concatenate(taken, axis=1),
            groups,
            part_rows,
        )
    last = last.reshape(seq_count, own, 3 * width)
    for bit in reversed(wires.seq_bits):
        last = wires.small_half(last, me, bit)
        if bits:
            sums = wires.small_half(sums, me, bits.pop(0))
    while bits:
        sums = wires.small_half(sums, me, bits.pop(0))
    sums = sums[0]
    grad_qkv = last[0].astype(wide)
    (
        g_final_gain, g_final_bias, g_fc2_bias, g_norm2_gain, g_norm2_bias, g_attn_bias,
        g_head_gain, g_head_bias, g_norm1_gain, g_norm1_bias, g_query_bias, g_value_bias,
    ) = sums[:12]
    g_fc1_bias = sums[12:].T.reshape(per)
    grad_head_fc2, grad_head_fc1, grad_pool_out, grad_pool_kv, row_sums, grad_probe = head_grads
    return (
        pooled, patch_grad, g_norm1_gain, g_norm1_bias, grad_qkv, g_query_bias, g_value_bias,
        grad_attn, g_attn_bias, g_norm2_gain, g_norm2_bias, grad_fc1, g_fc1_bias, grad_fc2,
        g_fc2_bias, g_final_gain, g_final_bias, grad_probe, grad_pool_query_weight,
        own_part(query_grad), grad_pool_kv, own_part(row_sum(SENT_PULL)), grad_pool_out,
        own_part(row_sum(SENT_BRANCH)), g_head_gain, g_head_bias, grad_head_fc1,
        g_head_fc1_bias, grad_head_fc2, own_part(row_sum(SENT_COT)),
    )


def solution(mesh):
    rows, vector = P(axes, None), P(axes)
    body = functools.partial(local, mesh.shape["img"], mesh.shape["seq"])
    vector_weights = (3, 4, 6, 7, 9, 10, 11, 13, 15, 16, 17, 18, 20, 22, 24, 25, 26, 28, 30)
    in_specs = (P("img", "seq", None), P("img"), P("img", None)) + tuple(
        vector if at in vector_weights else rows for at in range(3, 31)
    )
    out_specs = (P("img", None), P("img", "seq", None)) + in_specs[3:]
    return jax.shard_map(body, mesh=mesh, in_specs=in_specs, out_specs=out_specs, check_vma=False)
```

```python
import functools

import jax
import jax.numpy as jnp
from jax import lax
from jax.experimental import pallas as pl
from jax.experimental.pallas import tpu as pltpu
from jax.sharding import PartitionSpec as P

HEADS = 12
HEAD_DIM = 64
BLOCK = 256
PAIR = 128
wide = jnp.float32
low = jnp.bfloat16
masked_score = -1e30
norm_epsilon = 1e-06
root_two_pi = 0.7978845608028654
vmem_bytes = 60 * 1024 * 1024


def dot_nn(a, b):
    return jnp.dot(a, b, preferred_element_type=wide)


def dot_nt(a, b):
    return lax.dot_general(a, b, (((1,), (1,)), ((), ())), preferred_element_type=wide)


def dot_tn(a, b):
    return lax.dot_general(a, b, (((0,), (0,)), ((), ())), preferred_element_type=wide)


def halves(v):
    top = v.astype(low)
    return top, (v - top.astype(wide)).astype(low)


def normalise(v):
    centred = v - jnp.mean(v, axis=-1, keepdims=True)
    spread = jnp.mean(centred * centred, axis=-1, keepdims=True)
    scale = lax.rsqrt(spread + norm_epsilon)
    return centred * scale, scale


def norm_back(grad, gain, normal, scale):
    gn = grad * gain
    return (
        gn
        - jnp.mean(gn, axis=-1, keepdims=True)
        - normal * jnp.mean(gn * normal, axis=-1, keepdims=True)
    ) * scale


def column_sum(v):
    return jnp.sum(v, axis=0, keepdims=True)


def params(rank):
    return pltpu.CompilerParams(
        dimension_semantics=("arbitrary",) * rank, vmem_limit_bytes=vmem_bytes
    )


def whole(shape):
    return pl.BlockSpec(
        shape, lambda *_: (0,) * len(shape), pipeline_mode=pl.Buffered(1)
    )


def cost(flops, nbytes, exps=0):
    return pl.CostEstimate(flops=int(flops), bytes_accessed=int(nbytes), transcendentals=int(exps))


class Sizes:
    def __init__(self, images, length, width, hidden):
        self.images, self.length, self.width, self.hidden = images, length, width, hidden
        self.rows = images * length
        self.blocks = length // BLOCK
        self.pairs = width // PAIR

        self.units = 0

    def row_spec(self, cols):
        blocks = self.blocks

        def index(i, b, meta):
            return i * blocks + jnp.clip(b, 0, jnp.maximum(meta[i] - 1, 0)), 0

        return pl.BlockSpec((BLOCK, cols), index)

    def lane_spec(self, rows):
        def index(i, b, meta):
            return i, 0, jnp.clip(b, 0, jnp.maximum(meta[i] - 1, 0))

        return pl.BlockSpec((1, rows, BLOCK), index)

    def image_spec(self, rows, cols):
        return pl.BlockSpec((1, rows, cols), lambda i, b, meta: (i, 0, 0))


(
    NORM1_GAIN,
    NORM1_BIAS,
    QUERY_BIAS,
    VALUE_BIAS,
    ATTN_BIAS,
    NORM2_GAIN,
    NORM2_BIAS,
    FC2_BIAS,
    FINAL_GAIN,
    FINAL_BIAS,
    POOL_QUERY_BIAS,
    POOL_VALUE_BIAS,
    POOL_OUT_BIAS,
    HEAD_GAIN,
    HEAD_BIAS,
    HEAD_FC2_BIAS,
) = range(16)


PROBE = 16
FC1_BIAS = 17
VECTORS = 32


def row_of(ref, at):
    return ref[at : at + 1, :]


anywhere = pl.BlockSpec(memory_space=pl.ANY)


def fetch_all(meta, base, parts, held, sems):
    copies, place = [], 0
    for part in parts:
        for k in range(part.shape[0]):
            copies.append(
                pltpu.make_async_copy(part.at[k], held.at[meta[base + place]], sems.at[place])
            )
            place += 1
    for copy in copies:
        copy.start()
    for copy in copies:
        copy.wait()


def held_scratch(parts):
    units = sum(part.shape[0] for part in parts)
    return [
        pltpu.VMEM((units,) + parts[0].shape[1:], parts[0].dtype),
        pltpu.SemaphoreType.DMA((units,)),
    ]


def columns(held, start, size):
    units, rows, _ = held.shape
    return held[:, :, start : start + size].reshape(units * rows, size)


def is_first():
    return (pl.program_id(0) == 0) & (pl.program_id(1) == 0)


def packs_body(count, *refs):
    rows = refs[:count]
    qkv, pool_kv, pool_query, attn, fc1, fc2, pool_out, head_fc1, head_fc2 = refs[count:-4]
    first, block, head, lines = refs[-4:]
    own, width = attn.shape
    fold = fc1.shape[1] // width
    chunk = fold * PAIR
    at_from = lax.broadcasted_iota(jnp.int32, (chunk, chunk), 0)
    at_to = lax.broadcasted_iota(jnp.int32, (chunk, chunk), 1)
    spread = jnp.where(at_from == (at_to % PAIR) * fold + at_to // PAIR, 1.0, 0.0).astype(low)
    row_from = lax.broadcasted_iota(jnp.int32, (own, own * fold), 1)
    row_to = lax.broadcasted_iota(jnp.int32, (own, own * fold), 0)

    def by_part(ref, out, start):
        for k in range(width // PAIR):
            value = dot_nn(ref[:, k * chunk : (k + 1) * chunk], spread).astype(low)
            for j in range(fold):
                to = start + j * width + k * PAIR
                out[:, to : to + PAIR] = value[:, j * PAIR : (j + 1) * PAIR]

    def by_row(ref, out, start):
        for j in range(fold):
            pick = jnp.where(row_from == row_to * fold + j, 1.0, 0.0).astype(low)
            to = start + j * width
            out[:, to : to + width] = dot_nn(pick, ref[...]).astype(low)

    lines[...] = jnp.zeros_like(lines)
    at = 0
    for ref in rows:
        lines[at : at + ref.shape[0], :own] = ref[...].astype(wide)
        at += ref.shape[0]
    first[:, : 3 * width] = qkv[...]
    first[:, 3 * width :] = lines[...].T[:own].astype(low)
    block[:, : 2 * width] = pool_kv[...]
    block[:, 2 * width : 3 * width] = pool_query[...]
    block[:, 3 * width : 4 * width] = pool_out[...]
    block[:, 4 * width : 5 * width] = attn[...]
    by_part(fc1, block, 5 * width)
    by_row(fc2, block, (5 + fold) * width)
    by_part(head_fc1, head, 0)
    by_row(head_fc2, head, fold * width)


def packs_call(rows, *weights):
    own, width = weights[3].shape
    fold = weights[4].shape[1] // width
    ins = (*rows, *weights)
    vmem = pl.BlockSpec(memory_space=pltpu.VMEM)
    return pl.pallas_call(
        functools.partial(packs_body, len(rows)),
        in_specs=[vmem] * len(ins),
        out_specs=[vmem] * 3,
        out_shape=[
            jax.ShapeDtypeStruct((own, cols), low)
            for cols in (3 * width + PAIR, (5 + 2 * fold) * width, 2 * fold * width)
        ],
        scratch_shapes=[pltpu.VMEM((PAIR, PAIR), wide)],
        compiler_params=params(0),
        cost_estimate=cost(0, 4 * own * width * (9 + 4 * fold)),
        name="packs",
    )(*ins)


def qkv_body(base, meta, x, mine, theirs, qkv, normed, vec, held, sems):
    width = x.shape[1]

    @pl.when(is_first())
    def _():
        fetch_all(meta, base, (mine, theirs), held, sems)
        vec[...] = columns(held, 3 * width, PAIR).astype(wide).T[:VECTORS]

    @pl.when(pl.program_id(1) < meta[pl.program_id(0)])
    def _():
        normal, _ = normalise(x[...].astype(wide))
        rows = (normal * row_of(vec, NORM1_GAIN) + row_of(vec, NORM1_BIAS)).astype(low)
        normed[...] = rows
        for part, bias in enumerate((QUERY_BIAS, None, VALUE_BIAS)):
            out = dot_nn(rows, columns(held, part * width, width))
            if bias is not None:
                out = out + row_of(vec, bias)
            qkv[:, part * width : (part + 1) * width] = out.astype(low)


def qkv_call(sz, meta, x, weight):
    w = sz.width
    return pl.pallas_call(
        functools.partial(qkv_body, 2 * sz.images),
        grid_spec=pltpu.PrefetchScalarGridSpec(
            num_scalar_prefetch=1,
            grid=(sz.images, sz.blocks),
            in_specs=[sz.row_spec(w), anywhere, anywhere],
            out_specs=[
                sz.row_spec(3 * w),
                sz.row_spec(w),
                pl.BlockSpec((VECTORS, w), lambda i, b, m: (0, 0)),
            ],
            scratch_shapes=held_scratch(weight),
        ),
        out_shape=[
            jax.ShapeDtypeStruct((sz.rows, 3 * w), low),
            jax.ShapeDtypeStruct((sz.rows, w), low),
            jax.ShapeDtypeStruct((VECTORS, w), wide),
        ],
        compiler_params=params(2),
        cost_estimate=cost(6 * sz.rows * w * w, sz.rows * w * 10 + 6 * w * w),
        name="qkv",
    )(meta, x, *weight)


def attend_body(images, blocks, at, meta, q_ref, k_ref, v_ref, *rest):
    out_ref, lse_ref = rest[-2:]
    count, length = meta[at], meta[images + at]
    lane = lax.broadcasted_iota(jnp.int32, (BLOCK, PAIR), 1)
    first = lane < HEAD_DIM

    def variant(keys_in):
        near = keys_in - BLOCK
        column = lax.broadcasted_iota(jnp.int32, (BLOCK, BLOCK), 1) + near

        @pl.loop(0, count)
        def _(step):
            rows = pl.ds(pl.multiple_of(step * BLOCK, BLOCK), BLOCK)
            q = q_ref[rows, :]
            outs, logs = [], []
            for head in range(2):
                own = first if head == 0 else jnp.logical_not(first)
                qh = jnp.where(own, q, jnp.zeros_like(q))
                last = dot_nt(qh, k_ref[near:keys_in, :]) * 0.125
                last = jnp.where(column < length, last, masked_score)
                top = jnp.max(last, axis=1, keepdims=True)
                if near:
                    body = dot_nt(qh, k_ref[:near, :]) * 0.125
                    top = jnp.maximum(top, jnp.max(body, axis=1, keepdims=True))
                p_last = jnp.exp(last - top)
                total = jnp.sum(p_last, axis=1, keepdims=True)
                acc = dot_nn(p_last.astype(low), v_ref[near:keys_in, :])
                if near:
                    p_body = jnp.exp(body - top)
                    total = total + jnp.sum(p_body, axis=1, keepdims=True)
                    acc = acc + dot_nn(p_body.astype(low), v_ref[:near, :])
                outs.append(acc / total)
                logs.append(top + jnp.log(total))
            out_ref[rows, :] = jnp.where(first, outs[0], outs[1]).astype(low)
            both = jnp.where(lane == 0, logs[0], logs[1])
            lse_ref[0, :, rows] = both.T[:8, :]

    for keys in range(1, blocks + 1):
        pl.when(count == keys)(functools.partial(variant, keys * BLOCK))


def attend_call(sz, meta, qkv, at, before):
    pairs = sz.pairs

    def spec(part):
        return pl.BlockSpec((sz.length, PAIR), lambda p, m: (at, part * pairs + p))

    return pl.pallas_call(
        functools.partial(attend_body, sz.images, sz.blocks, at),
        grid_spec=pltpu.PrefetchScalarGridSpec(
            num_scalar_prefetch=1,
            grid=(pairs,),
            in_specs=[spec(0), spec(1), spec(2)] + [anywhere] * len(before),
            out_specs=[
                pl.BlockSpec((sz.length, PAIR), lambda p, m: (at, p)),
                pl.BlockSpec((1, 8, sz.length), lambda p, m: (at, p, 0)),
            ],
        ),
        out_shape=[
            jax.ShapeDtypeStruct((sz.rows, sz.width), low),
            jax.ShapeDtypeStruct((sz.images, 8 * pairs, sz.length), wide),
        ],
        input_output_aliases={4 + k: k for k in range(len(before))},
        compiler_params=params(1),
        cost_estimate=cost(
            4 * sz.length * sz.length * sz.width,
            8 * sz.length * sz.width,
            sz.length * sz.length * HEADS,
        ),
        name=f"attend_{at}",
    )(meta, qkv, qkv, qkv, *before)


AHEAD = 4


def mlp_body(meta, x, att, vec, weight, res, n2, slope, act, enc, fin):
    @pl.when(pl.program_id(1) < meta[pl.program_id(0)])
    def _():
        width = x.shape[1]
        fold = slope.shape[1] // width

        def part_of(k):
            return weight[:, (AHEAD + k) * width : (AHEAD + k + 1) * width]

        branch = dot_nn(att[...], part_of(0)) + row_of(vec, ATTN_BIAS)
        rows = x[...].astype(wide) + branch
        res[...] = rows
        normal, _ = normalise(rows)
        normed = (normal * row_of(vec, NORM2_GAIN) + row_of(vec, NORM2_BIAS)).astype(low)
        n2[...] = normed
        total = rows + row_of(vec, FC2_BIAS)
        for part in range(fold):
            cols = slice(part * width, (part + 1) * width)
            u = dot_nn(normed, part_of(1 + part)) + row_of(vec, FC1_BIAS + part)
            square = u * u
            bend = jnp.tanh(root_two_pi * u * (1.0 + 0.044715 * square))
            half = 0.5 * (1.0 + bend)
            hidden = (u * half).astype(low)
            slope[:, cols] = (
                half
                + (0.5 * root_two_pi) * u * (1.0 - bend * bend) * (1.0 + 0.134145 * square)
            ).astype(low)
            act[:, cols] = hidden
            total = total + dot_nn(hidden, part_of(1 + fold + part))
        enc[...] = total
        normal, _ = normalise(total)
        fin[...] = (normal * row_of(vec, FINAL_GAIN) + row_of(vec, FINAL_BIAS)).astype(low)


def mlp_call(sz, meta, x, att, vec, weight):
    w, f = sz.width, sz.hidden
    return pl.pallas_call(
        mlp_body,
        grid_spec=pltpu.PrefetchScalarGridSpec(
            num_scalar_prefetch=1,
            grid=(sz.images, sz.blocks),
            in_specs=[sz.row_spec(w), sz.row_spec(w), whole(vec.shape), whole(weight.shape)],
            out_specs=[sz.row_spec(c) for c in (w, w, f, f, w, w)],
        ),
        out_shape=[
            jax.ShapeDtypeStruct((sz.rows, w), wide),
            jax.ShapeDtypeStruct((sz.rows, w), low),
            jax.ShapeDtypeStruct((sz.rows, f), low),
            jax.ShapeDtypeStruct((sz.rows, f), low),
            jax.ShapeDtypeStruct((sz.rows, w), wide),
            jax.ShapeDtypeStruct((sz.rows, w), low),
        ],
        compiler_params=params(2),
        cost_estimate=cost(
            sz.rows * w * (2 * w + 4 * f), sz.rows * (14 * w + 4 * f) + 4 * w * f, sz.rows * f
        ),
        name="mlp",
    )(meta, x, att, vec, weight)


HEAD_ROWS = 16


SENT_ROWS = 48
SENT_MIX, SENT_ACT, SENT_GRAD, SENT_NORMED, SENT_POOLED = 16, 32, 36, 40, 41
SENT_BRANCH, SENT_PULL, SENT_COT, SENT_OUT, SENT_OUT_REST = 42, 43, 44, 45, 46
SENT_QUERY, SENT_QUERY_REST = 47, 31


def head_body(
    images, blocks, fold, meta, fin, cot_ref, vec, pool_w, mine, theirs, rest,
    shares, g_score, lift, probe_out, sent, sums, score, mixed, line, held, sems,
):
    width = fin.shape[1]
    fetch_all(meta, 2 * images, (mine, theirs, rest), held, sems)
    keys_w, values_w, query_w, out_w = (
        pool_w.at[:, k * width : (k + 1) * width] for k in range(AHEAD)
    )

    def part_of(k):
        return columns(held, k * width, width)

    head_row = lax.broadcasted_iota(jnp.int32, (HEAD_ROWS, width), 0)
    head_col = lax.broadcasted_iota(jnp.int32, (HEAD_ROWS, width), 1) // HEAD_DIM
    own = head_row == head_col
    row_id = lax.broadcasted_iota(jnp.int32, (HEAD_ROWS, 1), 0)
    probe = jnp.broadcast_to(row_of(vec, PROBE), (HEAD_ROWS, width)).astype(low)
    query = (dot_nn(probe, query_w[...]) + row_of(vec, POOL_QUERY_BIAS)).astype(low)
    probe_w = 0.125 * dot_nt(jnp.where(own, query, jnp.zeros_like(query)), keys_w[...])
    probe_out[...] = jnp.where(row_id == HEADS, query.astype(wide), probe_w)
    probe_top, probe_rest = halves(probe_w)
    pooled_heads = jnp.zeros((HEAD_ROWS, width), wide)

    def block_rows(i, b):
        start = (i * blocks + b) * BLOCK
        return fin[start : start + BLOCK, :]

    for i in range(images):
        count, length = meta[i], meta[images + i]
        for b in range(blocks):
            cols = slice(b * BLOCK, (b + 1) * BLOCK)
            score[:, cols] = jnp.full((HEAD_ROWS, BLOCK), masked_score, wide)

            @pl.when(b < count)
            def _(i=i, b=b, cols=cols, length=length):
                rows = block_rows(i, b)
                value = dot_nt(probe_top, rows) + dot_nt(probe_rest, rows)
                column = lax.broadcasted_iota(jnp.int32, (HEAD_ROWS, BLOCK), 1) + b * BLOCK
                score[:, cols] = jnp.where(column < length, value, masked_score)

        raised = jnp.exp(score[...] - jnp.max(score[...], axis=1, keepdims=True))
        shares[i] = raised / jnp.sum(raised, axis=1, keepdims=True)
        mixed[i] = jnp.zeros((HEAD_ROWS, width), wide)
        for b in range(blocks):
            cols = slice(b * BLOCK, (b + 1) * BLOCK)

            @pl.when(b < count)
            def _(i=i, b=b, cols=cols):
                rows = block_rows(i, b)
                top, rest = halves(shares[i, :, cols])
                mixed[i] += dot_nn(top, rows) + dot_nn(rest, rows)

        top, rest = halves(mixed[i])
        sent[i * SENT_ROWS : i * SENT_ROWS + HEAD_ROWS, :] = top
        heads = dot_nn(top, values_w[...]) + dot_nn(rest, values_w[...])
        row = column_sum(jnp.where(own, heads, 0.0)) + row_of(vec, POOL_VALUE_BIAS)
        pooled_heads = jnp.where(row_id == i, row, pooled_heads)
    real = row_id < jnp.where(meta[0] > 0, images, 0)
    cot = jnp.where(real, cot_ref[...], 0.0)
    pooled_low = pooled_heads.astype(low)
    branch = dot_nn(pooled_low, out_w[...]) + row_of(vec, POOL_OUT_BIAS)
    normal, scale = normalise(branch)
    gain = row_of(vec, HEAD_GAIN)
    normed = (normal * gain + row_of(vec, HEAD_BIAS)).astype(low)
    cot_low = cot.astype(low)
    total = branch + row_of(vec, HEAD_FC2_BIAS)
    back = jnp.zeros((HEAD_ROWS, width), wide)

    def keep(at, value):
        for i in range(images):
            line[i, at - 2 * HEAD_ROWS : at + 1 - 2 * HEAD_ROWS, :] = value[i : i + 1, :].astype(wide)

    for part in range(fold):
        u = dot_nn(normed, part_of(part)) + row_of(vec, FC1_BIAS + fold + part)
        square = u * u
        bend = jnp.tanh(root_two_pi * u * (1.0 + 0.044715 * square))
        half = 0.5 * (1.0 + bend)
        act = (u * half).astype(low)
        slope = half + (0.5 * root_two_pi) * u * (1.0 - bend * bend) * (1.0 + 0.134145 * square)
        second = part_of(fold + part)
        total = total + dot_nn(act, second)
        grad = jnp.where(real, dot_nt(cot_low, second) * slope, 0.0).astype(low)
        back = back + dot_nt(grad, part_of(part))
        keep(SENT_ACT + part, act)
        keep(SENT_GRAD + part, grad)
    sums[...] = jnp.zeros_like(sums)
    sums[0:1, :] = column_sum(jnp.where(real, back * normal, 0.0))
    sums[1:2, :] = column_sum(jnp.where(real, back, 0.0))
    branch_grad = jnp.where(real, cot + norm_back(back, gain, normal, scale), 0.0).astype(low)
    pull = dot_nt(branch_grad, out_w[...])
    keep(SENT_NORMED, normed)
    keep(SENT_POOLED, pooled_low)
    keep(SENT_BRANCH, branch_grad)
    keep(SENT_PULL, pull)
    keep(SENT_COT, cot_low)
    top, rest = halves(total)
    keep(SENT_OUT, top)
    keep(SENT_OUT_REST, rest)
    for i in range(images):
        top, rest = halves(jnp.where(own, pull[i : i + 1, :], 0.0))
        raised = dot_nt(top, values_w[...]) + dot_nt(rest, values_w[...])
        drop = jnp.sum(raised * mixed[i], axis=1, keepdims=True)
        lift[i] = raised
        lift_top, lift_rest = halves(raised)
        mixed[i] = jnp.zeros((HEAD_ROWS, width), wide)
        for b in range(blocks):
            cols = slice(b * BLOCK, (b + 1) * BLOCK)

            @pl.when(b < meta[i])
            def _(i=i, b=b, cols=cols):
                rows = block_rows(i, b)
                reach = dot_nt(lift_top, rows) + dot_nt(lift_rest, rows)
                grad = shares[i, :, cols] * (reach - drop)
                g_score[i, :, cols] = grad
                top, rest = halves(grad)
                mixed[i] += dot_nn(top, rows) + dot_nn(rest, rows)

        top, rest = halves(mixed[i])
        pulled = dot_nn(top, keys_w[...]) + dot_nn(rest, keys_w[...])
        query_grad = 0.125 * column_sum(jnp.where(own, pulled, 0.0))
        query_top, query_rest = halves(query_grad)
        line[i, HEAD_ROWS - 1 : HEAD_ROWS, :] = query_top.astype(wide)
        both = jnp.where(row_id == HEAD_ROWS - 1, query_rest.astype(wide), mixed[i])
        start = i * SENT_ROWS + HEAD_ROWS
        sent[start : start + HEAD_ROWS, :] = both.astype(low)
        sent[start + HEAD_ROWS : start + 2 * HEAD_ROWS, :] = line[i].astype(low)


def head_call(sz, meta, fin, cot, vec, block, weight):
    w, f, n = sz.width, sz.hidden, sz.images

    def out(shape, dtype):
        return jax.ShapeDtypeStruct(shape, dtype)

    shapes = [
        out((n, HEAD_ROWS, sz.length), wide),
        out((n, HEAD_ROWS, sz.length), wide),
        out((n, HEAD_ROWS, w), wide),
        out((HEAD_ROWS, w), wide),
        out((n * SENT_ROWS, w), low),
        out((8, w), wide),
    ]
    ins = (fin, cot, vec)
    return pl.pallas_call(
        functools.partial(head_body, sz.images, sz.blocks, f // w),
        grid_spec=pltpu.PrefetchScalarGridSpec(
            num_scalar_prefetch=1,
            grid=(1,),
            in_specs=[whole(v.shape) for v in ins]
            + [pl.BlockSpec((w, AHEAD * w), lambda *_: (0, 0), pipeline_mode=pl.Buffered(1))]
            + [anywhere] * 3,
            out_specs=[pl.BlockSpec(s.shape, lambda *_, r=len(s.shape): (0,) * r) for s in shapes],
            scratch_shapes=[
                pltpu.VMEM((HEAD_ROWS, sz.length), wide),
                pltpu.VMEM((n, HEAD_ROWS, w), wide),
                pltpu.VMEM((n, HEAD_ROWS, w), wide),
            ]
            + held_scratch(weight),
        ),
        out_shape=shapes,
        compiler_params=params(1),
        cost_estimate=cost(16 * 8 * w * f, sz.rows * w * 2 + 4 * w * f + 8 * w * w),
        name="head",
    )(meta, *ins, block, *weight)


def back_body(
    meta, fin, enc, res, att, slope, g_score, shares, lift, probe_w, spread, vec, weight,
    g_mlp, g_hidden, g_res, g_branch, g_att, delta, sums,
):
    @pl.when(is_first())
    def _():
        sums[...] = jnp.zeros_like(sums)

    @pl.when(pl.program_id(1) < meta[pl.program_id(0)])
    def _():
        width = fin.shape[1]
        fold = slope.shape[1] // width

        def part_of(k):
            return weight[:, (AHEAD + k) * width : (AHEAD + k + 1) * width]

        lift_top, lift_rest = halves(lift[0])
        probe_top, probe_rest = halves(probe_w[...])
        top, rest = halves(g_score[0])
        share_top, share_rest = halves(shares[0])
        left = jnp.concatenate([top, share_top, rest, share_rest, top, share_top], axis=0)
        right = jnp.concatenate(
            [probe_top, lift_top, probe_top, lift_top, probe_rest, lift_rest], axis=0
        )
        g_fin = dot_tn(left, right)
        normal, scale = normalise(enc[...])
        sums[0:1, :] += column_sum(g_fin * normal)
        sums[1:2, :] += column_sum(g_fin)
        g_enc = norm_back(g_fin, row_of(vec, FINAL_GAIN), normal, scale)
        low_enc = g_enc.astype(low)
        g_mlp[...] = low_enc
        sums[2:3, :] += column_sum(low_enc.astype(wide))
        back = jnp.zeros_like(g_enc)
        for part in range(fold):
            cols = slice(part * width, (part + 1) * width)
            grad = dot_nt(low_enc, part_of(1 + fold + part))
            grad = (grad * slope[:, cols].astype(wide)).astype(low)
            g_hidden[:, cols] = grad
            sums[8 + part : 9 + part, :] += column_sum(grad.astype(wide))
            back = back + dot_nt(grad, part_of(1 + part))
        normal, scale = normalise(res[...])
        sums[3:4, :] += column_sum(back * normal)
        sums[4:5, :] += column_sum(back)
        total = g_enc + norm_back(back, row_of(vec, NORM2_GAIN), normal, scale)
        g_res[...] = total
        low_res = total.astype(low)
        g_branch[...] = low_res
        sums[5:6, :] += column_sum(low_res.astype(wide))
        grad = dot_nt(low_res, part_of(0)).astype(low)
        g_att[...] = grad
        top, rest = halves(grad.astype(wide) * att[...].astype(wide))
        delta[0] = dot_nt(spread[...], top) + dot_nt(spread[...], rest)


def back_call(
    sz, meta, fin, enc, res, att, slope, g_score, shares, lift, probe_w, vec, weight
):
    w, f, n = sz.width, sz.hidden, sz.images
    lines = 8 * sz.pairs
    line = lax.broadcasted_iota(jnp.int32, (lines, w), 0)
    head = lax.broadcasted_iota(jnp.int32, (lines, w), 1) // HEAD_DIM
    spread = (head == 2 * (line // 8) + line % 8).astype(low)
    fixed = (probe_w, spread, vec, weight)

    def out(shape, dtype):
        return jax.ShapeDtypeStruct(shape, dtype)

    def kept(shape):
        return pl.BlockSpec(shape, lambda i, b, m: (0, 0))

    return pl.pallas_call(
        back_body,
        grid_spec=pltpu.PrefetchScalarGridSpec(
            num_scalar_prefetch=1,
            grid=(n, sz.blocks),
            in_specs=[
                sz.row_spec(w), sz.row_spec(w), sz.row_spec(w), sz.row_spec(w), sz.row_spec(f),
                sz.lane_spec(HEAD_ROWS), sz.lane_spec(HEAD_ROWS), sz.image_spec(HEAD_ROWS, w),
            ]
            + [whole(v.shape) for v in fixed],
            out_specs=[
                sz.row_spec(w), sz.row_spec(f), sz.row_spec(w), sz.row_spec(w), sz.row_spec(w),
                sz.lane_spec(lines), kept((16, w)),
            ],
        ),
        out_shape=[
            out((sz.rows, w), low), out((sz.rows, f), low), out((sz.rows, w), wide),
            out((sz.rows, w), low), out((sz.rows, w), low), out((n, lines, sz.length), wide),
            out((16, w), wide),
        ],
        compiler_params=params(2),
        cost_estimate=cost(
            sz.rows * w * (2 * w + 4 * f), sz.rows * (22 * w + 4 * f) + 4 * w * f
        ),
        name="mlp_back",
    )(meta, fin, enc, res, att, slope, g_score, shares, lift, *fixed)


def outer_body(images, blocks, units, meta, a_ref, b_ref, out_ref, acc):
    span = blocks * BLOCK

    def finish(term):
        if units == 0:
            out_ref[...] = term.astype(out_ref.dtype)
            return
        rows = term.shape[0] // units
        for u in range(units):
            out_ref[meta[2 * images + units + u]] = term[u * rows : (u + 1) * rows].astype(low)

    for i in range(images):
        for keys in range(blocks + 1):

            @pl.when(meta[i] == keys)
            def _(i=i, keys=keys):
                if keys:
                    rows = slice(i * span, i * span + keys * BLOCK)
                    term = dot_tn(a_ref[rows, :], b_ref[rows, :])
                else:
                    term = jnp.zeros(acc.shape, wide)
                if i > 0:
                    term = term + acc[...]
                if i < images - 1:
                    acc[...] = term
                else:
                    finish(term)


def outer_block_body(
    images, blocks, fold, meta, att_ref, g_att_ref, n2_ref, g_hidden_ref, act_ref, g_mlp_ref, out_ref, acc
):
    step = pl.program_id(0)
    for live, a_ref, b_ref in (
        (step == 0, att_ref, g_att_ref),
        ((step > 0) & (step <= fold), n2_ref, g_hidden_ref),
        (step > fold, act_ref, g_mlp_ref),
    ):
        pl.when(live)(
            functools.partial(outer_body, images, blocks, 0, meta, a_ref, b_ref, out_ref, acc)
        )


def outer_block_call(sz, meta, att, g_branch, n2, g_hidden, act, g_mlp):
    w, fold = sz.width, sz.hidden // sz.width
    one = whole((sz.rows, w))

    def part(first):
        return pl.BlockSpec((sz.rows, w), lambda j, c: (0, jnp.clip(j - first, 0, fold - 1)))

    return pl.pallas_call(
        functools.partial(outer_block_body, sz.images, sz.blocks, fold),
        grid_spec=pltpu.PrefetchScalarGridSpec(
            num_scalar_prefetch=1,
            grid=(1 + 2 * fold,),
            in_specs=[one, one, one, part(1), part(1 + fold), one],
            out_specs=pl.BlockSpec((w, w), lambda j, c: (0, j)),
            scratch_shapes=[pltpu.VMEM((w, w), wide)],
        ),
        out_shape=jax.ShapeDtypeStruct((w, (1 + 2 * fold) * w), low),
        compiler_params=params(1),
        cost_estimate=cost(2 * sz.rows * w * w * (1 + 2 * fold), 2 * sz.rows * w * (2 * fold + 4)),
        name="grad_block",
    )(meta, att, g_branch, n2, g_hidden, act, g_mlp)


def outer_qkv_body(images, blocks, units, meta, n1_ref, dq_ref, dk_ref, dv_ref, out_ref, acc):
    for k, b_ref in enumerate((dq_ref, dk_ref, dv_ref)):
        pl.when(pl.program_id(0) == k)(
            functools.partial(outer_body, images, blocks, units, meta, n1_ref, b_ref, out_ref, acc)
        )


def outer_qkv_call(sz, meta, n1, dq, dk, dv, units):
    w = sz.width
    return pl.pallas_call(
        functools.partial(outer_qkv_body, sz.images, sz.blocks, units),
        grid_spec=pltpu.PrefetchScalarGridSpec(
            num_scalar_prefetch=1,
            grid=(3,),
            in_specs=[whole((sz.rows, w))] * 4,
            out_specs=pl.BlockSpec((units, w // units, w), lambda j, c: (0, 0, j)),
            scratch_shapes=[pltpu.VMEM((w, w), wide)],
        ),
        out_shape=jax.ShapeDtypeStruct((units, w // units, 3 * w), low),
        compiler_params=params(1),
        cost_estimate=cost(6 * sz.rows * w * w, 8 * sz.rows * w),
        name="grad_qkv",
    )(meta, n1, dq, dk, dv)


def place_body(at, kept, taken, out):
    i = pl.program_id(0)

    @pl.when(at[2 * i] == 1)
    def _():
        out[...] = kept[0]

    @pl.when(at[2 * i] == 0)
    def _():
        out[...] = taken[...].astype(wide)


def place_call(at, kept, taken, groups, rows):
    width = kept.shape[-1]
    spec = pl.BlockSpec((1, rows, width), lambda i, at: (at[2 * i + 1], 0, 0))
    kept_spec = pl.BlockSpec(
        (1, 1, rows, width), lambda i, at: (at[2 * i + 1], at[2 * groups], 0, 0)
    )
    return pl.pallas_call(
        place_body,
        grid_spec=pltpu.PrefetchScalarGridSpec(
            num_scalar_prefetch=1,
            grid=(groups,),
            in_specs=[kept_spec, spec],
            out_specs=pl.BlockSpec((1, rows, width), lambda i, at: (i, 0, 0)),
        ),
        out_shape=jax.ShapeDtypeStruct((groups, rows, width), wide),
        compiler_params=params(1),
        cost_estimate=cost(0, groups * rows * width * 10),
        name="place",
    )(at, kept, taken)


def attend_back_body(
    images, blocks, meta, q_ref, k_ref, v_ref, g_ref, lse_ref, delta_ref, dq_ref, dk_ref, dv_ref,
    dk_acc, dv_acc,
):
    at = pl.program_id(0)
    count, length = meta[at], meta[images + at]
    lane = lax.broadcasted_iota(jnp.int32, (BLOCK, PAIR), 1)
    first = lane < HEAD_DIM

    def keep(value, head):
        own = first if head == 0 else jnp.logical_not(first)
        zero = jnp.zeros_like(value[:BLOCK])
        return jnp.concatenate(
            [
                jnp.where(own, value[r : r + BLOCK], zero)
                for r in range(0, value.shape[0], BLOCK)
            ],
            axis=0,
        )

    def variant(keys_in):
        near = keys_in - BLOCK
        valid = lax.broadcasted_iota(jnp.int32, (BLOCK, BLOCK), 0) + near < length
        keys = k_ref[:keys_in, :]
        kept_keys = [keep(keys, head) for head in range(2)]
        values = v_ref[:keys_in, :]
        kept_values = [keep(values, head) for head in range(2)]
        dk_acc[:keys_in, :] = jnp.zeros((keys_in, PAIR), wide)
        dv_acc[:keys_in, :] = jnp.zeros((keys_in, PAIR), wide)

        @pl.loop(0, count)
        def _(step):
            rows = pl.ds(pl.multiple_of(step * BLOCK, BLOCK), BLOCK)
            q, g = q_ref[rows, :], g_ref[rows, :]
            dq = None
            for head in range(2):
                log = lse_ref[0, head : head + 1, rows]
                drop = delta_ref[0, head : head + 1, rows]
                score = dot_nt(kept_keys[head], q) * 0.125
                share = jnp.exp(score - log)
                if near:
                    share = jnp.concatenate(
                        [share[:near], jnp.where(valid, share[near:], 0.0)], axis=0
                    )
                else:
                    share = jnp.where(valid, share, 0.0)
                reach = dot_nt(kept_values[head], g)
                grad = (share * (reach - drop)).astype(low)
                dv_acc[:keys_in, :] += dot_nn(share.astype(low), keep(g, head))
                dk_acc[:keys_in, :] += dot_nn(grad, keep(q, head))
                term = dot_tn(grad, kept_keys[head])
                dq = term if dq is None else dq + term
            dq_ref[rows, :] = (dq * 0.125).astype(low)

        dk_ref[:keys_in, :] = (dk_acc[:keys_in, :] * 0.125).astype(low)
        dv_ref[:keys_in, :] = dv_acc[:keys_in, :].astype(low)

    for keys in range(1, blocks + 1):
        pl.when(count == keys)(functools.partial(variant, keys * BLOCK))


def attend_back_call(sz, meta, qkv, g_att, lse, delta):
    pairs = sz.pairs

    def spec(part):
        return pl.BlockSpec((sz.length, PAIR), lambda i, p, m: (i, part * pairs + p))

    line = pl.BlockSpec((1, 8, sz.length), lambda i, p, m: (i, p, 0))
    out = jax.ShapeDtypeStruct((sz.rows, sz.width), low)
    return pl.pallas_call(
        functools.partial(attend_back_body, sz.images, sz.blocks),
        grid_spec=pltpu.PrefetchScalarGridSpec(
            num_scalar_prefetch=1,
            grid=(sz.images, pairs),
            in_specs=[spec(0), spec(1), spec(2), spec(0), line, line],
            out_specs=[spec(0), spec(0), spec(0)],
            scratch_shapes=[pltpu.VMEM((sz.length, PAIR), wide)] * 2,
        ),
        out_shape=[out, out, out],
        compiler_params=params(2),
        cost_estimate=cost(
            10 * sz.rows * sz.length * sz.width,
            14 * sz.rows * sz.width,
            sz.rows * sz.length * HEADS,
        ),
        name="attend_back",
    )(meta, qkv, qkv, qkv, g_att, lse, delta)


def qkv_back_body(
    base, meta, x, g_res, dq, dk, dv, vec, mine, theirs, grad_ref, low_ref, sums, held, sems
):
    @pl.when(is_first())
    def _():
        fetch_all(meta, base, (mine, theirs), held, sems)
        sums[...] = jnp.zeros_like(sums)

    live = pl.program_id(1) < meta[pl.program_id(0)]

    @pl.when(live)
    def _():
        width = x.shape[1]
        normal, scale = normalise(x[...].astype(wide))
        back = None
        for part, ref in enumerate((dq, dk, dv)):
            term = dot_nt(ref[...], columns(held, part * width, width))
            back = term if back is None else back + term
        sums[0:1, :] += column_sum(back * normal)
        sums[1:2, :] += column_sum(back)
        sums[2:3, :] += column_sum(dq[...].astype(wide))
        sums[3:4, :] += column_sum(dv[...].astype(wide))
        grad = g_res[...] + norm_back(back, row_of(vec, NORM1_GAIN), normal, scale)
        grad_ref[...] = grad
        low_ref[...] = grad.astype(low)

    @pl.when(jnp.logical_not(live))
    def _():
        grad_ref[...] = jnp.zeros_like(grad_ref)
        low_ref[...] = jnp.zeros_like(low_ref)


def qkv_back_call(sz, meta, x, g_res, dq, dk, dv, vec, weight):
    w, blocks = sz.width, sz.blocks
    plain = pl.BlockSpec((BLOCK, w), lambda i, b, m: (i * blocks + b, 0))
    return pl.pallas_call(
        functools.partial(qkv_back_body, 2 * sz.images),
        grid_spec=pltpu.PrefetchScalarGridSpec(
            num_scalar_prefetch=1,
            grid=(sz.images, blocks),
            in_specs=[sz.row_spec(w)] * 5 + [whole(vec.shape), anywhere, anywhere],
            out_specs=[plain, plain, pl.BlockSpec((8, w), lambda i, b, m: (0, 0))],
            scratch_shapes=held_scratch(weight),
        ),
        out_shape=[
            jax.ShapeDtypeStruct((sz.rows, w), wide),
            jax.ShapeDtypeStruct((sz.rows, w), low),
            jax.ShapeDtypeStruct((8, w), wide),
        ],
        compiler_params=params(2),
        cost_estimate=cost(6 * sz.rows * w * w, sz.rows * w * 18 + 6 * w * w),
        name="qkv_back",
    )(meta, x, g_res, dq, dk, dv, vec, *weight)


axes = ("img", "seq")


def bits_of(count):
    return [1 << k for k in range(count.bit_length() - 1)]


def tied(value, *after):
    return lax.optimization_barrier((value, *after))[0]


def together(*values):
    return lax.optimization_barrier(values)


def cut(size, shares):
    edges = [round(size * sum(shares[:k]) / sum(shares) / 16) * 16 for k in range(len(shares) + 1)]
    return [slice(p, q) for p, q in zip(edges[:-1], edges[1:], strict=True)]


class Wires:
    def __init__(self, img_count, seq_count):
        self.count, self.seq_count = img_count * seq_count, seq_count
        self.core = seq_count
        self.units = img_count
        self.seq_bits = bits_of(seq_count)
        inner = [bit for bit in bits_of(self.count) if bit > self.core]
        inner = inner[:1] + inner[:0:-1]
        self.orders = (inner, inner[1:] + inner[:1])

    def swap(self, value, bit):
        return lax.ppermute(value, axes, [(i, i ^ bit) for i in range(self.count)])

    def step(self, value, at):
        pairs = [(i, i ^ self.orders[1 if i & self.core else 0][at]) for i in range(self.count)]
        return lax.ppermute(value, axes, pairs)

    def tables(self, me):
        img = me // self.seq_count
        core = img % 2

        def at(place, side):
            by_core = []
            for order in self.orders:
                unit = 0
                for k, bit in enumerate(order):
                    unit |= ((place >> k) & 1) * (bit // self.seq_count)
                by_core.append(unit)
            which = core if side == 0 else 1 - core
            return (img ^ side) ^ jnp.where(which == 0, by_core[0], by_core[1])

        def place(unit):
            side = (unit ^ img) & 1
            delta = unit ^ img
            by_core = []
            for order in self.orders:
                total = jnp.zeros((), jnp.int32)
                for k, bit in enumerate(order):
                    shift = (bit // self.seq_count).bit_length() - 1
                    total = total | (((delta >> shift) & 1) << k)
                by_core.append(total)
            which = core ^ side
            return side * (self.units // 2) + jnp.where(which == 0, by_core[0], by_core[1])

        half = self.units // 2
        order = [at(k, side) for side in range(2) for k in range(half)]
        inverse = [place(unit) for unit in range(self.units)]
        return jnp.stack(order + inverse)

    def join_seq(self, value, me):
        for bit in self.seq_bits:
            other = self.swap(value, bit)
            value = jnp.where(
                (me & bit) > 0,
                jnp.concatenate([other, value], axis=0),
                jnp.concatenate([value, other], axis=0),
            )
        return value

    def joined(self, value, at):
        return jnp.concatenate([value, self.step(value, at)], axis=0)

    def halved(self, value, at):
        half = value.shape[0] // 2
        return value[:half] + self.step(value[half:], at)

    def small_scatter(self, value, me, bits):
        for bit in reversed(bits):
            value = self.small_half(value, me, bit)
        return value[0]

    def small_half(self, value, me, bit):
        pair = value.reshape((2, value.shape[0] // 2) + value.shape[1:])
        up = (me & bit) > 0
        return jnp.where(up, pair[1], pair[0]) + self.swap(jnp.where(up, pair[0], pair[1]), bit)


def local(img_count, seq_count, *args):
    (
        patches, lengths, pooled_cot, norm1_gain, norm1_bias, qkv_weight, query_bias, value_bias,
        attn_weight, attn_bias, norm2_gain, norm2_bias, fc1_weight, fc1_bias, fc2_weight, fc2_bias,
        final_gain, final_bias, probe_vector, pool_query_weight, pool_query_bias, pool_kv_weight,
        pool_value_bias, pool_out_weight, pool_out_bias, head_gain, head_bias, head_fc1_weight,
        head_fc1_bias, head_fc2_weight, head_fc2_bias,
    ) = args
    count = img_count * seq_count
    groups, part_rows, width = patches.shape
    length = part_rows * seq_count
    hidden = fc1_weight.shape[1]
    images = max(1, groups // seq_count)
    share = max(1, seq_count // groups)
    own = width // count
    per = hidden // count
    fold = hidden // width
    sz = Sizes(images, length, width, hidden)
    wires = Wires(img_count, seq_count)
    me = lax.axis_index(axes)
    seq_at = lax.axis_index("seq")
    first_image = (seq_at // share) * images

    slots = list(range(groups))
    if share == 1:
        turn = [r % seq_count if (r // seq_count) % 2 == 0 else -1 - r % seq_count for r in slots]
        slots = [(t % seq_count) * images + r // seq_count for r, t in zip(slots, turn, strict=True)]
        ahead = (lengths[None, :] > lengths[:, None]) | (
            (lengths[None, :] == lengths[:, None])
            & (jnp.arange(groups)[None, :] < jnp.arange(groups)[:, None])
        )
        rank = jnp.sum(ahead, axis=1)
        slot_of = sum(jnp.where(rank == r, slot, 0) for r, slot in enumerate(slots))
    else:
        slot_of = jnp.arange(groups)
    order = jnp.sum(
        jnp.where(slot_of[None, :] == jnp.arange(groups)[:, None], jnp.arange(groups)[None, :], 0),
        axis=1,
    )

    def of_slots(value, first):
        at = lax.dynamic_slice_in_dim(order, first, images)
        return jnp.concatenate(
            [lax.dynamic_slice_in_dim(value, at[k], 1) for k in range(images)], axis=0
        )

    own_lengths = of_slots(lengths, first_image)
    own_lengths = jnp.where(seq_at % share == 0, own_lengths, 0)
    own_cot = of_slots(pooled_cot, first_image)
    meta = jnp.concatenate(
        [(own_lengths + BLOCK - 1) // BLOCK, own_lengths, wires.tables(me)]
    ).astype(jnp.int32)

    def by_unit(bias):
        return bias.reshape(own, fold).T

    vectors = [
        v.reshape(1, own)
        for v in (
            norm1_gain, norm1_bias, query_bias, value_bias, attn_bias, norm2_gain, norm2_bias,
            fc2_bias, final_gain, final_bias, pool_query_bias, pool_value_bias, pool_out_bias,
            head_gain, head_bias, head_fc2_bias, probe_vector,
        )
    ]
    vectors += [by_unit(fc1_bias), by_unit(head_fc1_bias)]
    unit_a, block, pack = packs_call(
        vectors, qkv_weight, pool_kv_weight, pool_query_weight, attn_weight, fc1_weight, fc2_weight,
        pool_out_weight, head_fc1_weight, head_fc2_weight,
    )
    block = lax.all_gather(block, axes, axis=0, tiled=True)

    pairwise = seq_count == 2 and share == 1
    steps = len(wires.orders[0])
    if pairwise:
        kept = of_slots(patches, first_image)
        given = of_slots(patches, (1 - seq_at) * images)
        parts = cut(part_rows, list(range(2, steps + 2)))
    else:
        ordered = jnp.concatenate(
            [lax.dynamic_slice_in_dim(patches, order[k], 1) for k in range(groups)], axis=0
        )
        given = jnp.repeat(ordered, share, axis=0)
    mine = wires.join_seq(unit_a, me)[None]
    mine, given = together(mine, given)
    taken = []
    for at in range(steps):
        mine = wires.joined(mine, at)
        if pairwise:
            mine, one = together(mine, wires.swap(given[:, parts[at]], 1))
            taken.append(one)
        if at == 1:
            mine, meta = together(mine, meta)
    mine, pack = together(mine, pack)
    theirs = wires.swap(mine, wires.core)
    theirs, pack = together(theirs, pack)
    qkv_full = (mine, theirs)
    if pairwise:
        taken = jnp.concatenate(taken, axis=1)
        x = jnp.where(
            seq_at == 0,
            jnp.concatenate([kept, taken], axis=1),
            jnp.concatenate([taken, kept], axis=1),
        )
    else:
        x = lax.all_to_all(given, "seq", split_axis=0, concat_axis=1, tiled=True)
    x = x.reshape(sz.rows, width)

    qkv, n1, vec = qkv_call(sz, meta, x, qkv_full)
    pack = wires.join_seq(pack, me)[None]
    qkv, pack = together(qkv, pack)
    done, forward = 0, ()
    for at in range(images):
        forward = attend_call(sz, meta, qkv, at, forward)
        stop = steps - 1 if at == images - 1 else min(done + 1, steps - 1)
        while done < stop:
            pack = wires.joined(pack, done)
            done += 1
        *forward, pack = together(*forward, pack)
    att, lse = forward
    res, n2, slope, act, enc, fin = mlp_call(sz, meta, x, att, vec, block)
    other = wires.swap(pack, wires.core)
    pack_rest = wires.step(pack, steps - 1)
    fin, other, pack_rest = together(fin, other, pack_rest)
    other_rest = wires.swap(pack_rest, wires.core)
    head_full = (jnp.concatenate([pack, pack_rest], axis=0), other, other_rest)
    cot_rows = jnp.pad(own_cot, ((0, HEAD_ROWS - images), (0, 0)))
    shares, g_score, lift, probe_w, sent, head_sums = head_call(
        sz, meta, fin, cot_rows, vec, block, head_full
    )
    rows = lax.all_gather(sent, axes, axis=0, tiled=True)

    g_mlp, g_hidden, g_res, g_branch, g_att, delta, back_sums = back_call(
        sz, meta, fin, enc, res, att, slope, g_score, shares, lift, probe_w, vec, block
    )
    terms = outer_block_call(sz, meta, att, g_branch, n2, g_hidden, act, g_mlp)
    terms, g_att, rows = together(terms, g_att, rows)
    totals = lax.psum_scatter(terms, axes, scatter_dimension=0, tiled=True)

    def by_column(grad):
        return grad.reshape(own, fold, width).transpose(0, 2, 1).reshape(own, hidden)

    def own_part(v, axis=-1):
        return lax.dynamic_slice_in_dim(v, me * own, own, axis=axis)

    half = wires.units // 2
    dq, dk, dv = attend_back_call(sz, meta, qkv, g_att, lse, delta)
    last = outer_qkv_call(sz, meta, n1, dq, dk, dv, wires.units)
    g_res, last = together(g_res, last)
    last = last[:half] + wires.swap(last[half:], wires.core)
    patch_grad, patch_low, qkv_sums = qkv_back_call(sz, meta, x, g_res, dq, dk, dv, vec, qkv_full)
    patch_low = patch_low.reshape(images, length, width)
    sums = jnp.concatenate(
        [back_sums[:6], head_sums[:2], qkv_sums[:4], back_sums[8 : 8 + fold]], axis=0
    )
    sums = sums.reshape(-1, count, own).transpose(1, 0, 2)
    if pairwise:
        given = lax.dynamic_slice_in_dim(patch_low, (1 - seq_at) * part_rows, part_rows, axis=1)
    else:
        given = lax.all_to_all(patch_low, "seq", split_axis=1, concat_axis=0, tiled=True)[::share]

    def head_part(rows):
        narrow = own_part(rows.reshape(count * images, SENT_ROWS, width))
        rows = rows.reshape(count * images, SENT_ROWS, width)
        act_own = narrow[:, SENT_ACT : SENT_ACT + fold].transpose(0, 2, 1).reshape(-1, per)
        grad_pool_v = jnp.einsum(
            "ihr,ihd->rhd",
            narrow[:, :HEADS],
            rows[:, SENT_PULL].reshape(-1, HEADS, HEAD_DIM),
            preferred_element_type=wide,
        ).reshape(own, width)
        return (
            dot_tn(act_own, rows[:, SENT_COT]),
            dot_tn(narrow[:, SENT_POOLED], rows[:, SENT_BRANCH]),
            grad_pool_v,
            narrow[:, SENT_NORMED],
            jnp.sum(narrow[:, SENT_MIX : SENT_MIX + HEADS].astype(wide), axis=0),
        )

    def hidden_part(rows, normed_own):
        rows = rows.reshape(count * images, SENT_ROWS, width)
        head_grad = rows[:, SENT_GRAD : SENT_GRAD + fold].reshape(count * images, hidden)
        return by_column(dot_tn(normed_own, head_grad))

    def sums_part(rows, mix_own):
        rows = rows.reshape(count * images, SENT_ROWS, width)
        row_sums = jnp.sum(rows[:, 2 * HEAD_ROWS - 1 :].astype(wide), axis=0)
        query_grad = row_sums[SENT_QUERY - 2 * HEAD_ROWS + 1] + row_sums[0]
        pool_query = probe_w[HEADS]
        grad_pool_k = (
            0.125 * mix_own.T[:, :, None] * pool_query.reshape(1, HEADS, HEAD_DIM)
        ).reshape(own, width)
        pooled = rows[:, SENT_OUT].astype(wide) + rows[:, SENT_OUT_REST].astype(wide)
        pooled = pooled.reshape(img_count, seq_count, images, width)[:, ::share]
        pooled = lax.dynamic_index_in_dim(pooled, me // seq_count, 0, keepdims=False)
        pooled = pooled.reshape(groups, width)
        pooled = jnp.concatenate(
            [lax.dynamic_slice_in_dim(pooled, slot_of[k], 1) for k in range(groups)], axis=0
        )
        return (
            pooled,
            probe_vector.astype(wide)[:, None] * query_grad[None, :],
            jnp.sum(pool_query_weight.astype(wide) * query_grad[None, :], axis=1),
            grad_pool_k,
            own_part(query_grad),
            own_part(row_sums),
        )

    last, sums, given, rows = together(last, sums, given, rows)
    parts, taken, made = cut(part_rows, (1,) * steps), [], []
    bits = list(reversed(bits_of(count)))
    for tick, at in enumerate(reversed(range(steps))):
        last = wires.halved(last, at)
        sums = wires.small_half(sums, me, bits.pop(0))
        taken.append(wires.swap(given[:, parts[tick]], 1) if pairwise else given)
        if tick == 0:
            made.append(head_part(rows))
        elif tick == 1:
            made.append(hidden_part(rows, made[0][3]))
        elif tick == 2:
            made.append(sums_part(rows, made[0][4]))
        last, sums, rows, taken, made = together(last, sums, rows, taken, made)
    (grad_head_fc2, grad_pool_out, grad_pool_v, _, _), grad_head_fc1, made = made
    pooled, grad_pool_query_weight, grad_probe, grad_pool_k, g_pool_query_bias, own_sums = made
    grad_pool_kv = jnp.concatenate([grad_pool_k, grad_pool_v], axis=1)

    def own_sum(at):
        return own_sums[at - 2 * HEAD_ROWS + 1]

    g_head_fc1_bias = own_sums[SENT_GRAD - 2 * HEAD_ROWS + 1 :][:fold].T.reshape(per)
    last = last.reshape(seq_count, own, 3 * width)
    for bit in reversed(wires.seq_bits):
        last = wires.small_half(last, me, bit)
    while bits:
        sums = wires.small_half(sums, me, bits.pop(0))
    if pairwise:
        at_slot = jnp.stack(
            [(slot_of // images == seq_at).astype(jnp.int32), slot_of % images], axis=1
        )
        at_slot = jnp.concatenate([at_slot.reshape(-1), seq_at[None]]).astype(jnp.int32)
        patch_grad = place_call(
            at_slot,
            patch_grad.reshape(images, seq_count, part_rows, width),
            jnp.concatenate(taken, axis=1),
            groups,
            part_rows,
        )
    else:
        patch_grad = jnp.concatenate(
            [lax.dynamic_slice_in_dim(taken[0], slot_of[k], 1) for k in range(groups)], axis=0
        ).astype(wide)
    totals = totals.astype(wide)
    grad_attn = totals[:, :width]
    grad_fc1 = by_column(totals[:, width : width + hidden])
    grad_fc2 = totals[:, width + hidden :].reshape(per, width)
    grad_qkv = last[0].astype(wide)
    sums = sums[0]
    (
        g_final_gain, g_final_bias, g_fc2_bias, g_norm2_gain, g_norm2_bias, g_attn_bias,
        g_head_gain, g_head_bias, g_norm1_gain, g_norm1_bias, g_query_bias, g_value_bias,
    ) = sums[:12]
    g_fc1_bias = sums[12:].T.reshape(per)
    return (
        pooled, patch_grad, g_norm1_gain, g_norm1_bias, grad_qkv, g_query_bias, g_value_bias,
        grad_attn, g_attn_bias, g_norm2_gain, g_norm2_bias, grad_fc1, g_fc1_bias, grad_fc2,
        g_fc2_bias, g_final_gain, g_final_bias, grad_probe, grad_pool_query_weight,
        g_pool_query_bias, grad_pool_kv, own_sum(SENT_PULL), grad_pool_out,
        own_sum(SENT_BRANCH), g_head_gain, g_head_bias, grad_head_fc1,
        g_head_fc1_bias, grad_head_fc2, own_sum(SENT_COT),
    )


def solution(mesh):
    rows, vector = P(axes, None), P(axes)
    body = functools.partial(local, mesh.shape["img"], mesh.shape["seq"])
    vector_weights = (3, 4, 6, 7, 9, 10, 11, 13, 15, 16, 17, 18, 20, 22, 24, 25, 26, 28, 30)
    in_specs = (P("img", "seq", None), P("img"), P("img", None)) + tuple(
        vector if at in vector_weights else rows for at in range(3, 31)
    )
    out_specs = (P("img", None), P("img", "seq", None)) + in_specs[3:]
    return jax.shard_map(body, mesh=mesh, in_specs=in_specs, out_specs=out_specs, check_vma=False)
```

```python
import functools

import jax
import jax.numpy as jnp
from jax import lax
from jax.experimental import pallas as pl
from jax.experimental.pallas import tpu as pltpu
from jax.sharding import PartitionSpec as P

HEADS = 12
HEAD_DIM = 64
BLOCK = 256
PAIR = 128
SPAN = 512
BACK_SPAN = 256
wide = jnp.float32
low = jnp.bfloat16
masked_score = -1e30
base_two = 1.4426950408889634
score_scale = 0.125 * base_two
norm_epsilon = 1e-06
root_two_pi = 0.7978845608028654
vmem_bytes = 60 * 1024 * 1024


def dot_nn(a, b):
    return jnp.dot(a, b, preferred_element_type=wide)


def dot_nt(a, b):
    return lax.dot_general(a, b, (((1,), (1,)), ((), ())), preferred_element_type=wide)


def dot_tn(a, b):
    return lax.dot_general(a, b, (((0,), (0,)), ((), ())), preferred_element_type=wide)


def halves(v):
    top = v.astype(low)
    return top, (v - top.astype(wide)).astype(low)


def normalise(v):
    centred = v - jnp.mean(v, axis=-1, keepdims=True)
    spread = jnp.mean(centred * centred, axis=-1, keepdims=True)
    scale = lax.rsqrt(spread + norm_epsilon)
    return centred * scale, scale


def norm_back(grad, gain, normal, scale):
    gn = grad * gain
    return (
        gn
        - jnp.mean(gn, axis=-1, keepdims=True)
        - normal * jnp.mean(gn * normal, axis=-1, keepdims=True)
    ) * scale


def column_sum(v):
    return jnp.sum(v, axis=0, keepdims=True)


def params(rank):
    return pltpu.CompilerParams(
        dimension_semantics=("arbitrary",) * rank, vmem_limit_bytes=vmem_bytes
    )


def whole(shape):
    return pl.BlockSpec(
        shape, lambda *_: (0,) * len(shape), pipeline_mode=pl.Buffered(1)
    )


def cost(flops, nbytes, exps=0):
    return pl.CostEstimate(flops=int(flops), bytes_accessed=int(nbytes), transcendentals=int(exps))


class Sizes:
    def __init__(self, images, length, width, hidden):
        self.images, self.length, self.width, self.hidden = images, length, width, hidden
        self.rows = images * length
        self.blocks = length // BLOCK
        self.pairs = width // PAIR

        self.units = 0

    def row_spec(self, cols):
        blocks = self.blocks

        def index(i, b, meta):
            return i * blocks + jnp.clip(b, 0, jnp.maximum(meta[i] - 1, 0)), 0

        return pl.BlockSpec((BLOCK, cols), index)

    def lane_spec(self, rows):
        def index(i, b, meta):
            return i, 0, jnp.clip(b, 0, jnp.maximum(meta[i] - 1, 0))

        return pl.BlockSpec((1, rows, BLOCK), index)

    def image_spec(self, rows, cols):
        return pl.BlockSpec((1, rows, cols), lambda i, b, meta: (i, 0, 0))


(
    NORM1_GAIN,
    NORM1_BIAS,
    QUERY_BIAS,
    VALUE_BIAS,
    ATTN_BIAS,
    NORM2_GAIN,
    NORM2_BIAS,
    FC2_BIAS,
    FINAL_GAIN,
    FINAL_BIAS,
    POOL_QUERY_BIAS,
    POOL_VALUE_BIAS,
    POOL_OUT_BIAS,
    HEAD_GAIN,
    HEAD_BIAS,
    HEAD_FC2_BIAS,
) = range(16)


PROBE = 16
FC1_BIAS = 17
VECTORS = 32


def row_of(ref, at):
    return ref[at : at + 1, :]


anywhere = pl.BlockSpec(memory_space=pl.ANY)


def fetch_all(meta, base, parts, held, sems):
    copies, place = [], 0
    for part in parts:
        for k in range(part.shape[0]):
            copies.append(
                pltpu.make_async_copy(part.at[k], held.at[meta[base + place]], sems.at[place])
            )
            place += 1
    for copy in copies:
        copy.start()
    for copy in copies:
        copy.wait()


def held_scratch(parts):
    units = sum(part.shape[0] for part in parts)
    return [
        pltpu.VMEM((units,) + parts[0].shape[1:], parts[0].dtype),
        pltpu.SemaphoreType.DMA((units,)),
    ]


def columns(held, start, size):
    units, rows, _ = held.shape
    return held[:, :, start : start + size].reshape(units * rows, size)


def is_first():
    return (pl.program_id(0) == 0) & (pl.program_id(1) == 0)


def packs_body(count, *refs):
    rows = refs[:count]
    qkv, pool_kv, pool_query, attn, fc1, fc2, pool_out, head_fc1, head_fc2 = refs[count:-4]
    first, block, head, lines = refs[-4:]
    own, width = attn.shape
    fold = fc1.shape[1] // width
    chunk = fold * PAIR
    at_from = lax.broadcasted_iota(jnp.int32, (chunk, chunk), 0)
    at_to = lax.broadcasted_iota(jnp.int32, (chunk, chunk), 1)
    spread = jnp.where(at_from == (at_to % PAIR) * fold + at_to // PAIR, 1.0, 0.0).astype(low)
    row_from = lax.broadcasted_iota(jnp.int32, (own, own * fold), 1)
    row_to = lax.broadcasted_iota(jnp.int32, (own, own * fold), 0)

    def by_part(ref, out, start):
        for k in range(width // PAIR):
            value = dot_nn(ref[:, k * chunk : (k + 1) * chunk], spread).astype(low)
            for j in range(fold):
                to = start + j * width + k * PAIR
                out[:, to : to + PAIR] = value[:, j * PAIR : (j + 1) * PAIR]

    def by_row(ref, out, start):
        for j in range(fold):
            pick = jnp.where(row_from == row_to * fold + j, 1.0, 0.0).astype(low)
            to = start + j * width
            out[:, to : to + width] = dot_nn(pick, ref[...]).astype(low)

    lines[...] = jnp.zeros_like(lines)
    at = 0
    for ref in rows:
        lines[at : at + ref.shape[0], :own] = ref[...].astype(wide)
        at += ref.shape[0]
    first[:, : 3 * width] = qkv[...]
    first[:, 3 * width :] = lines[...].T[:own].astype(low)
    block[:, : 2 * width] = pool_kv[...]
    block[:, 2 * width : 3 * width] = pool_query[...]
    block[:, 3 * width : 4 * width] = pool_out[...]
    block[:, 4 * width : 5 * width] = attn[...]
    by_part(fc1, block, 5 * width)
    by_row(fc2, block, (5 + fold) * width)
    by_part(head_fc1, head, 0)
    by_row(head_fc2, head, fold * width)


def packs_call(rows, *weights):
    own, width = weights[3].shape
    fold = weights[4].shape[1] // width
    ins = (*rows, *weights)
    vmem = pl.BlockSpec(memory_space=pltpu.VMEM)
    return pl.pallas_call(
        functools.partial(packs_body, len(rows)),
        in_specs=[vmem] * len(ins),
        out_specs=[vmem] * 3,
        out_shape=[
            jax.ShapeDtypeStruct((own, cols), low)
            for cols in (3 * width + PAIR, (5 + 2 * fold) * width, 2 * fold * width)
        ],
        scratch_shapes=[pltpu.VMEM((PAIR, PAIR), wide)],
        compiler_params=params(0),
        cost_estimate=cost(0, 4 * own * width * (9 + 4 * fold)),
        name="packs",
    )(*ins)


def qkv_body(base, meta, x, mine, theirs, qkv, normed, vec, held, sems):
    width = x.shape[1]

    @pl.when(is_first())
    def _():
        fetch_all(meta, base, (mine, theirs), held, sems)
        vec[...] = columns(held, 3 * width, PAIR).astype(wide).T[:VECTORS]

    @pl.when(pl.program_id(1) < meta[pl.program_id(0)])
    def _():
        normal, _ = normalise(x[...].astype(wide))
        rows = (normal * row_of(vec, NORM1_GAIN) + row_of(vec, NORM1_BIAS)).astype(low)
        normed[...] = rows
        for part, bias in enumerate((QUERY_BIAS, None, VALUE_BIAS)):
            out = dot_nn(rows, columns(held, part * width, width))
            if bias is not None:
                out = out + row_of(vec, bias)
            qkv[:, part * width : (part + 1) * width] = out.astype(low)


def qkv_call(sz, meta, x, weight):
    w = sz.width
    return pl.pallas_call(
        functools.partial(qkv_body, 2 * sz.images),
        grid_spec=pltpu.PrefetchScalarGridSpec(
            num_scalar_prefetch=1,
            grid=(sz.images, sz.blocks),
            in_specs=[sz.row_spec(w), anywhere, anywhere],
            out_specs=[
                sz.row_spec(3 * w),
                sz.row_spec(w),
                pl.BlockSpec((VECTORS, w), lambda i, b, m: (0, 0)),
            ],
            scratch_shapes=held_scratch(weight),
        ),
        out_shape=[
            jax.ShapeDtypeStruct((sz.rows, 3 * w), low),
            jax.ShapeDtypeStruct((sz.rows, w), low),
            jax.ShapeDtypeStruct((VECTORS, w), wide),
        ],
        compiler_params=params(2),
        cost_estimate=cost(6 * sz.rows * w * w, sz.rows * w * 10 + 6 * w * w),
        name="qkv",
    )(meta, x, *weight)


def attend_body(images, blocks, at, meta, q_ref, k_ref, v_ref, *rest):
    out_ref, lse_ref = rest[-2:]
    count, length = meta[at], meta[images + at]

    def variant(keys_in):
        near = keys_in - BLOCK
        start = 0
        while start < keys_in:
            size = min(SPAN, keys_in - start)
            rows = slice(start, start + size)
            start += size
            lane = lax.broadcasted_iota(jnp.int32, (size, PAIR), 1)
            first = lane < HEAD_DIM
            column = lax.broadcasted_iota(jnp.int32, (size, BLOCK), 1) + near
            q = q_ref[rows, :]
            outs, logs = [], []
            for head in range(2):
                own = first if head == 0 else jnp.logical_not(first)
                qh = jnp.where(own, q, jnp.zeros_like(q))
                last = dot_nt(qh, k_ref[near:keys_in, :])
                last = jnp.where(column < length, last, masked_score)
                top = jnp.max(last, axis=1, keepdims=True)
                if near:
                    body = dot_nt(qh, k_ref[:near, :])
                    top = jnp.maximum(top, jnp.max(body, axis=1, keepdims=True))
                drop = top * score_scale
                share = jnp.exp2(last * score_scale - drop)
                total = jnp.sum(share, axis=1, keepdims=True)
                acc = dot_nn(share.astype(low), v_ref[near:keys_in, :])
                if near:
                    share = jnp.exp2(body * score_scale - drop)
                    total = total + jnp.sum(share, axis=1, keepdims=True)
                    acc = acc + dot_nn(share.astype(low), v_ref[:near, :])
                outs.append(acc / total)
                logs.append(drop + jnp.log2(total))
            out_ref[rows, :] = jnp.where(first, outs[0], outs[1]).astype(low)
            both = jnp.where(lane == 0, logs[0], logs[1])
            lse_ref[0, :, rows] = both.T[:8, :]

    for keys in range(1, blocks + 1):
        pl.when(count == keys)(functools.partial(variant, keys * BLOCK))


def attend_call(sz, meta, qkv, at, before):
    pairs = sz.pairs

    def spec(part):
        return pl.BlockSpec((sz.length, PAIR), lambda p, m: (at, part * pairs + p))

    return pl.pallas_call(
        functools.partial(attend_body, sz.images, sz.blocks, at),
        grid_spec=pltpu.PrefetchScalarGridSpec(
            num_scalar_prefetch=1,
            grid=(pairs,),
            in_specs=[spec(0), spec(1), spec(2)] + [anywhere] * len(before),
            out_specs=[
                pl.BlockSpec((sz.length, PAIR), lambda p, m: (at, p)),
                pl.BlockSpec((1, 8, sz.length), lambda p, m: (at, p, 0)),
            ],
        ),
        out_shape=[
            jax.ShapeDtypeStruct((sz.rows, sz.width), low),
            jax.ShapeDtypeStruct((sz.images, 8 * pairs, sz.length), wide),
        ],
        input_output_aliases={4 + k: k for k in range(len(before))},
        compiler_params=params(1),
        cost_estimate=cost(
            4 * sz.length * sz.length * sz.width,
            8 * sz.length * sz.width,
            sz.length * sz.length * HEADS,
        ),
        name=f"attend_{at}",
    )(meta, qkv, qkv, qkv, *before)


AHEAD = 4


def mlp_body(meta, x, att, vec, weight, res, n2, slope, act, enc, fin):
    @pl.when(pl.program_id(1) < meta[pl.program_id(0)])
    def _():
        width = x.shape[1]
        fold = slope.shape[1] // width

        def part_of(k):
            return weight[:, (AHEAD + k) * width : (AHEAD + k + 1) * width]

        branch = dot_nn(att[...], part_of(0)) + row_of(vec, ATTN_BIAS)
        rows = x[...].astype(wide) + branch
        res[...] = rows
        normal, _ = normalise(rows)
        normed = (normal * row_of(vec, NORM2_GAIN) + row_of(vec, NORM2_BIAS)).astype(low)
        n2[...] = normed
        total = rows + row_of(vec, FC2_BIAS)
        for part in range(fold):
            cols = slice(part * width, (part + 1) * width)
            u = dot_nn(normed, part_of(1 + part)) + row_of(vec, FC1_BIAS + part)
            square = u * u
            bend = jnp.tanh(root_two_pi * u * (1.0 + 0.044715 * square))
            half = 0.5 * (1.0 + bend)
            hidden = (u * half).astype(low)
            slope[:, cols] = (
                half
                + (0.5 * root_two_pi) * u * (1.0 - bend * bend) * (1.0 + 0.134145 * square)
            ).astype(low)
            act[:, cols] = hidden
            total = total + dot_nn(hidden, part_of(1 + fold + part))
        enc[...] = total
        normal, _ = normalise(total)
        fin[...] = (normal * row_of(vec, FINAL_GAIN) + row_of(vec, FINAL_BIAS)).astype(low)


def mlp_call(sz, meta, x, att, vec, weight):
    w, f = sz.width, sz.hidden
    return pl.pallas_call(
        mlp_body,
        grid_spec=pltpu.PrefetchScalarGridSpec(
            num_scalar_prefetch=1,
            grid=(sz.images, sz.blocks),
            in_specs=[sz.row_spec(w), sz.row_spec(w), whole(vec.shape), whole(weight.shape)],
            out_specs=[sz.row_spec(c) for c in (w, w, f, f, w, w)],
        ),
        out_shape=[
            jax.ShapeDtypeStruct((sz.rows, w), wide),
            jax.ShapeDtypeStruct((sz.rows, w), low),
            jax.ShapeDtypeStruct((sz.rows, f), low),
            jax.ShapeDtypeStruct((sz.rows, f), low),
            jax.ShapeDtypeStruct((sz.rows, w), wide),
            jax.ShapeDtypeStruct((sz.rows, w), low),
        ],
        compiler_params=params(2),
        cost_estimate=cost(
            sz.rows * w * (2 * w + 4 * f), sz.rows * (14 * w + 4 * f) + 4 * w * f, sz.rows * f
        ),
        name="mlp",
    )(meta, x, att, vec, weight)


HEAD_ROWS = 16


SENT_ROWS = 48
SENT_MIX, SENT_ACT, SENT_GRAD, SENT_NORMED, SENT_POOLED = 16, 32, 36, 40, 41
SENT_BRANCH, SENT_PULL, SENT_COT, SENT_OUT, SENT_OUT_REST = 42, 43, 44, 45, 46
SENT_QUERY, SENT_QUERY_REST = 47, 31


def head_body(
    images, blocks, fold, meta, fin, cot_ref, vec, pool_w, mine, theirs, rest,
    shares, g_score, lift, probe_out, sent, sums, score, mixed, line, held, sems,
):
    width = fin.shape[1]
    fetch_all(meta, 2 * images, (mine, theirs, rest), held, sems)
    keys_w, values_w, query_w, out_w = (
        pool_w.at[:, k * width : (k + 1) * width] for k in range(AHEAD)
    )

    def part_of(k):
        return columns(held, k * width, width)

    head_row = lax.broadcasted_iota(jnp.int32, (HEAD_ROWS, width), 0)
    head_col = lax.broadcasted_iota(jnp.int32, (HEAD_ROWS, width), 1) // HEAD_DIM
    own = head_row == head_col
    row_id = lax.broadcasted_iota(jnp.int32, (HEAD_ROWS, 1), 0)
    probe = jnp.broadcast_to(row_of(vec, PROBE), (HEAD_ROWS, width)).astype(low)
    query = (dot_nn(probe, query_w[...]) + row_of(vec, POOL_QUERY_BIAS)).astype(low)
    probe_w = 0.125 * dot_nt(jnp.where(own, query, jnp.zeros_like(query)), keys_w[...])
    probe_out[...] = jnp.where(row_id == HEADS, query.astype(wide), probe_w)
    probe_top, probe_rest = halves(probe_w)
    pooled_heads = jnp.zeros((HEAD_ROWS, width), wide)

    def block_rows(i, b):
        start = (i * blocks + b) * BLOCK
        return fin[start : start + BLOCK, :]

    for i in range(images):
        count, length = meta[i], meta[images + i]
        for b in range(blocks):
            cols = slice(b * BLOCK, (b + 1) * BLOCK)
            score[:, cols] = jnp.full((HEAD_ROWS, BLOCK), masked_score, wide)

            @pl.when(b < count)
            def _(i=i, b=b, cols=cols, length=length):
                rows = block_rows(i, b)
                value = dot_nt(probe_top, rows) + dot_nt(probe_rest, rows)
                column = lax.broadcasted_iota(jnp.int32, (HEAD_ROWS, BLOCK), 1) + b * BLOCK
                score[:, cols] = jnp.where(column < length, value, masked_score)

        raised = jnp.exp(score[...] - jnp.max(score[...], axis=1, keepdims=True))
        shares[i] = raised / jnp.sum(raised, axis=1, keepdims=True)
        mixed[i] = jnp.zeros((HEAD_ROWS, width), wide)
        for b in range(blocks):
            cols = slice(b * BLOCK, (b + 1) * BLOCK)

            @pl.when(b < count)
            def _(i=i, b=b, cols=cols):
                rows = block_rows(i, b)
                top, rest = halves(shares[i, :, cols])
                mixed[i] += dot_nn(top, rows) + dot_nn(rest, rows)

        top, rest = halves(mixed[i])
        sent[i * SENT_ROWS : i * SENT_ROWS + HEAD_ROWS, :] = top
        heads = dot_nn(top, values_w[...]) + dot_nn(rest, values_w[...])
        row = column_sum(jnp.where(own, heads, 0.0)) + row_of(vec, POOL_VALUE_BIAS)
        pooled_heads = jnp.where(row_id == i, row, pooled_heads)
    real = row_id < jnp.where(meta[0] > 0, images, 0)
    cot = jnp.where(real, cot_ref[...], 0.0)
    pooled_low = pooled_heads.astype(low)
    branch = dot_nn(pooled_low, out_w[...]) + row_of(vec, POOL_OUT_BIAS)
    normal, scale = normalise(branch)
    gain = row_of(vec, HEAD_GAIN)
    normed = (normal * gain + row_of(vec, HEAD_BIAS)).astype(low)
    cot_low = cot.astype(low)
    total = branch + row_of(vec, HEAD_FC2_BIAS)
    back = jnp.zeros((HEAD_ROWS, width), wide)

    def keep(at, value):
        for i in range(images):
            line[i, at - 2 * HEAD_ROWS : at + 1 - 2 * HEAD_ROWS, :] = value[i : i + 1, :].astype(wide)

    for part in range(fold):
        u = dot_nn(normed, part_of(part)) + row_of(vec, FC1_BIAS + fold + part)
        square = u * u
        bend = jnp.tanh(root_two_pi * u * (1.0 + 0.044715 * square))
        half = 0.5 * (1.0 + bend)
        act = (u * half).astype(low)
        slope = half + (0.5 * root_two_pi) * u * (1.0 - bend * bend) * (1.0 + 0.134145 * square)
        second = part_of(fold + part)
        total = total + dot_nn(act, second)
        grad = jnp.where(real, dot_nt(cot_low, second) * slope, 0.0).astype(low)
        back = back + dot_nt(grad, part_of(part))
        keep(SENT_ACT + part, act)
        keep(SENT_GRAD + part, grad)
    sums[...] = jnp.zeros_like(sums)
    sums[0:1, :] = column_sum(jnp.where(real, back * normal, 0.0))
    sums[1:2, :] = column_sum(jnp.where(real, back, 0.0))
    branch_grad = jnp.where(real, cot + norm_back(back, gain, normal, scale), 0.0).astype(low)
    pull = dot_nt(branch_grad, out_w[...])
    keep(SENT_NORMED, normed)
    keep(SENT_POOLED, pooled_low)
    keep(SENT_BRANCH, branch_grad)
    keep(SENT_PULL, pull)
    keep(SENT_COT, cot_low)
    top, rest = halves(total)
    keep(SENT_OUT, top)
    keep(SENT_OUT_REST, rest)
    for i in range(images):
        top, rest = halves(jnp.where(own, pull[i : i + 1, :], 0.0))
        raised = dot_nt(top, values_w[...]) + dot_nt(rest, values_w[...])
        drop = jnp.sum(raised * mixed[i], axis=1, keepdims=True)
        lift[i] = raised
        lift_top, lift_rest = halves(raised)
        mixed[i] = jnp.zeros((HEAD_ROWS, width), wide)
        for b in range(blocks):
            cols = slice(b * BLOCK, (b + 1) * BLOCK)

            @pl.when(b < meta[i])
            def _(i=i, b=b, cols=cols):
                rows = block_rows(i, b)
                reach = dot_nt(lift_top, rows) + dot_nt(lift_rest, rows)
                grad = shares[i, :, cols] * (reach - drop)
                g_score[i, :, cols] = grad
                top, rest = halves(grad)
                mixed[i] += dot_nn(top, rows) + dot_nn(rest, rows)

        top, rest = halves(mixed[i])
        pulled = dot_nn(top, keys_w[...]) + dot_nn(rest, keys_w[...])
        query_grad = 0.125 * column_sum(jnp.where(own, pulled, 0.0))
        query_top, query_rest = halves(query_grad)
        line[i, HEAD_ROWS - 1 : HEAD_ROWS, :] = query_top.astype(wide)
        both = jnp.where(row_id == HEAD_ROWS - 1, query_rest.astype(wide), mixed[i])
        start = i * SENT_ROWS + HEAD_ROWS
        sent[start : start + HEAD_ROWS, :] = both.astype(low)
        sent[start + HEAD_ROWS : start + 2 * HEAD_ROWS, :] = line[i].astype(low)


def head_call(sz, meta, fin, cot, vec, block, weight):
    w, f, n = sz.width, sz.hidden, sz.images

    def out(shape, dtype):
        return jax.ShapeDtypeStruct(shape, dtype)

    shapes = [
        out((n, HEAD_ROWS, sz.length), wide),
        out((n, HEAD_ROWS, sz.length), wide),
        out((n, HEAD_ROWS, w), wide),
        out((HEAD_ROWS, w), wide),
        out((n * SENT_ROWS, w), low),
        out((8, w), wide),
    ]
    ins = (fin, cot, vec)
    return pl.pallas_call(
        functools.partial(head_body, sz.images, sz.blocks, f // w),
        grid_spec=pltpu.PrefetchScalarGridSpec(
            num_scalar_prefetch=1,
            grid=(1,),
            in_specs=[whole(v.shape) for v in ins]
            + [pl.BlockSpec((w, AHEAD * w), lambda *_: (0, 0), pipeline_mode=pl.Buffered(1))]
            + [anywhere] * 3,
            out_specs=[pl.BlockSpec(s.shape, lambda *_, r=len(s.shape): (0,) * r) for s in shapes],
            scratch_shapes=[
                pltpu.VMEM((HEAD_ROWS, sz.length), wide),
                pltpu.VMEM((n, HEAD_ROWS, w), wide),
                pltpu.VMEM((n, HEAD_ROWS, w), wide),
            ]
            + held_scratch(weight),
        ),
        out_shape=shapes,
        compiler_params=params(1),
        cost_estimate=cost(16 * 8 * w * f, sz.rows * w * 2 + 4 * w * f + 8 * w * w),
        name="head",
    )(meta, *ins, block, *weight)


def owner_body(own, fold, at, rows, probe, g_fc2, g_fc1, g_out, g_kv, sums, wide_rows, near, far):
    count, _, width = rows.shape
    group = HEAD_ROWS
    select = lax.broadcasted_iota(jnp.int32, (width, PAIR), 1)
    source = lax.broadcasted_iota(jnp.int32, (width, PAIR), 0)
    select = jnp.where((source == at[0] * own + select) & (select < own), 1.0, 0.0).astype(low)

    def rows_of(k):
        return rows[:, k * group : (k + 1) * group, :]

    def every(ref, r):
        return ref[pl.ds(r, count, stride=group), :].astype(low)

    def full(r):
        at_row = pl.ds(r - 2 * group, count, stride=group)
        return jnp.concatenate(
            [wide_rows[c, at_row, :] for c in range(width // PAIR)], axis=1
        ).astype(low)

    near[...] = dot_nn(rows_of(0).reshape(count * group, width), select)
    last = rows_of(2).reshape(count * group, width)
    far[...] = dot_nn(last, select)
    for c in range(width // PAIR):
        wide_rows[c] = last[:, c * PAIR : (c + 1) * PAIR].astype(wide)
    mixed = jnp.sum(rows_of(1).astype(wide), axis=0)
    sums[:group, :] = mixed
    sums[group:, :] = jnp.sum(rows_of(2).astype(wide), axis=0)
    cot = full(SENT_COT)
    normed = every(far, SENT_NORMED - 2 * group)
    for j in range(fold):
        g_fc2[j] = dot_tn(every(far, SENT_ACT + j - 2 * group), cot)[:own]
        g_fc1[:, j * width : (j + 1) * width] = dot_tn(normed, full(SENT_GRAD + j))[:own]
    g_out[...] = dot_tn(every(far, SENT_POOLED - 2 * group), full(SENT_BRANCH))[:own]
    pull = full(SENT_PULL)
    first = lax.broadcasted_iota(jnp.int32, (PAIR, PAIR), 1) < HEAD_DIM
    for p in range(width // PAIR):
        piece = pull[:, p * PAIR : (p + 1) * PAIR]
        both = [dot_tn(every(near, 2 * p + k), piece) for k in range(2)]
        at_cols = slice(width + p * PAIR, width + (p + 1) * PAIR)
        g_kv[:, at_cols] = jnp.where(first, both[0], both[1])[:own]
    head_row = lax.broadcasted_iota(jnp.int32, (group, width), 0)
    head_col = lax.broadcasted_iota(jnp.int32, (group, width), 1) // HEAD_DIM
    query = jnp.broadcast_to(probe[HEADS : HEADS + 1, :], (group, width))
    query = jnp.where(head_row == head_col, query, 0.0).astype(low)
    top, rest = halves(mixed)
    top, rest = halves(dot_nn(top, select) + dot_nn(rest, select))
    g_kv[:, :width] = 0.125 * (dot_tn(top, query) + dot_tn(rest, query))[:own]


def owner_call(at, rows, probe_w, own, fold):
    count, _, width = rows.shape
    shapes = [
        jax.ShapeDtypeStruct(shape, wide)
        for shape in (
            (fold, own, width), (own, fold * width), (own, width), (own, 2 * width),
            (2 * HEAD_ROWS, width),
        )
    ]
    return pl.pallas_call(
        functools.partial(owner_body, own, fold),
        grid_spec=pltpu.PrefetchScalarGridSpec(
            num_scalar_prefetch=1,
            grid=(1,),
            in_specs=[whole(rows.shape), whole(probe_w.shape)],
            out_specs=[pl.BlockSpec(s.shape, lambda *_, r=len(s.shape): (0,) * r) for s in shapes],
            scratch_shapes=[
                pltpu.VMEM((width // PAIR, count * HEAD_ROWS, PAIR), wide),
                pltpu.VMEM((count * HEAD_ROWS, PAIR), wide),
                pltpu.VMEM((count * HEAD_ROWS, PAIR), wide),
            ],
        ),
        out_shape=shapes,
        compiler_params=params(1),
        cost_estimate=cost(64 * count * width * PAIR, 8 * rows.size),
        name="owner",
    )(at, rows, probe_w)


def back_body(
    meta, fin, enc, res, att, slope, g_score, shares, lift, probe_w, spread, vec, weight,
    g_mlp, g_hidden, g_res, g_branch, g_att, delta, sums,
):
    @pl.when(is_first())
    def _():
        sums[...] = jnp.zeros_like(sums)

    @pl.when(pl.program_id(1) < meta[pl.program_id(0)])
    def _():
        width = fin.shape[1]
        fold = slope.shape[1] // width

        def part_of(k):
            return weight[:, (AHEAD + k) * width : (AHEAD + k + 1) * width]

        lift_top, lift_rest = halves(lift[0])
        probe_top, probe_rest = halves(probe_w[...])
        top, rest = halves(g_score[0])
        share_top, share_rest = halves(shares[0])
        left = jnp.concatenate([top, share_top, rest, share_rest, top, share_top], axis=0)
        right = jnp.concatenate(
            [probe_top, lift_top, probe_top, lift_top, probe_rest, lift_rest], axis=0
        )
        g_fin = dot_tn(left, right)
        normal, scale = normalise(enc[...])
        sums[0:1, :] += column_sum(g_fin * normal)
        sums[1:2, :] += column_sum(g_fin)
        g_enc = norm_back(g_fin, row_of(vec, FINAL_GAIN), normal, scale)
        low_enc = g_enc.astype(low)
        g_mlp[...] = low_enc
        sums[2:3, :] += column_sum(low_enc.astype(wide))
        back = jnp.zeros_like(g_enc)
        for part in range(fold):
            cols = slice(part * width, (part + 1) * width)
            grad = dot_nt(low_enc, part_of(1 + fold + part))
            grad = (grad * slope[:, cols].astype(wide)).astype(low)
            g_hidden[:, cols] = grad
            sums[8 + part : 9 + part, :] += column_sum(grad.astype(wide))
            back = back + dot_nt(grad, part_of(1 + part))
        normal, scale = normalise(res[...])
        sums[3:4, :] += column_sum(back * normal)
        sums[4:5, :] += column_sum(back)
        total = g_enc + norm_back(back, row_of(vec, NORM2_GAIN), normal, scale)
        g_res[...] = total
        low_res = total.astype(low)
        g_branch[...] = low_res
        sums[5:6, :] += column_sum(low_res.astype(wide))
        grad = dot_nt(low_res, part_of(0)).astype(low)
        g_att[...] = grad
        top, rest = halves(grad.astype(wide) * att[...].astype(wide))
        delta[0] = dot_nt(spread[...], top) + dot_nt(spread[...], rest)


def back_call(
    sz, meta, fin, enc, res, att, slope, g_score, shares, lift, probe_w, vec, weight
):
    w, f, n = sz.width, sz.hidden, sz.images
    lines = 8 * sz.pairs
    line = lax.broadcasted_iota(jnp.int32, (lines, w), 0)
    head = lax.broadcasted_iota(jnp.int32, (lines, w), 1) // HEAD_DIM
    spread = (head == 2 * (line // 8) + line % 8).astype(low)
    fixed = (probe_w, spread, vec, weight)

    def out(shape, dtype):
        return jax.ShapeDtypeStruct(shape, dtype)

    def kept(shape):
        return pl.BlockSpec(shape, lambda i, b, m: (0, 0))

    return pl.pallas_call(
        back_body,
        grid_spec=pltpu.PrefetchScalarGridSpec(
            num_scalar_prefetch=1,
            grid=(n, sz.blocks),
            in_specs=[
                sz.row_spec(w), sz.row_spec(w), sz.row_spec(w), sz.row_spec(w), sz.row_spec(f),
                sz.lane_spec(HEAD_ROWS), sz.lane_spec(HEAD_ROWS), sz.image_spec(HEAD_ROWS, w),
            ]
            + [whole(v.shape) for v in fixed],
            out_specs=[
                sz.row_spec(w), sz.row_spec(f), sz.row_spec(w), sz.row_spec(w), sz.row_spec(w),
                sz.lane_spec(lines), kept((16, w)),
            ],
        ),
        out_shape=[
            out((sz.rows, w), low), out((sz.rows, f), low), out((sz.rows, w), wide),
            out((sz.rows, w), low), out((sz.rows, w), low), out((n, lines, sz.length), wide),
            out((16, w), wide),
        ],
        compiler_params=params(2),
        cost_estimate=cost(
            sz.rows * w * (2 * w + 4 * f), sz.rows * (22 * w + 4 * f) + 4 * w * f
        ),
        name="mlp_back",
    )(meta, fin, enc, res, att, slope, g_score, shares, lift, *fixed)


def outer_body(images, blocks, units, meta, a_ref, b_ref, out_ref, acc):
    span = blocks * BLOCK

    def finish(term):
        if units == 0:
            out_ref[...] = term.astype(out_ref.dtype)
            return
        rows = term.shape[0] // units
        for u in range(units):
            out_ref[meta[2 * images + units + u]] = term[u * rows : (u + 1) * rows].astype(low)

    for i in range(images):
        for keys in range(blocks + 1):

            @pl.when(meta[i] == keys)
            def _(i=i, keys=keys):
                if keys:
                    rows = slice(i * span, i * span + keys * BLOCK)
                    term = dot_tn(a_ref[rows, :], b_ref[rows, :])
                else:
                    term = jnp.zeros(acc.shape, wide)
                if i > 0:
                    term = term + acc[...]
                if i < images - 1:
                    acc[...] = term
                else:
                    finish(term)


def outer_block_body(
    images, blocks, fold, meta, att_ref, g_att_ref, n2_ref, g_hidden_ref, act_ref, g_mlp_ref, out_ref, acc
):
    step = pl.program_id(0)
    for live, a_ref, b_ref in (
        (step == 0, att_ref, g_att_ref),
        ((step > 0) & (step <= fold), n2_ref, g_hidden_ref),
        (step > fold, act_ref, g_mlp_ref),
    ):
        pl.when(live)(
            functools.partial(outer_body, images, blocks, 0, meta, a_ref, b_ref, out_ref, acc)
        )


def outer_block_call(sz, meta, att, g_branch, n2, g_hidden, act, g_mlp):
    w, fold = sz.width, sz.hidden // sz.width
    one = whole((sz.rows, w))

    def part(first):
        return pl.BlockSpec((sz.rows, w), lambda j, c: (0, jnp.clip(j - first, 0, fold - 1)))

    return pl.pallas_call(
        functools.partial(outer_block_body, sz.images, sz.blocks, fold),
        grid_spec=pltpu.PrefetchScalarGridSpec(
            num_scalar_prefetch=1,
            grid=(1 + 2 * fold,),
            in_specs=[one, one, one, part(1), part(1 + fold), one],
            out_specs=pl.BlockSpec((w, w), lambda j, c: (0, j)),
            scratch_shapes=[pltpu.VMEM((w, w), wide)],
        ),
        out_shape=jax.ShapeDtypeStruct((w, (1 + 2 * fold) * w), low),
        compiler_params=params(1),
        cost_estimate=cost(2 * sz.rows * w * w * (1 + 2 * fold), 2 * sz.rows * w * (2 * fold + 4)),
        name="grad_block",
    )(meta, att, g_branch, n2, g_hidden, act, g_mlp)


def outer_qkv_body(images, blocks, units, meta, n1_ref, dq_ref, dk_ref, dv_ref, out_ref, acc):
    for k, b_ref in enumerate((dq_ref, dk_ref, dv_ref)):
        pl.when(pl.program_id(0) == k)(
            functools.partial(outer_body, images, blocks, units, meta, n1_ref, b_ref, out_ref, acc)
        )


def outer_qkv_call(sz, meta, n1, dq, dk, dv, units):
    w = sz.width
    return pl.pallas_call(
        functools.partial(outer_qkv_body, sz.images, sz.blocks, units),
        grid_spec=pltpu.PrefetchScalarGridSpec(
            num_scalar_prefetch=1,
            grid=(3,),
            in_specs=[whole((sz.rows, w))] * 4,
            out_specs=pl.BlockSpec((units, w // units, w), lambda j, c: (0, 0, j)),
            scratch_shapes=[pltpu.VMEM((w, w), wide)],
        ),
        out_shape=jax.ShapeDtypeStruct((units, w // units, 3 * w), low),
        compiler_params=params(1),
        cost_estimate=cost(6 * sz.rows * w * w, 8 * sz.rows * w),
        name="grad_qkv",
    )(meta, n1, dq, dk, dv)


def place_body(at, kept, taken, out):
    i = pl.program_id(0)

    @pl.when(at[2 * i] == 1)
    def _():
        out[...] = kept[0]

    @pl.when(at[2 * i] == 0)
    def _():
        out[...] = taken[...].astype(wide)


def place_call(at, kept, taken, groups, rows):
    width = kept.shape[-1]
    spec = pl.BlockSpec((1, rows, width), lambda i, at: (at[2 * i + 1], 0, 0))
    kept_spec = pl.BlockSpec(
        (1, 1, rows, width), lambda i, at: (at[2 * i + 1], at[2 * groups], 0, 0)
    )
    return pl.pallas_call(
        place_body,
        grid_spec=pltpu.PrefetchScalarGridSpec(
            num_scalar_prefetch=1,
            grid=(groups,),
            in_specs=[kept_spec, spec],
            out_specs=pl.BlockSpec((1, rows, width), lambda i, at: (i, 0, 0)),
        ),
        out_shape=jax.ShapeDtypeStruct((groups, rows, width), wide),
        compiler_params=params(1),
        cost_estimate=cost(0, groups * rows * width * 10),
        name="place",
    )(at, kept, taken)


def attend_back_body(
    images, blocks, meta, q_ref, k_ref, v_ref, g_ref, lse_ref, delta_ref, dq_ref, dk_ref, dv_ref,
    dk_acc, dv_acc,
):
    at = pl.program_id(0)
    count, length = meta[at], meta[images + at]
    lane = lax.broadcasted_iota(jnp.int32, (BLOCK, PAIR), 1)
    first = lane < HEAD_DIM

    def keep(value, head):
        own = first if head == 0 else jnp.logical_not(first)
        zero = jnp.zeros_like(value[:BLOCK])
        return jnp.concatenate(
            [
                jnp.where(own, value[r : r + BLOCK], zero)
                for r in range(0, value.shape[0], BLOCK)
            ],
            axis=0,
        )

    def variant(keys_in):
        near = keys_in - BLOCK
        keys = k_ref[:keys_in, :]
        kept_keys = [keep(keys, head) for head in range(2)]
        values = v_ref[:keys_in, :]
        kept_values = [keep(values, head) for head in range(2)]
        start = 0
        while start < keys_in:
            size = min(BACK_SPAN, keys_in - start)
            rows = slice(start, start + size)
            valid = lax.broadcasted_iota(jnp.int32, (BLOCK, size), 0) + near < length
            q, g = q_ref[rows, :], g_ref[rows, :]
            dq = dk = dv = None
            for head in range(2):
                log = lse_ref[0, head : head + 1, rows]
                drop = delta_ref[0, head : head + 1, rows]
                share = jnp.exp2(dot_nt(kept_keys[head], q) * score_scale - log)
                if near:
                    share = jnp.concatenate(
                        [share[:near], jnp.where(valid, share[near:], 0.0)], axis=0
                    )
                else:
                    share = jnp.where(valid, share, 0.0)
                reach = dot_nt(kept_values[head], g)
                grad = (share * (reach - drop)).astype(low)
                terms = (
                    dot_tn(grad, kept_keys[head]),
                    dot_nn(grad, keep(q, head)),
                    dot_nn(share.astype(low), keep(g, head)),
                )
                if head == 0:
                    dq, dk, dv = terms
                else:
                    dq, dk, dv = dq + terms[0], dk + terms[1], dv + terms[2]
            dq_ref[rows, :] = (dq * 0.125).astype(low)
            if start > 0:
                dk, dv = dk + dk_acc[:keys_in, :], dv + dv_acc[:keys_in, :]
            start += size
            if start < keys_in:
                dk_acc[:keys_in, :] = dk
                dv_acc[:keys_in, :] = dv
            else:
                dk_ref[:keys_in, :] = (dk * 0.125).astype(low)
                dv_ref[:keys_in, :] = dv.astype(low)

    for keys in range(1, blocks + 1):
        pl.when(count == keys)(functools.partial(variant, keys * BLOCK))


def attend_back_call(sz, meta, qkv, g_att, lse, delta):
    pairs = sz.pairs

    def spec(part):
        return pl.BlockSpec((sz.length, PAIR), lambda i, p, m: (i, part * pairs + p))

    line = pl.BlockSpec((1, 8, sz.length), lambda i, p, m: (i, p, 0))
    out = jax.ShapeDtypeStruct((sz.rows, sz.width), low)
    return pl.pallas_call(
        functools.partial(attend_back_body, sz.images, sz.blocks),
        grid_spec=pltpu.PrefetchScalarGridSpec(
            num_scalar_prefetch=1,
            grid=(sz.images, pairs),
            in_specs=[spec(0), spec(1), spec(2), spec(0), line, line],
            out_specs=[spec(0), spec(0), spec(0)],
            scratch_shapes=[pltpu.VMEM((sz.length, PAIR), wide)] * 2,
        ),
        out_shape=[out, out, out],
        compiler_params=params(2),
        cost_estimate=cost(
            10 * sz.rows * sz.length * sz.width,
            14 * sz.rows * sz.width,
            sz.rows * sz.length * HEADS,
        ),
        name="attend_back",
    )(meta, qkv, qkv, qkv, g_att, lse, delta)


def qkv_back_body(
    base, meta, x, g_res, dq, dk, dv, vec, mine, theirs, grad_ref, low_ref, sums, held, sems
):
    @pl.when(is_first())
    def _():
        fetch_all(meta, base, (mine, theirs), held, sems)
        sums[...] = jnp.zeros_like(sums)

    live = pl.program_id(1) < meta[pl.program_id(0)]

    @pl.when(live)
    def _():
        width = x.shape[1]
        normal, scale = normalise(x[...].astype(wide))
        back = None
        for part, ref in enumerate((dq, dk, dv)):
            term = dot_nt(ref[...], columns(held, part * width, width))
            back = term if back is None else back + term
        sums[0:1, :] += column_sum(back * normal)
        sums[1:2, :] += column_sum(back)
        sums[2:3, :] += column_sum(dq[...].astype(wide))
        sums[3:4, :] += column_sum(dv[...].astype(wide))
        grad = g_res[...] + norm_back(back, row_of(vec, NORM1_GAIN), normal, scale)
        grad_ref[...] = grad
        low_ref[...] = grad.astype(low)

    @pl.when(jnp.logical_not(live))
    def _():
        grad_ref[...] = jnp.zeros_like(grad_ref)
        low_ref[...] = jnp.zeros_like(low_ref)


def qkv_back_call(sz, meta, x, g_res, dq, dk, dv, vec, weight):
    w, blocks = sz.width, sz.blocks
    plain = pl.BlockSpec((BLOCK, w), lambda i, b, m: (i * blocks + b, 0))
    return pl.pallas_call(
        functools.partial(qkv_back_body, 2 * sz.images),
        grid_spec=pltpu.PrefetchScalarGridSpec(
            num_scalar_prefetch=1,
            grid=(sz.images, blocks),
            in_specs=[sz.row_spec(w)] * 5 + [whole(vec.shape), anywhere, anywhere],
            out_specs=[plain, plain, pl.BlockSpec((8, w), lambda i, b, m: (0, 0))],
            scratch_shapes=held_scratch(weight),
        ),
        out_shape=[
            jax.ShapeDtypeStruct((sz.rows, w), wide),
            jax.ShapeDtypeStruct((sz.rows, w), low),
            jax.ShapeDtypeStruct((8, w), wide),
        ],
        compiler_params=params(2),
        cost_estimate=cost(6 * sz.rows * w * w, sz.rows * w * 18 + 6 * w * w),
        name="qkv_back",
    )(meta, x, g_res, dq, dk, dv, vec, *weight)


axes = ("img", "seq")


def bits_of(count):
    return [1 << k for k in range(count.bit_length() - 1)]


def tied(value, *after):
    return lax.optimization_barrier((value, *after))[0]


def together(*values):
    return lax.optimization_barrier(values)


def cut(size, shares):
    edges = [round(size * sum(shares[:k]) / sum(shares) / 16) * 16 for k in range(len(shares) + 1)]
    return [slice(p, q) for p, q in zip(edges[:-1], edges[1:], strict=True)]


class Wires:
    def __init__(self, img_count, seq_count):
        self.count, self.seq_count = img_count * seq_count, seq_count
        self.core = seq_count
        self.units = img_count
        self.seq_bits = bits_of(seq_count)
        inner = [bit for bit in bits_of(self.count) if bit > self.core]
        inner = inner[:1] + inner[:0:-1]
        self.orders = (inner, inner[1:] + inner[:1])

    def swap(self, value, bit):
        return lax.ppermute(value, axes, [(i, i ^ bit) for i in range(self.count)])

    def step(self, value, at):
        pairs = [(i, i ^ self.orders[1 if i & self.core else 0][at]) for i in range(self.count)]
        return lax.ppermute(value, axes, pairs)

    def tables(self, me):
        img = me // self.seq_count
        core = img % 2

        def at(place, side):
            by_core = []
            for order in self.orders:
                unit = 0
                for k, bit in enumerate(order):
                    unit |= ((place >> k) & 1) * (bit // self.seq_count)
                by_core.append(unit)
            which = core if side == 0 else 1 - core
            return (img ^ side) ^ jnp.where(which == 0, by_core[0], by_core[1])

        def place(unit):
            side = (unit ^ img) & 1
            delta = unit ^ img
            by_core = []
            for order in self.orders:
                total = jnp.zeros((), jnp.int32)
                for k, bit in enumerate(order):
                    shift = (bit // self.seq_count).bit_length() - 1
                    total = total | (((delta >> shift) & 1) << k)
                by_core.append(total)
            which = core ^ side
            return side * (self.units // 2) + jnp.where(which == 0, by_core[0], by_core[1])

        half = self.units // 2
        order = [at(k, side) for side in range(2) for k in range(half)]
        inverse = [place(unit) for unit in range(self.units)]
        return jnp.stack(order + inverse)

    def join_seq(self, value, me):
        for bit in self.seq_bits:
            other = self.swap(value, bit)
            value = jnp.where(
                (me & bit) > 0,
                jnp.concatenate([other, value], axis=0),
                jnp.concatenate([value, other], axis=0),
            )
        return value

    def joined(self, value, at):
        return jnp.concatenate([value, self.step(value, at)], axis=0)

    def halved(self, value, at):
        half = value.shape[0] // 2
        return value[:half] + self.step(value[half:], at)

    def small_scatter(self, value, me, bits):
        for bit in reversed(bits):
            value = self.small_half(value, me, bit)
        return value[0]

    def small_half(self, value, me, bit):
        pair = value.reshape((2, value.shape[0] // 2) + value.shape[1:])
        up = (me & bit) > 0
        return jnp.where(up, pair[1], pair[0]) + self.swap(jnp.where(up, pair[0], pair[1]), bit)


def local(img_count, seq_count, *args):
    (
        patches, lengths, pooled_cot, norm1_gain, norm1_bias, qkv_weight, query_bias, value_bias,
        attn_weight, attn_bias, norm2_gain, norm2_bias, fc1_weight, fc1_bias, fc2_weight, fc2_bias,
        final_gain, final_bias, probe_vector, pool_query_weight, pool_query_bias, pool_kv_weight,
        pool_value_bias, pool_out_weight, pool_out_bias, head_gain, head_bias, head_fc1_weight,
        head_fc1_bias, head_fc2_weight, head_fc2_bias,
    ) = args
    count = img_count * seq_count
    groups, part_rows, width = patches.shape
    length = part_rows * seq_count
    hidden = fc1_weight.shape[1]
    images = max(1, groups // seq_count)
    share = max(1, seq_count // groups)
    own = width // count
    per = hidden // count
    fold = hidden // width
    sz = Sizes(images, length, width, hidden)
    wires = Wires(img_count, seq_count)
    me = lax.axis_index(axes)
    seq_at = lax.axis_index("seq")
    first_image = (seq_at // share) * images

    slots = list(range(groups))
    if share == 1:
        turn = [r % seq_count if (r // seq_count) % 2 == 0 else -1 - r % seq_count for r in slots]
        slots = [(t % seq_count) * images + r // seq_count for r, t in zip(slots, turn, strict=True)]
        ahead = (lengths[None, :] > lengths[:, None]) | (
            (lengths[None, :] == lengths[:, None])
            & (jnp.arange(groups)[None, :] < jnp.arange(groups)[:, None])
        )
        rank = jnp.sum(ahead, axis=1)
        slot_of = sum(jnp.where(rank == r, slot, 0) for r, slot in enumerate(slots))
    else:
        slot_of = jnp.arange(groups)
    order = jnp.sum(
        jnp.where(slot_of[None, :] == jnp.arange(groups)[:, None], jnp.arange(groups)[None, :], 0),
        axis=1,
    )

    def of_slots(value, first):
        at = lax.dynamic_slice_in_dim(order, first, images)
        return jnp.concatenate(
            [lax.dynamic_slice_in_dim(value, at[k], 1) for k in range(images)], axis=0
        )

    own_lengths = of_slots(lengths, first_image)
    own_lengths = jnp.where(seq_at % share == 0, own_lengths, 0)
    own_cot = of_slots(pooled_cot, first_image)
    meta = jnp.concatenate(
        [(own_lengths + BLOCK - 1) // BLOCK, own_lengths, wires.tables(me)]
    ).astype(jnp.int32)

    def by_unit(bias):
        return bias.reshape(own, fold).T

    vectors = [
        v.reshape(1, own)
        for v in (
            norm1_gain, norm1_bias, query_bias, value_bias, attn_bias, norm2_gain, norm2_bias,
            fc2_bias, final_gain, final_bias, pool_query_bias, pool_value_bias, pool_out_bias,
            head_gain, head_bias, head_fc2_bias, probe_vector,
        )
    ]
    vectors += [by_unit(fc1_bias), by_unit(head_fc1_bias)]
    unit_a, block, pack = packs_call(
        vectors, qkv_weight, pool_kv_weight, pool_query_weight, attn_weight, fc1_weight, fc2_weight,
        pool_out_weight, head_fc1_weight, head_fc2_weight,
    )
    block = lax.all_gather(block, axes, axis=0, tiled=True)

    pairwise = seq_count == 2 and share == 1
    steps = len(wires.orders[0])
    if pairwise:
        kept = of_slots(patches, first_image)
        given = of_slots(patches, (1 - seq_at) * images)
        parts = cut(part_rows, list(range(2, steps + 2)))
    else:
        ordered = jnp.concatenate(
            [lax.dynamic_slice_in_dim(patches, order[k], 1) for k in range(groups)], axis=0
        )
        given = jnp.repeat(ordered, share, axis=0)
    mine = wires.join_seq(unit_a, me)[None]
    mine, given = together(mine, given)
    taken = []
    for at in range(steps):
        mine = wires.joined(mine, at)
        if pairwise:
            mine, one = together(mine, wires.swap(given[:, parts[at]], 1))
            taken.append(one)
        if at == 1:
            mine, meta = together(mine, meta)
    mine, pack = together(mine, pack)
    theirs = wires.swap(mine, wires.core)
    theirs, pack = together(theirs, pack)
    qkv_full = (mine, theirs)
    if pairwise:
        taken = jnp.concatenate(taken, axis=1)
        x = jnp.where(
            seq_at == 0,
            jnp.concatenate([kept, taken], axis=1),
            jnp.concatenate([taken, kept], axis=1),
        )
    else:
        x = lax.all_to_all(given, "seq", split_axis=0, concat_axis=1, tiled=True)
    x = x.reshape(sz.rows, width)

    qkv, n1, vec = qkv_call(sz, meta, x, qkv_full)
    pack = wires.join_seq(pack, me)[None]
    qkv, pack = together(qkv, pack)
    done, forward = 0, ()
    for at in range(images):
        forward = attend_call(sz, meta, qkv, at, forward)
        stop = steps - 1 if at == images - 1 else min(done + 1, steps - 1)
        while done < stop:
            pack = wires.joined(pack, done)
            done += 1
        *forward, pack = together(*forward, pack)
    att, lse = forward
    res, n2, slope, act, enc, fin = mlp_call(sz, meta, x, att, vec, block)
    other = wires.swap(pack, wires.core)
    pack_rest = wires.step(pack, steps - 1)
    fin, other, pack_rest = together(fin, other, pack_rest)
    other_rest = wires.swap(pack_rest, wires.core)
    head_full = (jnp.concatenate([pack, pack_rest], axis=0), other, other_rest)
    cot_rows = jnp.pad(own_cot, ((0, HEAD_ROWS - images), (0, 0)))
    shares, g_score, lift, probe_w, sent, head_sums = head_call(
        sz, meta, fin, cot_rows, vec, block, head_full
    )
    rows = lax.all_gather(sent, axes, axis=0, tiled=True)

    g_mlp, g_hidden, g_res, g_branch, g_att, delta, back_sums = back_call(
        sz, meta, fin, enc, res, att, slope, g_score, shares, lift, probe_w, vec, block
    )
    terms = outer_block_call(sz, meta, att, g_branch, n2, g_hidden, act, g_mlp)
    terms, g_att, rows = together(terms, g_att, rows)
    totals = lax.psum_scatter(terms, axes, scatter_dimension=0, tiled=True)

    def by_column(grad):
        return grad.reshape(own, fold, width).transpose(0, 2, 1).reshape(own, hidden)

    def own_part(v, axis=-1):
        return lax.dynamic_slice_in_dim(v, me * own, own, axis=axis)

    half = wires.units // 2
    dq, dk, dv = attend_back_call(sz, meta, qkv, g_att, lse, delta)
    last = outer_qkv_call(sz, meta, n1, dq, dk, dv, wires.units)
    g_res, last = together(g_res, last)
    last = last[:half] + wires.swap(last[half:], wires.core)
    patch_grad, patch_low, qkv_sums = qkv_back_call(sz, meta, x, g_res, dq, dk, dv, vec, qkv_full)
    patch_low = patch_low.reshape(images, length, width)
    sums = jnp.concatenate(
        [back_sums[:6], head_sums[:2], qkv_sums[:4], back_sums[8 : 8 + fold]], axis=0
    )
    sums = sums.reshape(-1, count, own).transpose(1, 0, 2)
    if pairwise:
        given = lax.dynamic_slice_in_dim(patch_low, (1 - seq_at) * part_rows, part_rows, axis=1)
    else:
        given = lax.all_to_all(patch_low, "seq", split_axis=1, concat_axis=0, tiled=True)[::share]

    def head_part(rows):
        rows = rows.reshape(count * images, SENT_ROWS, width)
        return owner_call(me[None].astype(jnp.int32), rows, probe_w, own, fold)

    def sums_part(rows, row_sums):
        rows = lax.dynamic_slice_in_dim(
            rows.reshape(img_count, seq_count, images, SENT_ROWS, width), me // seq_count, 1
        )[0, ::share]
        query_grad = row_sums[SENT_QUERY - HEAD_ROWS] + row_sums[SENT_QUERY_REST - HEAD_ROWS]
        pooled = rows[:, :, SENT_OUT].astype(wide) + rows[:, :, SENT_OUT_REST].astype(wide)
        pooled = pooled.reshape(groups, width)
        pooled = jnp.concatenate(
            [lax.dynamic_slice_in_dim(pooled, slot_of[k], 1) for k in range(groups)], axis=0
        )
        return (
            pooled,
            probe_vector.astype(wide)[:, None] * query_grad[None, :],
            jnp.sum(pool_query_weight.astype(wide) * query_grad[None, :], axis=1),
            own_part(query_grad),
            own_part(row_sums),
        )

    last, sums, given, rows = together(last, sums, given, rows)
    parts, taken, made = cut(part_rows, (1,) * steps), [], []
    bits = list(reversed(bits_of(count)))
    for tick, at in enumerate(reversed(range(steps))):
        last = wires.halved(last, at)
        sums = wires.small_half(sums, me, bits.pop(0))
        taken.append(wires.swap(given[:, parts[tick]], 1) if pairwise else given)
        if tick == 0:
            made.append(head_part(rows))
        elif tick == 1:
            made.append(sums_part(rows, made[0][4]))
        last, sums, rows, taken, made = together(last, sums, rows, taken, made)
    (grad_head_fc2, grad_head_fc1, grad_pool_out, grad_pool_kv, _), made = made
    grad_head_fc2 = grad_head_fc2.transpose(1, 0, 2).reshape(per, width)
    grad_head_fc1 = by_column(grad_head_fc1)
    pooled, grad_pool_query_weight, grad_probe, g_pool_query_bias, own_sums = made

    def own_sum(at):
        return own_sums[at - HEAD_ROWS]

    g_head_fc1_bias = own_sums[SENT_GRAD - HEAD_ROWS :][:fold].T.reshape(per)
    last = last.reshape(seq_count, own, 3 * width)
    for bit in reversed(wires.seq_bits):
        last = wires.small_half(last, me, bit)
    while bits:
        sums = wires.small_half(sums, me, bits.pop(0))
    if pairwise:
        at_slot = jnp.stack(
            [(slot_of // images == seq_at).astype(jnp.int32), slot_of % images], axis=1
        )
        at_slot = jnp.concatenate([at_slot.reshape(-1), seq_at[None]]).astype(jnp.int32)
        patch_grad = place_call(
            at_slot,
            patch_grad.reshape(images, seq_count, part_rows, width),
            jnp.concatenate(taken, axis=1),
            groups,
            part_rows,
        )
    else:
        patch_grad = jnp.concatenate(
            [lax.dynamic_slice_in_dim(taken[0], slot_of[k], 1) for k in range(groups)], axis=0
        ).astype(wide)
    totals = totals.astype(wide)
    grad_attn = totals[:, :width]
    grad_fc1 = by_column(totals[:, width : width + hidden])
    grad_fc2 = totals[:, width + hidden :].reshape(per, width)
    grad_qkv = last[0].astype(wide)
    sums = sums[0]
    (
        g_final_gain, g_final_bias, g_fc2_bias, g_norm2_gain, g_norm2_bias, g_attn_bias,
        g_head_gain, g_head_bias, g_norm1_gain, g_norm1_bias, g_query_bias, g_value_bias,
    ) = sums[:12]
    g_fc1_bias = sums[12:].T.reshape(per)
    return (
        pooled, patch_grad, g_norm1_gain, g_norm1_bias, grad_qkv, g_query_bias, g_value_bias,
        grad_attn, g_attn_bias, g_norm2_gain, g_norm2_bias, grad_fc1, g_fc1_bias, grad_fc2,
        g_fc2_bias, g_final_gain, g_final_bias, grad_probe, grad_pool_query_weight,
        g_pool_query_bias, grad_pool_kv, own_sum(SENT_PULL), grad_pool_out,
        own_sum(SENT_BRANCH), g_head_gain, g_head_bias, grad_head_fc1,
        g_head_fc1_bias, grad_head_fc2, own_sum(SENT_COT),
    )


def solution(mesh):
    rows, vector = P(axes, None), P(axes)
    body = functools.partial(local, mesh.shape["img"], mesh.shape["seq"])
    vector_weights = (3, 4, 6, 7, 9, 10, 11, 13, 15, 16, 17, 18, 20, 22, 24, 25, 26, 28, 30)
    in_specs = (P("img", "seq", None), P("img"), P("img", None)) + tuple(
        vector if at in vector_weights else rows for at in range(3, 31)
    )
    out_specs = (P("img", None), P("img", "seq", None)) + in_specs[3:]
    return jax.shard_map(body, mesh=mesh, in_specs=in_specs, out_specs=out_specs, check_vma=False)
```

```python
import functools

import jax
import jax.numpy as jnp
from jax import lax
from jax.experimental import pallas as pl
from jax.experimental.pallas import tpu as pltpu
from jax.sharding import PartitionSpec as P

HEADS = 12
HEAD_DIM = 64
BLOCK = 256
PAIR = 128
SPAN = 512
BACK_SPAN = 256
wide = jnp.float32
low = jnp.bfloat16
masked_score = -1e30
base_two = 1.4426950408889634
score_scale = 0.125 * base_two
norm_epsilon = 1e-06
root_two_pi = 0.7978845608028654
vmem_bytes = 60 * 1024 * 1024


def dot_nn(a, b):
    return jnp.dot(a, b, preferred_element_type=wide)


def dot_nt(a, b):
    return lax.dot_general(a, b, (((1,), (1,)), ((), ())), preferred_element_type=wide)


def dot_tn(a, b):
    return lax.dot_general(a, b, (((0,), (0,)), ((), ())), preferred_element_type=wide)


def halves(v):
    top = v.astype(low)
    return top, (v - top.astype(wide)).astype(low)


def normalise(v):
    centred = v - jnp.mean(v, axis=-1, keepdims=True)
    spread = jnp.mean(centred * centred, axis=-1, keepdims=True)
    scale = lax.rsqrt(spread + norm_epsilon)
    return centred * scale, scale


def norm_back(grad, gain, normal, scale):
    gn = grad * gain
    return (
        gn
        - jnp.mean(gn, axis=-1, keepdims=True)
        - normal * jnp.mean(gn * normal, axis=-1, keepdims=True)
    ) * scale


def column_sum(v):
    return jnp.sum(v, axis=0, keepdims=True)


def params(rank):
    return pltpu.CompilerParams(
        dimension_semantics=("arbitrary",) * rank, vmem_limit_bytes=vmem_bytes
    )


def whole(shape):
    return pl.BlockSpec(
        shape, lambda *_: (0,) * len(shape), pipeline_mode=pl.Buffered(1)
    )


def cost(flops, nbytes, exps=0):
    return pl.CostEstimate(flops=int(flops), bytes_accessed=int(nbytes), transcendentals=int(exps))


class Sizes:
    def __init__(self, images, length, width, hidden):
        self.images, self.length, self.width, self.hidden = images, length, width, hidden
        self.rows = images * length
        self.blocks = length // BLOCK
        self.pairs = width // PAIR

        self.units = 0

    def row_spec(self, cols):
        blocks = self.blocks

        def index(i, b, meta):
            return i * blocks + jnp.clip(b, 0, jnp.maximum(meta[i] - 1, 0)), 0

        return pl.BlockSpec((BLOCK, cols), index)

    def lane_spec(self, rows):
        def index(i, b, meta):
            return i, 0, jnp.clip(b, 0, jnp.maximum(meta[i] - 1, 0))

        return pl.BlockSpec((1, rows, BLOCK), index)

    def image_spec(self, rows, cols):
        return pl.BlockSpec((1, rows, cols), lambda i, b, meta: (i, 0, 0))


(
    NORM1_GAIN,
    NORM1_BIAS,
    QUERY_BIAS,
    VALUE_BIAS,
    ATTN_BIAS,
    NORM2_GAIN,
    NORM2_BIAS,
    FC2_BIAS,
    FINAL_GAIN,
    FINAL_BIAS,
    POOL_QUERY_BIAS,
    POOL_VALUE_BIAS,
    POOL_OUT_BIAS,
    HEAD_GAIN,
    HEAD_BIAS,
    HEAD_FC2_BIAS,
) = range(16)


PROBE = 16
FC1_BIAS = 17
VECTORS = 32


def row_of(ref, at):
    return ref[at : at + 1, :]


anywhere = pl.BlockSpec(memory_space=pl.ANY)


def fetch_all(meta, base, parts, held, sems):
    copies, place = [], 0
    for part in parts:
        for k in range(part.shape[0]):
            copies.append(
                pltpu.make_async_copy(part.at[k], held.at[meta[base + place]], sems.at[place])
            )
            place += 1
    for copy in copies:
        copy.start()
    for copy in copies:
        copy.wait()


def held_scratch(parts):
    units = sum(part.shape[0] for part in parts)
    return [
        pltpu.VMEM((units,) + parts[0].shape[1:], parts[0].dtype),
        pltpu.SemaphoreType.DMA((units,)),
    ]


def columns(held, start, size):
    units, rows, _ = held.shape
    return held[:, :, start : start + size].reshape(units * rows, size)


def is_first():
    return (pl.program_id(0) == 0) & (pl.program_id(1) == 0)


def packs_body(count, *refs):
    rows = refs[:count]
    qkv, pool_kv, pool_query, attn, fc1, fc2, pool_out, head_fc1, head_fc2 = refs[count:-4]
    first, block, head, lines = refs[-4:]
    own, width = attn.shape
    fold = fc1.shape[1] // width
    chunk = fold * PAIR
    at_from = lax.broadcasted_iota(jnp.int32, (chunk, chunk), 0)
    at_to = lax.broadcasted_iota(jnp.int32, (chunk, chunk), 1)
    spread = jnp.where(at_from == (at_to % PAIR) * fold + at_to // PAIR, 1.0, 0.0).astype(low)
    row_from = lax.broadcasted_iota(jnp.int32, (own, own * fold), 1)
    row_to = lax.broadcasted_iota(jnp.int32, (own, own * fold), 0)

    def by_part(ref, out, start):
        for k in range(width // PAIR):
            value = dot_nn(ref[:, k * chunk : (k + 1) * chunk], spread).astype(low)
            for j in range(fold):
                to = start + j * width + k * PAIR
                out[:, to : to + PAIR] = value[:, j * PAIR : (j + 1) * PAIR]

    def by_row(ref, out, start, parts):
        for j in parts:
            pick = jnp.where(row_from == row_to * fold + j, 1.0, 0.0).astype(low)
            to = start + (j - parts[0]) * width
            out[:, to : to + width] = dot_nn(pick, ref[...]).astype(low)

    lines[...] = jnp.zeros_like(lines)
    at = 0
    for ref in rows:
        lines[at : at + ref.shape[0], :own] = ref[...].astype(wide)
        at += ref.shape[0]
    first[:, : 3 * width] = qkv[...]
    first[:, 3 * width :] = lines[...].T[:own].astype(low)
    block[:, : 2 * width] = pool_kv[...]
    block[:, 2 * width : 3 * width] = pool_query[...]
    block[:, 3 * width : 4 * width] = pool_out[...]
    early = fold - (AHEAD - 4)
    by_row(head_fc2, block, 4 * width, range(early, fold))
    block[:, AHEAD * width : (AHEAD + 1) * width] = attn[...]
    by_part(fc1, block, (AHEAD + 1) * width)
    by_row(fc2, block, (AHEAD + 1 + fold) * width, range(fold))
    by_part(head_fc1, head, 0)
    by_row(head_fc2, head, fold * width, range(early))


def packs_call(rows, *weights):
    own, width = weights[3].shape
    fold = weights[4].shape[1] // width
    ins = (*rows, *weights)
    vmem = pl.BlockSpec(memory_space=pltpu.VMEM)
    return pl.pallas_call(
        functools.partial(packs_body, len(rows)),
        in_specs=[vmem] * len(ins),
        out_specs=[vmem] * 3,
        out_shape=[
            jax.ShapeDtypeStruct((own, cols), low)
            for cols in (
                3 * width + PAIR, (AHEAD + 1 + 2 * fold) * width, (2 * fold + 4 - AHEAD) * width
            )
        ],
        scratch_shapes=[pltpu.VMEM((PAIR, PAIR), wide)],
        compiler_params=params(0),
        cost_estimate=cost(0, 4 * own * width * (9 + 4 * fold)),
        name="packs",
    )(*ins)


def qkv_body(base, meta, x, mine, theirs, qkv, normed, vec, held, sems):
    width = x.shape[1]

    @pl.when(is_first())
    def _():
        fetch_all(meta, base, (mine, theirs), held, sems)
        vec[...] = columns(held, 3 * width, PAIR).astype(wide).T[:VECTORS]

    @pl.when(pl.program_id(1) < meta[pl.program_id(0)])
    def _():
        normal, _ = normalise(x[...].astype(wide))
        rows = (normal * row_of(vec, NORM1_GAIN) + row_of(vec, NORM1_BIAS)).astype(low)
        normed[...] = rows
        for part, bias in enumerate((QUERY_BIAS, None, VALUE_BIAS)):
            out = dot_nn(rows, columns(held, part * width, width))
            if bias is not None:
                out = out + row_of(vec, bias)
            qkv[:, part * width : (part + 1) * width] = out.astype(low)


def qkv_call(sz, meta, x, weight):
    w = sz.width
    return pl.pallas_call(
        functools.partial(qkv_body, 2 * sz.images),
        grid_spec=pltpu.PrefetchScalarGridSpec(
            num_scalar_prefetch=1,
            grid=(sz.images, sz.blocks),
            in_specs=[sz.row_spec(w), anywhere, anywhere],
            out_specs=[
                sz.row_spec(3 * w),
                sz.row_spec(w),
                pl.BlockSpec((VECTORS, w), lambda i, b, m: (0, 0)),
            ],
            scratch_shapes=held_scratch(weight),
        ),
        out_shape=[
            jax.ShapeDtypeStruct((sz.rows, 3 * w), low),
            jax.ShapeDtypeStruct((sz.rows, w), low),
            jax.ShapeDtypeStruct((VECTORS, w), wide),
        ],
        compiler_params=params(2),
        cost_estimate=cost(6 * sz.rows * w * w, sz.rows * w * 10 + 6 * w * w),
        name="qkv",
    )(meta, x, *weight)


def attend_body(images, blocks, at, meta, q_ref, k_ref, v_ref, *rest):
    out_ref, lse_ref = rest[-2:]
    count, length = meta[at], meta[images + at]

    def variant(keys_in):
        near = keys_in - BLOCK
        start = 0
        while start < keys_in:
            size = min(SPAN, keys_in - start)
            rows = slice(start, start + size)
            start += size
            lane = lax.broadcasted_iota(jnp.int32, (size, PAIR), 1)
            first = lane < HEAD_DIM
            column = lax.broadcasted_iota(jnp.int32, (size, BLOCK), 1) + near
            q = q_ref[rows, :]
            outs, logs = [], []
            for head in range(2):
                own = first if head == 0 else jnp.logical_not(first)
                qh = jnp.where(own, q, jnp.zeros_like(q))
                last = dot_nt(qh, k_ref[near:keys_in, :])
                last = jnp.where(column < length, last, masked_score)
                top = jnp.max(last, axis=1, keepdims=True)
                if near:
                    body = dot_nt(qh, k_ref[:near, :])
                    top = jnp.maximum(top, jnp.max(body, axis=1, keepdims=True))
                drop = top * score_scale
                share = jnp.exp2(last * score_scale - drop)
                total = jnp.sum(share, axis=1, keepdims=True)
                acc = dot_nn(share.astype(low), v_ref[near:keys_in, :])
                if near:
                    share = jnp.exp2(body * score_scale - drop)
                    total = total + jnp.sum(share, axis=1, keepdims=True)
                    acc = acc + dot_nn(share.astype(low), v_ref[:near, :])
                outs.append(acc / total)
                logs.append(drop + jnp.log2(total))
            out_ref[rows, :] = jnp.where(first, outs[0], outs[1]).astype(low)
            both = jnp.where(lane == 0, logs[0], logs[1])
            lse_ref[0, :, rows] = both.T[:8, :]

    for keys in range(1, blocks + 1):
        pl.when(count == keys)(functools.partial(variant, keys * BLOCK))


def attend_call(sz, meta, qkv, at, before):
    pairs = sz.pairs

    def spec(part):
        return pl.BlockSpec((sz.length, PAIR), lambda p, m: (at, part * pairs + p))

    return pl.pallas_call(
        functools.partial(attend_body, sz.images, sz.blocks, at),
        grid_spec=pltpu.PrefetchScalarGridSpec(
            num_scalar_prefetch=1,
            grid=(pairs,),
            in_specs=[spec(0), spec(1), spec(2)] + [anywhere] * len(before),
            out_specs=[
                pl.BlockSpec((sz.length, PAIR), lambda p, m: (at, p)),
                pl.BlockSpec((1, 8, sz.length), lambda p, m: (at, p, 0)),
            ],
        ),
        out_shape=[
            jax.ShapeDtypeStruct((sz.rows, sz.width), low),
            jax.ShapeDtypeStruct((sz.images, 8 * pairs, sz.length), wide),
        ],
        input_output_aliases={4 + k: k for k in range(len(before))},
        compiler_params=params(1),
        cost_estimate=cost(
            4 * sz.length * sz.length * sz.width,
            8 * sz.length * sz.width,
            sz.length * sz.length * HEADS,
        ),
        name=f"attend_{at}",
    )(meta, qkv, qkv, qkv, *before)


AHEAD = 6


def mlp_body(meta, x, att, vec, weight, res, n2, slope, act, enc, fin):
    @pl.when(pl.program_id(1) < meta[pl.program_id(0)])
    def _():
        width = x.shape[1]
        fold = slope.shape[1] // width

        def part_of(k):
            return weight[:, (AHEAD + k) * width : (AHEAD + k + 1) * width]

        branch = dot_nn(att[...], part_of(0)) + row_of(vec, ATTN_BIAS)
        rows = x[...].astype(wide) + branch
        res[...] = rows
        normal, _ = normalise(rows)
        normed = (normal * row_of(vec, NORM2_GAIN) + row_of(vec, NORM2_BIAS)).astype(low)
        n2[...] = normed
        total = rows + row_of(vec, FC2_BIAS)
        for part in range(fold):
            cols = slice(part * width, (part + 1) * width)
            u = dot_nn(normed, part_of(1 + part)) + row_of(vec, FC1_BIAS + part)
            square = u * u
            bend = jnp.tanh(root_two_pi * u * (1.0 + 0.044715 * square))
            half = 0.5 * (1.0 + bend)
            hidden = (u * half).astype(low)
            slope[:, cols] = (
                half
                + (0.5 * root_two_pi) * u * (1.0 - bend * bend) * (1.0 + 0.134145 * square)
            ).astype(low)
            act[:, cols] = hidden
            total = total + dot_nn(hidden, part_of(1 + fold + part))
        enc[...] = total
        normal, _ = normalise(total)
        fin[...] = (normal * row_of(vec, FINAL_GAIN) + row_of(vec, FINAL_BIAS)).astype(low)


def mlp_call(sz, meta, x, att, vec, weight):
    w, f = sz.width, sz.hidden
    return pl.pallas_call(
        mlp_body,
        grid_spec=pltpu.PrefetchScalarGridSpec(
            num_scalar_prefetch=1,
            grid=(sz.images, sz.blocks),
            in_specs=[sz.row_spec(w), sz.row_spec(w), whole(vec.shape), whole(weight.shape)],
            out_specs=[sz.row_spec(c) for c in (w, w, f, f, w, w)],
        ),
        out_shape=[
            jax.ShapeDtypeStruct((sz.rows, w), wide),
            jax.ShapeDtypeStruct((sz.rows, w), low),
            jax.ShapeDtypeStruct((sz.rows, f), low),
            jax.ShapeDtypeStruct((sz.rows, f), low),
            jax.ShapeDtypeStruct((sz.rows, w), wide),
            jax.ShapeDtypeStruct((sz.rows, w), low),
        ],
        compiler_params=params(2),
        cost_estimate=cost(
            sz.rows * w * (2 * w + 4 * f), sz.rows * (14 * w + 4 * f) + 4 * w * f, sz.rows * f
        ),
        name="mlp",
    )(meta, x, att, vec, weight)


HEAD_ROWS = 16


SENT_ROWS = 48
SENT_MIX, SENT_ACT, SENT_GRAD, SENT_NORMED, SENT_POOLED = 16, 32, 36, 40, 41
SENT_BRANCH, SENT_PULL, SENT_COT, SENT_OUT, SENT_OUT_REST = 42, 43, 44, 45, 46
SENT_QUERY, SENT_QUERY_REST = 47, 31


def head_body(
    images, blocks, fold, meta, fin, cot_ref, vec, pool_w, mine, theirs, rest,
    shares, g_score, lift, probe_out, sent, sums, score, mixed, line, held, sems,
):
    width = fin.shape[1]
    fetch_all(meta, 2 * images, (mine, theirs, rest), held, sems)
    keys_w, values_w, query_w, out_w, *late_w = (
        pool_w.at[:, k * width : (k + 1) * width] for k in range(AHEAD)
    )
    early = fold - len(late_w)

    def part_of(k):
        return columns(held, k * width, width)

    head_row = lax.broadcasted_iota(jnp.int32, (HEAD_ROWS, width), 0)
    head_col = lax.broadcasted_iota(jnp.int32, (HEAD_ROWS, width), 1) // HEAD_DIM
    own = head_row == head_col
    row_id = lax.broadcasted_iota(jnp.int32, (HEAD_ROWS, 1), 0)
    probe = jnp.broadcast_to(row_of(vec, PROBE), (HEAD_ROWS, width)).astype(low)
    query = (dot_nn(probe, query_w[...]) + row_of(vec, POOL_QUERY_BIAS)).astype(low)
    probe_w = 0.125 * dot_nt(jnp.where(own, query, jnp.zeros_like(query)), keys_w[...])
    probe_out[...] = jnp.where(row_id == HEADS, query.astype(wide), probe_w)
    probe_top, probe_rest = halves(probe_w)
    pooled_heads = jnp.zeros((HEAD_ROWS, width), wide)

    def block_rows(i, b):
        start = (i * blocks + b) * BLOCK
        return fin[start : start + BLOCK, :]

    for i in range(images):
        count, length = meta[i], meta[images + i]
        for b in range(blocks):
            cols = slice(b * BLOCK, (b + 1) * BLOCK)
            score[:, cols] = jnp.full((HEAD_ROWS, BLOCK), masked_score, wide)

            @pl.when(b < count)
            def _(i=i, b=b, cols=cols, length=length):
                rows = block_rows(i, b)
                value = dot_nt(probe_top, rows) + dot_nt(probe_rest, rows)
                column = lax.broadcasted_iota(jnp.int32, (HEAD_ROWS, BLOCK), 1) + b * BLOCK
                score[:, cols] = jnp.where(column < length, value, masked_score)

        raised = jnp.exp(score[...] - jnp.max(score[...], axis=1, keepdims=True))
        shares[i] = raised / jnp.sum(raised, axis=1, keepdims=True)
        mixed[i] = jnp.zeros((HEAD_ROWS, width), wide)
        for b in range(blocks):
            cols = slice(b * BLOCK, (b + 1) * BLOCK)

            @pl.when(b < count)
            def _(i=i, b=b, cols=cols):
                rows = block_rows(i, b)
                top, rest = halves(shares[i, :, cols])
                mixed[i] += dot_nn(top, rows) + dot_nn(rest, rows)

        top, rest = halves(mixed[i])
        sent[i * SENT_ROWS : i * SENT_ROWS + HEAD_ROWS, :] = top
        heads = dot_nn(top, values_w[...]) + dot_nn(rest, values_w[...])
        row = column_sum(jnp.where(own, heads, 0.0)) + row_of(vec, POOL_VALUE_BIAS)
        pooled_heads = jnp.where(row_id == i, row, pooled_heads)
    real = row_id < jnp.where(meta[0] > 0, images, 0)
    cot = jnp.where(real, cot_ref[...], 0.0)
    pooled_low = pooled_heads.astype(low)
    branch = dot_nn(pooled_low, out_w[...]) + row_of(vec, POOL_OUT_BIAS)
    normal, scale = normalise(branch)
    gain = row_of(vec, HEAD_GAIN)
    normed = (normal * gain + row_of(vec, HEAD_BIAS)).astype(low)
    cot_low = cot.astype(low)
    total = branch + row_of(vec, HEAD_FC2_BIAS)
    back = jnp.zeros((HEAD_ROWS, width), wide)

    def keep(at, value):
        for i in range(images):
            line[i, at - 2 * HEAD_ROWS : at + 1 - 2 * HEAD_ROWS, :] = value[i : i + 1, :].astype(wide)

    for part in range(fold):
        u = dot_nn(normed, part_of(part)) + row_of(vec, FC1_BIAS + fold + part)
        square = u * u
        bend = jnp.tanh(root_two_pi * u * (1.0 + 0.044715 * square))
        half = 0.5 * (1.0 + bend)
        act = (u * half).astype(low)
        slope = half + (0.5 * root_two_pi) * u * (1.0 - bend * bend) * (1.0 + 0.134145 * square)
        second = part_of(fold + part) if part < early else late_w[part - early][...]
        total = total + dot_nn(act, second)
        grad = jnp.where(real, dot_nt(cot_low, second) * slope, 0.0).astype(low)
        back = back + dot_nt(grad, part_of(part))
        keep(SENT_ACT + part, act)
        keep(SENT_GRAD + part, grad)
    sums[...] = jnp.zeros_like(sums)
    sums[0:1, :] = column_sum(jnp.where(real, back * normal, 0.0))
    sums[1:2, :] = column_sum(jnp.where(real, back, 0.0))
    branch_grad = jnp.where(real, cot + norm_back(back, gain, normal, scale), 0.0).astype(low)
    pull = dot_nt(branch_grad, out_w[...])
    keep(SENT_NORMED, normed)
    keep(SENT_POOLED, pooled_low)
    keep(SENT_BRANCH, branch_grad)
    keep(SENT_PULL, pull)
    keep(SENT_COT, cot_low)
    top, rest = halves(total)
    keep(SENT_OUT, top)
    keep(SENT_OUT_REST, rest)
    for i in range(images):
        top, rest = halves(jnp.where(own, pull[i : i + 1, :], 0.0))
        raised = dot_nt(top, values_w[...]) + dot_nt(rest, values_w[...])
        drop = jnp.sum(raised * mixed[i], axis=1, keepdims=True)
        lift[i] = raised
        lift_top, lift_rest = halves(raised)
        mixed[i] = jnp.zeros((HEAD_ROWS, width), wide)
        for b in range(blocks):
            cols = slice(b * BLOCK, (b + 1) * BLOCK)

            @pl.when(b < meta[i])
            def _(i=i, b=b, cols=cols):
                rows = block_rows(i, b)
                reach = dot_nt(lift_top, rows) + dot_nt(lift_rest, rows)
                grad = shares[i, :, cols] * (reach - drop)
                g_score[i, :, cols] = grad
                top, rest = halves(grad)
                mixed[i] += dot_nn(top, rows) + dot_nn(rest, rows)

        top, rest = halves(mixed[i])
        pulled = dot_nn(top, keys_w[...]) + dot_nn(rest, keys_w[...])
        query_grad = 0.125 * column_sum(jnp.where(own, pulled, 0.0))
        query_top, query_rest = halves(query_grad)
        line[i, HEAD_ROWS - 1 : HEAD_ROWS, :] = query_top.astype(wide)
        both = jnp.where(row_id == HEAD_ROWS - 1, query_rest.astype(wide), mixed[i])
        start = i * SENT_ROWS + HEAD_ROWS
        sent[start : start + HEAD_ROWS, :] = both.astype(low)
        sent[start + HEAD_ROWS : start + 2 * HEAD_ROWS, :] = line[i].astype(low)


def head_call(sz, meta, fin, cot, vec, block, weight):
    w, f, n = sz.width, sz.hidden, sz.images

    def out(shape, dtype):
        return jax.ShapeDtypeStruct(shape, dtype)

    shapes = [
        out((n, HEAD_ROWS, sz.length), wide),
        out((n, HEAD_ROWS, sz.length), wide),
        out((n, HEAD_ROWS, w), wide),
        out((HEAD_ROWS, w), wide),
        out((n * SENT_ROWS, w), low),
        out((8, w), wide),
    ]
    ins = (fin, cot, vec)
    return pl.pallas_call(
        functools.partial(head_body, sz.images, sz.blocks, f // w),
        grid_spec=pltpu.PrefetchScalarGridSpec(
            num_scalar_prefetch=1,
            grid=(1,),
            in_specs=[whole(v.shape) for v in ins]
            + [pl.BlockSpec((w, AHEAD * w), lambda *_: (0, 0), pipeline_mode=pl.Buffered(1))]
            + [anywhere] * 3,
            out_specs=[pl.BlockSpec(s.shape, lambda *_, r=len(s.shape): (0,) * r) for s in shapes],
            scratch_shapes=[
                pltpu.VMEM((HEAD_ROWS, sz.length), wide),
                pltpu.VMEM((n, HEAD_ROWS, w), wide),
                pltpu.VMEM((n, HEAD_ROWS, w), wide),
            ]
            + held_scratch(weight),
        ),
        out_shape=shapes,
        compiler_params=params(1),
        cost_estimate=cost(16 * 8 * w * f, sz.rows * w * 2 + 4 * w * f + 8 * w * w),
        name="head",
    )(meta, *ins, block, *weight)


def owner_body(own, fold, at, rows, probe, g_fc2, g_fc1, g_out, g_kv, sums, wide_rows, near, far):
    count, _, width = rows.shape
    group = HEAD_ROWS
    select = lax.broadcasted_iota(jnp.int32, (width, PAIR), 1)
    source = lax.broadcasted_iota(jnp.int32, (width, PAIR), 0)
    select = jnp.where((source == at[0] * own + select) & (select < own), 1.0, 0.0).astype(low)

    def rows_of(k):
        return rows[:, k * group : (k + 1) * group, :]

    def every(ref, r):
        return ref[pl.ds(r, count, stride=group), :].astype(low)

    def full(r):
        at_row = pl.ds(r - 2 * group, count, stride=group)
        return jnp.concatenate(
            [wide_rows[c, at_row, :] for c in range(width // PAIR)], axis=1
        ).astype(low)

    near[...] = dot_nn(rows_of(0).reshape(count * group, width), select)
    last = rows_of(2).reshape(count * group, width)
    far[...] = dot_nn(last, select)
    for c in range(width // PAIR):
        wide_rows[c] = last[:, c * PAIR : (c + 1) * PAIR].astype(wide)
    mixed = jnp.sum(rows_of(1).astype(wide), axis=0)
    sums[:group, :] = mixed
    sums[group:, :] = jnp.sum(rows_of(2).astype(wide), axis=0)
    cot = full(SENT_COT)
    normed = every(far, SENT_NORMED - 2 * group)
    for j in range(fold):
        g_fc2[j] = dot_tn(every(far, SENT_ACT + j - 2 * group), cot)[:own]
        g_fc1[:, j * width : (j + 1) * width] = dot_tn(normed, full(SENT_GRAD + j))[:own]
    g_out[...] = dot_tn(every(far, SENT_POOLED - 2 * group), full(SENT_BRANCH))[:own]
    pull = full(SENT_PULL)
    first = lax.broadcasted_iota(jnp.int32, (PAIR, PAIR), 1) < HEAD_DIM
    for p in range(width // PAIR):
        piece = pull[:, p * PAIR : (p + 1) * PAIR]
        both = [dot_tn(every(near, 2 * p + k), piece) for k in range(2)]
        at_cols = slice(width + p * PAIR, width + (p + 1) * PAIR)
        g_kv[:, at_cols] = jnp.where(first, both[0], both[1])[:own]
    head_row = lax.broadcasted_iota(jnp.int32, (group, width), 0)
    head_col = lax.broadcasted_iota(jnp.int32, (group, width), 1) // HEAD_DIM
    query = jnp.broadcast_to(probe[HEADS : HEADS + 1, :], (group, width))
    query = jnp.where(head_row == head_col, query, 0.0).astype(low)
    top, rest = halves(mixed)
    top, rest = halves(dot_nn(top, select) + dot_nn(rest, select))
    g_kv[:, :width] = 0.125 * (dot_tn(top, query) + dot_tn(rest, query))[:own]


def owner_call(at, rows, probe_w, own, fold):
    count, _, width = rows.shape
    shapes = [
        jax.ShapeDtypeStruct(shape, wide)
        for shape in (
            (fold, own, width), (own, fold * width), (own, width), (own, 2 * width),
            (2 * HEAD_ROWS, width),
        )
    ]
    return pl.pallas_call(
        functools.partial(owner_body, own, fold),
        grid_spec=pltpu.PrefetchScalarGridSpec(
            num_scalar_prefetch=1,
            grid=(1,),
            in_specs=[whole(rows.shape), whole(probe_w.shape)],
            out_specs=[pl.BlockSpec(s.shape, lambda *_, r=len(s.shape): (0,) * r) for s in shapes],
            scratch_shapes=[
                pltpu.VMEM((width // PAIR, count * HEAD_ROWS, PAIR), wide),
                pltpu.VMEM((count * HEAD_ROWS, PAIR), wide),
                pltpu.VMEM((count * HEAD_ROWS, PAIR), wide),
            ],
        ),
        out_shape=shapes,
        compiler_params=params(1),
        cost_estimate=cost(64 * count * width * PAIR, 8 * rows.size),
        name="owner",
    )(at, rows, probe_w)


def back_body(
    meta, fin, enc, res, att, slope, g_score, shares, lift, probe_w, spread, vec, weight,
    g_mlp, g_hidden, g_res, g_branch, g_att, delta, sums,
):
    @pl.when(is_first())
    def _():
        sums[...] = jnp.zeros_like(sums)

    @pl.when(pl.program_id(1) < meta[pl.program_id(0)])
    def _():
        width = fin.shape[1]
        fold = slope.shape[1] // width

        def part_of(k):
            return weight[:, (AHEAD + k) * width : (AHEAD + k + 1) * width]

        lift_top, lift_rest = halves(lift[0])
        probe_top, probe_rest = halves(probe_w[...])
        top, rest = halves(g_score[0])
        share_top, share_rest = halves(shares[0])
        left = jnp.concatenate([top, share_top, rest, share_rest, top, share_top], axis=0)
        right = jnp.concatenate(
            [probe_top, lift_top, probe_top, lift_top, probe_rest, lift_rest], axis=0
        )
        g_fin = dot_tn(left, right)
        normal, scale = normalise(enc[...])
        sums[0:1, :] += column_sum(g_fin * normal)
        sums[1:2, :] += column_sum(g_fin)
        g_enc = norm_back(g_fin, row_of(vec, FINAL_GAIN), normal, scale)
        low_enc = g_enc.astype(low)
        g_mlp[...] = low_enc
        sums[2:3, :] += column_sum(low_enc.astype(wide))
        back = jnp.zeros_like(g_enc)
        for part in range(fold):
            cols = slice(part * width, (part + 1) * width)
            grad = dot_nt(low_enc, part_of(1 + fold + part))
            grad = (grad * slope[:, cols].astype(wide)).astype(low)
            g_hidden[:, cols] = grad
            sums[8 + part : 9 + part, :] += column_sum(grad.astype(wide))
            back = back + dot_nt(grad, part_of(1 + part))
        normal, scale = normalise(res[...])
        sums[3:4, :] += column_sum(back * normal)
        sums[4:5, :] += column_sum(back)
        total = g_enc + norm_back(back, row_of(vec, NORM2_GAIN), normal, scale)
        g_res[...] = total
        low_res = total.astype(low)
        g_branch[...] = low_res
        sums[5:6, :] += column_sum(low_res.astype(wide))
        grad = dot_nt(low_res, part_of(0)).astype(low)
        g_att[...] = grad
        top, rest = halves(grad.astype(wide) * att[...].astype(wide))
        delta[0] = dot_nt(spread[...], top) + dot_nt(spread[...], rest)


def back_call(
    sz, meta, fin, enc, res, att, slope, g_score, shares, lift, probe_w, vec, weight
):
    w, f, n = sz.width, sz.hidden, sz.images
    lines = 8 * sz.pairs
    line = lax.broadcasted_iota(jnp.int32, (lines, w), 0)
    head = lax.broadcasted_iota(jnp.int32, (lines, w), 1) // HEAD_DIM
    spread = (head == 2 * (line // 8) + line % 8).astype(low)
    fixed = (probe_w, spread, vec, weight)

    def out(shape, dtype):
        return jax.ShapeDtypeStruct(shape, dtype)

    def kept(shape):
        return pl.BlockSpec(shape, lambda i, b, m: (0, 0))

    return pl.pallas_call(
        back_body,
        grid_spec=pltpu.PrefetchScalarGridSpec(
            num_scalar_prefetch=1,
            grid=(n, sz.blocks),
            in_specs=[
                sz.row_spec(w), sz.row_spec(w), sz.row_spec(w), sz.row_spec(w), sz.row_spec(f),
                sz.lane_spec(HEAD_ROWS), sz.lane_spec(HEAD_ROWS), sz.image_spec(HEAD_ROWS, w),
            ]
            + [whole(v.shape) for v in fixed],
            out_specs=[
                sz.row_spec(w), sz.row_spec(f), sz.row_spec(w), sz.row_spec(w), sz.row_spec(w),
                sz.lane_spec(lines), kept((16, w)),
            ],
        ),
        out_shape=[
            out((sz.rows, w), low), out((sz.rows, f), low), out((sz.rows, w), wide),
            out((sz.rows, w), low), out((sz.rows, w), low), out((n, lines, sz.length), wide),
            out((16, w), wide),
        ],
        compiler_params=params(2),
        cost_estimate=cost(
            sz.rows * w * (2 * w + 4 * f), sz.rows * (22 * w + 4 * f) + 4 * w * f
        ),
        name="mlp_back",
    )(meta, fin, enc, res, att, slope, g_score, shares, lift, *fixed)


def outer_body(images, blocks, units, meta, a_ref, b_ref, out_ref, acc):
    span = blocks * BLOCK

    def finish(term):
        if units == 0:
            out_ref[...] = term.astype(out_ref.dtype)
            return
        rows = term.shape[0] // units
        for u in range(units):
            out_ref[meta[2 * images + units + u]] = term[u * rows : (u + 1) * rows].astype(low)

    for i in range(images):
        for keys in range(blocks + 1):

            @pl.when(meta[i] == keys)
            def _(i=i, keys=keys):
                if keys:
                    rows = slice(i * span, i * span + keys * BLOCK)
                    term = dot_tn(a_ref[rows, :], b_ref[rows, :])
                else:
                    term = jnp.zeros(acc.shape, wide)
                if i > 0:
                    term = term + acc[...]
                if i < images - 1:
                    acc[...] = term
                else:
                    finish(term)


def outer_block_body(
    images, blocks, fold, meta, att_ref, g_att_ref, n2_ref, g_hidden_ref, act_ref, g_mlp_ref, out_ref, acc
):
    step = pl.program_id(0)
    for live, a_ref, b_ref in (
        (step == 0, att_ref, g_att_ref),
        ((step > 0) & (step <= fold), n2_ref, g_hidden_ref),
        (step > fold, act_ref, g_mlp_ref),
    ):
        pl.when(live)(
            functools.partial(outer_body, images, blocks, 0, meta, a_ref, b_ref, out_ref, acc)
        )


def outer_block_call(sz, meta, att, g_branch, n2, g_hidden, act, g_mlp):
    w, fold = sz.width, sz.hidden // sz.width
    one = whole((sz.rows, w))

    def part(first):
        return pl.BlockSpec((sz.rows, w), lambda j, c: (0, jnp.clip(j - first, 0, fold - 1)))

    return pl.pallas_call(
        functools.partial(outer_block_body, sz.images, sz.blocks, fold),
        grid_spec=pltpu.PrefetchScalarGridSpec(
            num_scalar_prefetch=1,
            grid=(1 + 2 * fold,),
            in_specs=[one, one, one, part(1), part(1 + fold), one],
            out_specs=pl.BlockSpec((w, w), lambda j, c: (0, j)),
            scratch_shapes=[pltpu.VMEM((w, w), wide)],
        ),
        out_shape=jax.ShapeDtypeStruct((w, (1 + 2 * fold) * w), low),
        compiler_params=params(1),
        cost_estimate=cost(2 * sz.rows * w * w * (1 + 2 * fold), 2 * sz.rows * w * (2 * fold + 4)),
        name="grad_block",
    )(meta, att, g_branch, n2, g_hidden, act, g_mlp)


def outer_qkv_body(images, blocks, units, meta, n1_ref, dq_ref, dk_ref, dv_ref, out_ref, acc):
    for k, b_ref in enumerate((dq_ref, dk_ref, dv_ref)):
        pl.when(pl.program_id(0) == k)(
            functools.partial(outer_body, images, blocks, units, meta, n1_ref, b_ref, out_ref, acc)
        )


def outer_qkv_call(sz, meta, n1, dq, dk, dv, units):
    w = sz.width
    return pl.pallas_call(
        functools.partial(outer_qkv_body, sz.images, sz.blocks, units),
        grid_spec=pltpu.PrefetchScalarGridSpec(
            num_scalar_prefetch=1,
            grid=(3,),
            in_specs=[whole((sz.rows, w))] * 4,
            out_specs=pl.BlockSpec((units, w // units, w), lambda j, c: (0, 0, j)),
            scratch_shapes=[pltpu.VMEM((w, w), wide)],
        ),
        out_shape=jax.ShapeDtypeStruct((units, w // units, 3 * w), low),
        compiler_params=params(1),
        cost_estimate=cost(6 * sz.rows * w * w, 8 * sz.rows * w),
        name="grad_qkv",
    )(meta, n1, dq, dk, dv)


def place_body(at, kept, taken, out):
    i = pl.program_id(0)

    @pl.when(at[2 * i] == 1)
    def _():
        out[...] = kept[0]

    @pl.when(at[2 * i] == 0)
    def _():
        out[...] = taken[...].astype(wide)


def place_call(at, kept, taken, groups, rows):
    width = kept.shape[-1]
    spec = pl.BlockSpec((1, rows, width), lambda i, at: (at[2 * i + 1], 0, 0))
    kept_spec = pl.BlockSpec(
        (1, 1, rows, width), lambda i, at: (at[2 * i + 1], at[2 * groups], 0, 0)
    )
    return pl.pallas_call(
        place_body,
        grid_spec=pltpu.PrefetchScalarGridSpec(
            num_scalar_prefetch=1,
            grid=(groups,),
            in_specs=[kept_spec, spec],
            out_specs=pl.BlockSpec((1, rows, width), lambda i, at: (i, 0, 0)),
        ),
        out_shape=jax.ShapeDtypeStruct((groups, rows, width), wide),
        compiler_params=params(1),
        cost_estimate=cost(0, groups * rows * width * 10),
        name="place",
    )(at, kept, taken)


def attend_back_body(
    images, blocks, meta, q_ref, k_ref, v_ref, g_ref, lse_ref, delta_ref, dq_ref, dk_ref, dv_ref,
    dk_acc, dv_acc,
):
    at = pl.program_id(0)
    count, length = meta[at], meta[images + at]
    lane = lax.broadcasted_iota(jnp.int32, (BLOCK, PAIR), 1)
    first = lane < HEAD_DIM

    def keep(value, head):
        own = first if head == 0 else jnp.logical_not(first)
        zero = jnp.zeros_like(value[:BLOCK])
        return jnp.concatenate(
            [
                jnp.where(own, value[r : r + BLOCK], zero)
                for r in range(0, value.shape[0], BLOCK)
            ],
            axis=0,
        )

    def variant(keys_in):
        near = keys_in - BLOCK
        keys = k_ref[:keys_in, :]
        kept_keys = [keep(keys, head) for head in range(2)]
        values = v_ref[:keys_in, :]
        kept_values = [keep(values, head) for head in range(2)]
        start = 0
        while start < keys_in:
            size = min(BACK_SPAN, keys_in - start)
            rows = slice(start, start + size)
            valid = lax.broadcasted_iota(jnp.int32, (BLOCK, size), 0) + near < length
            q, g = q_ref[rows, :], g_ref[rows, :]
            dq = dk = dv = None
            for head in range(2):
                log = lse_ref[0, head : head + 1, rows]
                drop = delta_ref[0, head : head + 1, rows]
                share = jnp.exp2(dot_nt(kept_keys[head], q) * score_scale - log)
                if near:
                    share = jnp.concatenate(
                        [share[:near], jnp.where(valid, share[near:], 0.0)], axis=0
                    )
                else:
                    share = jnp.where(valid, share, 0.0)
                reach = dot_nt(kept_values[head], g)
                grad = (share * (reach - drop)).astype(low)
                terms = (
                    dot_tn(grad, kept_keys[head]),
                    dot_nn(grad, keep(q, head)),
                    dot_nn(share.astype(low), keep(g, head)),
                )
                if head == 0:
                    dq, dk, dv = terms
                else:
                    dq, dk, dv = dq + terms[0], dk + terms[1], dv + terms[2]
            dq_ref[rows, :] = (dq * 0.125).astype(low)
            if start > 0:
                dk, dv = dk + dk_acc[:keys_in, :], dv + dv_acc[:keys_in, :]
            start += size
            if start < keys_in:
                dk_acc[:keys_in, :] = dk
                dv_acc[:keys_in, :] = dv
            else:
                dk_ref[:keys_in, :] = (dk * 0.125).astype(low)
                dv_ref[:keys_in, :] = dv.astype(low)

    for keys in range(1, blocks + 1):
        pl.when(count == keys)(functools.partial(variant, keys * BLOCK))


def attend_back_call(sz, meta, qkv, g_att, lse, delta):
    pairs = sz.pairs

    def spec(part):
        return pl.BlockSpec((sz.length, PAIR), lambda i, p, m: (i, part * pairs + p))

    line = pl.BlockSpec((1, 8, sz.length), lambda i, p, m: (i, p, 0))
    out = jax.ShapeDtypeStruct((sz.rows, sz.width), low)
    return pl.pallas_call(
        functools.partial(attend_back_body, sz.images, sz.blocks),
        grid_spec=pltpu.PrefetchScalarGridSpec(
            num_scalar_prefetch=1,
            grid=(sz.images, pairs),
            in_specs=[spec(0), spec(1), spec(2), spec(0), line, line],
            out_specs=[spec(0), spec(0), spec(0)],
            scratch_shapes=[pltpu.VMEM((sz.length, PAIR), wide)] * 2,
        ),
        out_shape=[out, out, out],
        compiler_params=params(2),
        cost_estimate=cost(
            10 * sz.rows * sz.length * sz.width,
            14 * sz.rows * sz.width,
            sz.rows * sz.length * HEADS,
        ),
        name="attend_back",
    )(meta, qkv, qkv, qkv, g_att, lse, delta)


def qkv_back_body(
    base, meta, x, g_res, dq, dk, dv, vec, mine, theirs, grad_ref, low_ref, sums, held, sems
):
    @pl.when(is_first())
    def _():
        fetch_all(meta, base, (mine, theirs), held, sems)
        sums[...] = jnp.zeros_like(sums)

    live = pl.program_id(1) < meta[pl.program_id(0)]

    @pl.when(live)
    def _():
        width = x.shape[1]
        normal, scale = normalise(x[...].astype(wide))
        back = None
        for part, ref in enumerate((dq, dk, dv)):
            term = dot_nt(ref[...], columns(held, part * width, width))
            back = term if back is None else back + term
        sums[0:1, :] += column_sum(back * normal)
        sums[1:2, :] += column_sum(back)
        sums[2:3, :] += column_sum(dq[...].astype(wide))
        sums[3:4, :] += column_sum(dv[...].astype(wide))
        grad = g_res[...] + norm_back(back, row_of(vec, NORM1_GAIN), normal, scale)
        grad_ref[...] = grad
        low_ref[...] = grad.astype(low)

    @pl.when(jnp.logical_not(live))
    def _():
        grad_ref[...] = jnp.zeros_like(grad_ref)
        low_ref[...] = jnp.zeros_like(low_ref)


def qkv_back_call(sz, meta, x, g_res, dq, dk, dv, vec, weight):
    w, blocks = sz.width, sz.blocks
    plain = pl.BlockSpec((BLOCK, w), lambda i, b, m: (i * blocks + b, 0))
    return pl.pallas_call(
        functools.partial(qkv_back_body, 2 * sz.images),
        grid_spec=pltpu.PrefetchScalarGridSpec(
            num_scalar_prefetch=1,
            grid=(sz.images, blocks),
            in_specs=[sz.row_spec(w)] * 5 + [whole(vec.shape), anywhere, anywhere],
            out_specs=[plain, plain, pl.BlockSpec((8, w), lambda i, b, m: (0, 0))],
            scratch_shapes=held_scratch(weight),
        ),
        out_shape=[
            jax.ShapeDtypeStruct((sz.rows, w), wide),
            jax.ShapeDtypeStruct((sz.rows, w), low),
            jax.ShapeDtypeStruct((8, w), wide),
        ],
        compiler_params=params(2),
        cost_estimate=cost(6 * sz.rows * w * w, sz.rows * w * 18 + 6 * w * w),
        name="qkv_back",
    )(meta, x, g_res, dq, dk, dv, vec, *weight)


axes = ("img", "seq")


def bits_of(count):
    return [1 << k for k in range(count.bit_length() - 1)]


def tied(value, *after):
    return lax.optimization_barrier((value, *after))[0]


def together(*values):
    return lax.optimization_barrier(values)


def cut(size, shares):
    edges = [round(size * sum(shares[:k]) / sum(shares) / 16) * 16 for k in range(len(shares) + 1)]
    return [slice(p, q) for p, q in zip(edges[:-1], edges[1:], strict=True)]


class Wires:
    def __init__(self, img_count, seq_count):
        self.count, self.seq_count = img_count * seq_count, seq_count
        self.core = seq_count
        self.units = img_count
        self.seq_bits = bits_of(seq_count)
        inner = [bit for bit in bits_of(self.count) if bit > self.core]
        inner = inner[:1] + inner[:0:-1]
        self.orders = (inner, inner[1:] + inner[:1])

    def swap(self, value, bit):
        return lax.ppermute(value, axes, [(i, i ^ bit) for i in range(self.count)])

    def step(self, value, at):
        pairs = [(i, i ^ self.orders[1 if i & self.core else 0][at]) for i in range(self.count)]
        return lax.ppermute(value, axes, pairs)

    def tables(self, me):
        img = me // self.seq_count
        core = img % 2

        def at(place, side):
            by_core = []
            for order in self.orders:
                unit = 0
                for k, bit in enumerate(order):
                    unit |= ((place >> k) & 1) * (bit // self.seq_count)
                by_core.append(unit)
            which = core if side == 0 else 1 - core
            return (img ^ side) ^ jnp.where(which == 0, by_core[0], by_core[1])

        def place(unit):
            side = (unit ^ img) & 1
            delta = unit ^ img
            by_core = []
            for order in self.orders:
                total = jnp.zeros((), jnp.int32)
                for k, bit in enumerate(order):
                    shift = (bit // self.seq_count).bit_length() - 1
                    total = total | (((delta >> shift) & 1) << k)
                by_core.append(total)
            which = core ^ side
            return side * (self.units // 2) + jnp.where(which == 0, by_core[0], by_core[1])

        half = self.units // 2
        order = [at(k, side) for side in range(2) for k in range(half)]
        inverse = [place(unit) for unit in range(self.units)]
        return jnp.stack(order + inverse)

    def join_seq(self, value, me):
        for bit in self.seq_bits:
            other = self.swap(value, bit)
            value = jnp.where(
                (me & bit) > 0,
                jnp.concatenate([other, value], axis=0),
                jnp.concatenate([value, other], axis=0),
            )
        return value

    def joined(self, value, at):
        return jnp.concatenate([value, self.step(value, at)], axis=0)

    def halved(self, value, at):
        half = value.shape[0] // 2
        return value[:half] + self.step(value[half:], at)

    def small_scatter(self, value, me, bits):
        for bit in reversed(bits):
            value = self.small_half(value, me, bit)
        return value[0]

    def small_half(self, value, me, bit):
        pair = value.reshape((2, value.shape[0] // 2) + value.shape[1:])
        up = (me & bit) > 0
        return jnp.where(up, pair[1], pair[0]) + self.swap(jnp.where(up, pair[0], pair[1]), bit)


def local(img_count, seq_count, *args):
    (
        patches, lengths, pooled_cot, norm1_gain, norm1_bias, qkv_weight, query_bias, value_bias,
        attn_weight, attn_bias, norm2_gain, norm2_bias, fc1_weight, fc1_bias, fc2_weight, fc2_bias,
        final_gain, final_bias, probe_vector, pool_query_weight, pool_query_bias, pool_kv_weight,
        pool_value_bias, pool_out_weight, pool_out_bias, head_gain, head_bias, head_fc1_weight,
        head_fc1_bias, head_fc2_weight, head_fc2_bias,
    ) = args
    count = img_count * seq_count
    groups, part_rows, width = patches.shape
    length = part_rows * seq_count
    hidden = fc1_weight.shape[1]
    images = max(1, groups // seq_count)
    share = max(1, seq_count // groups)
    own = width // count
    per = hidden // count
    fold = hidden // width
    sz = Sizes(images, length, width, hidden)
    wires = Wires(img_count, seq_count)
    me = lax.axis_index(axes)
    seq_at = lax.axis_index("seq")
    first_image = (seq_at // share) * images

    slots = list(range(groups))
    if share == 1:
        turn = [r % seq_count if (r // seq_count) % 2 == 0 else -1 - r % seq_count for r in slots]
        slots = [(t % seq_count) * images + r // seq_count for r, t in zip(slots, turn, strict=True)]
        ahead = (lengths[None, :] > lengths[:, None]) | (
            (lengths[None, :] == lengths[:, None])
            & (jnp.arange(groups)[None, :] < jnp.arange(groups)[:, None])
        )
        rank = jnp.sum(ahead, axis=1)
        slot_of = sum(jnp.where(rank == r, slot, 0) for r, slot in enumerate(slots))
    else:
        slot_of = jnp.arange(groups)
    order = jnp.sum(
        jnp.where(slot_of[None, :] == jnp.arange(groups)[:, None], jnp.arange(groups)[None, :], 0),
        axis=1,
    )

    def of_slots(value, first):
        at = lax.dynamic_slice_in_dim(order, first, images)
        return jnp.concatenate(
            [lax.dynamic_slice_in_dim(value, at[k], 1) for k in range(images)], axis=0
        )

    own_lengths = of_slots(lengths, first_image)
    own_lengths = jnp.where(seq_at % share == 0, own_lengths, 0)
    own_cot = of_slots(pooled_cot, first_image)
    meta = jnp.concatenate(
        [(own_lengths + BLOCK - 1) // BLOCK, own_lengths, wires.tables(me)]
    ).astype(jnp.int32)

    def by_unit(bias):
        return bias.reshape(own, fold).T

    vectors = [
        v.reshape(1, own)
        for v in (
            norm1_gain, norm1_bias, query_bias, value_bias, attn_bias, norm2_gain, norm2_bias,
            fc2_bias, final_gain, final_bias, pool_query_bias, pool_value_bias, pool_out_bias,
            head_gain, head_bias, head_fc2_bias, probe_vector,
        )
    ]
    vectors += [by_unit(fc1_bias), by_unit(head_fc1_bias)]
    unit_a, block, pack = packs_call(
        vectors, qkv_weight, pool_kv_weight, pool_query_weight, attn_weight, fc1_weight, fc2_weight,
        pool_out_weight, head_fc1_weight, head_fc2_weight,
    )
    block = lax.all_gather(block, axes, axis=0, tiled=True)

    pairwise = seq_count == 2 and share == 1
    steps = len(wires.orders[0])
    if pairwise:
        kept = of_slots(patches, first_image)
        given = of_slots(patches, (1 - seq_at) * images)
        parts = cut(part_rows, list(range(2, steps + 2)))
    else:
        ordered = jnp.concatenate(
            [lax.dynamic_slice_in_dim(patches, order[k], 1) for k in range(groups)], axis=0
        )
        given = jnp.repeat(ordered, share, axis=0)
    mine = wires.join_seq(unit_a, me)[None]
    mine, given = together(mine, given)
    taken = []
    for at in range(steps):
        mine = wires.joined(mine, at)
        if pairwise:
            mine, one = together(mine, wires.swap(given[:, parts[at]], 1))
            taken.append(one)
        if at == 1:
            mine, meta = together(mine, meta)
    mine, pack = together(mine, pack)
    theirs = wires.swap(mine, wires.core)
    theirs, pack = together(theirs, pack)
    qkv_full = (mine, theirs)
    if pairwise:
        taken = jnp.concatenate(taken, axis=1)
        x = jnp.where(
            seq_at == 0,
            jnp.concatenate([kept, taken], axis=1),
            jnp.concatenate([taken, kept], axis=1),
        )
    else:
        x = lax.all_to_all(given, "seq", split_axis=0, concat_axis=1, tiled=True)
    x = x.reshape(sz.rows, width)

    qkv, n1, vec = qkv_call(sz, meta, x, qkv_full)
    pack = wires.join_seq(pack, me)[None]
    qkv, pack = together(qkv, pack)
    done, forward = 0, ()
    for at in range(images):
        forward = attend_call(sz, meta, qkv, at, forward)
        stop = steps - 1 if at == images - 1 else min(done + 1, steps - 1)
        while done < stop:
            pack = wires.joined(pack, done)
            done += 1
        *forward, pack = together(*forward, pack)
    att, lse = forward
    res, n2, slope, act, enc, fin = mlp_call(sz, meta, x, att, vec, block)
    other = wires.swap(pack, wires.core)
    pack_rest = wires.step(pack, steps - 1)
    fin, other, pack_rest = together(fin, other, pack_rest)
    other_rest = wires.swap(pack_rest, wires.core)
    head_full = (jnp.concatenate([pack, pack_rest], axis=0), other, other_rest)
    cot_rows = jnp.pad(own_cot, ((0, HEAD_ROWS - images), (0, 0)))
    shares, g_score, lift, probe_w, sent, head_sums = head_call(
        sz, meta, fin, cot_rows, vec, block, head_full
    )
    rows = lax.all_gather(sent, axes, axis=0, tiled=True)

    g_mlp, g_hidden, g_res, g_branch, g_att, delta, back_sums = back_call(
        sz, meta, fin, enc, res, att, slope, g_score, shares, lift, probe_w, vec, block
    )
    terms = outer_block_call(sz, meta, att, g_branch, n2, g_hidden, act, g_mlp)
    terms, g_att, rows = together(terms, g_att, rows)
    totals = lax.psum_scatter(terms, axes, scatter_dimension=0, tiled=True)

    def by_column(grad):
        return grad.reshape(own, fold, width).transpose(0, 2, 1).reshape(own, hidden)

    def own_part(v, axis=-1):
        return lax.dynamic_slice_in_dim(v, me * own, own, axis=axis)

    half = wires.units // 2
    dq, dk, dv = attend_back_call(sz, meta, qkv, g_att, lse, delta)
    last = outer_qkv_call(sz, meta, n1, dq, dk, dv, wires.units)
    g_res, last = together(g_res, last)
    last = last[:half] + wires.swap(last[half:], wires.core)
    patch_grad, patch_low, qkv_sums = qkv_back_call(sz, meta, x, g_res, dq, dk, dv, vec, qkv_full)
    patch_low = patch_low.reshape(images, length, width)
    sums = jnp.concatenate(
        [back_sums[:6], head_sums[:2], qkv_sums[:4], back_sums[8 : 8 + fold]], axis=0
    )
    sums = sums.reshape(-1, count, own).transpose(1, 0, 2)
    if pairwise:
        given = lax.dynamic_slice_in_dim(patch_low, (1 - seq_at) * part_rows, part_rows, axis=1)
    else:
        given = lax.all_to_all(patch_low, "seq", split_axis=1, concat_axis=0, tiled=True)[::share]

    def head_part(rows):
        rows = rows.reshape(count * images, SENT_ROWS, width)
        return owner_call(me[None].astype(jnp.int32), rows, probe_w, own, fold)

    def sums_part(rows, row_sums):
        rows = lax.dynamic_slice_in_dim(
            rows.reshape(img_count, seq_count, images, SENT_ROWS, width), me // seq_count, 1
        )[0, ::share]
        query_grad = row_sums[SENT_QUERY - HEAD_ROWS] + row_sums[SENT_QUERY_REST - HEAD_ROWS]
        pooled = rows[:, :, SENT_OUT].astype(wide) + rows[:, :, SENT_OUT_REST].astype(wide)
        pooled = pooled.reshape(groups, width)
        pooled = jnp.concatenate(
            [lax.dynamic_slice_in_dim(pooled, slot_of[k], 1) for k in range(groups)], axis=0
        )
        return (
            pooled,
            probe_vector.astype(wide)[:, None] * query_grad[None, :],
            jnp.sum(pool_query_weight.astype(wide) * query_grad[None, :], axis=1),
            own_part(query_grad),
            own_part(row_sums),
        )

    last, sums, given, rows = together(last, sums, given, rows)
    parts, taken, made = cut(part_rows, (1,) * steps), [], []
    bits = list(reversed(bits_of(count)))
    for tick, at in enumerate(reversed(range(steps))):
        last = wires.halved(last, at)
        sums = wires.small_half(sums, me, bits.pop(0))
        taken.append(wires.swap(given[:, parts[tick]], 1) if pairwise else given)
        if tick == 0:
            made.append(head_part(rows))
        elif tick == 1:
            made.append(sums_part(rows, made[0][4]))
        last, sums, rows, taken, made = together(last, sums, rows, taken, made)
    (grad_head_fc2, grad_head_fc1, grad_pool_out, grad_pool_kv, _), made = made
    grad_head_fc2 = grad_head_fc2.transpose(1, 0, 2).reshape(per, width)
    grad_head_fc1 = by_column(grad_head_fc1)
    pooled, grad_pool_query_weight, grad_probe, g_pool_query_bias, own_sums = made

    def own_sum(at):
        return own_sums[at - HEAD_ROWS]

    g_head_fc1_bias = own_sums[SENT_GRAD - HEAD_ROWS :][:fold].T.reshape(per)
    last = last.reshape(seq_count, own, 3 * width)
    for bit in reversed(wires.seq_bits):
        last = wires.small_half(last, me, bit)
    while bits:
        sums = wires.small_half(sums, me, bits.pop(0))
    if pairwise:
        at_slot = jnp.stack(
            [(slot_of // images == seq_at).astype(jnp.int32), slot_of % images], axis=1
        )
        at_slot = jnp.concatenate([at_slot.reshape(-1), seq_at[None]]).astype(jnp.int32)
        patch_grad = place_call(
            at_slot,
            patch_grad.reshape(images, seq_count, part_rows, width),
            jnp.concatenate(taken, axis=1),
            groups,
            part_rows,
        )
    else:
        patch_grad = jnp.concatenate(
            [lax.dynamic_slice_in_dim(taken[0], slot_of[k], 1) for k in range(groups)], axis=0
        ).astype(wide)
    totals = totals.astype(wide)
    grad_attn = totals[:, :width]
    grad_fc1 = by_column(totals[:, width : width + hidden])
    grad_fc2 = totals[:, width + hidden :].reshape(per, width)
    grad_qkv = last[0].astype(wide)
    sums = sums[0]
    (
        g_final_gain, g_final_bias, g_fc2_bias, g_norm2_gain, g_norm2_bias, g_attn_bias,
        g_head_gain, g_head_bias, g_norm1_gain, g_norm1_bias, g_query_bias, g_value_bias,
    ) = sums[:12]
    g_fc1_bias = sums[12:].T.reshape(per)
    return (
        pooled, patch_grad, g_norm1_gain, g_norm1_bias, grad_qkv, g_query_bias, g_value_bias,
        grad_attn, g_attn_bias, g_norm2_gain, g_norm2_bias, grad_fc1, g_fc1_bias, grad_fc2,
        g_fc2_bias, g_final_gain, g_final_bias, grad_probe, grad_pool_query_weight,
        g_pool_query_bias, grad_pool_kv, own_sum(SENT_PULL), grad_pool_out,
        own_sum(SENT_BRANCH), g_head_gain, g_head_bias, grad_head_fc1,
        g_head_fc1_bias, grad_head_fc2, own_sum(SENT_COT),
    )


def solution(mesh):
    rows, vector = P(axes, None), P(axes)
    body = functools.partial(local, mesh.shape["img"], mesh.shape["seq"])
    vector_weights = (3, 4, 6, 7, 9, 10, 11, 13, 15, 16, 17, 18, 20, 22, 24, 25, 26, 28, 30)
    in_specs = (P("img", "seq", None), P("img"), P("img", None)) + tuple(
        vector if at in vector_weights else rows for at in range(3, 31)
    )
    out_specs = (P("img", None), P("img", "seq", None)) + in_specs[3:]
    return jax.shard_map(body, mesh=mesh, in_specs=in_specs, out_specs=out_specs, check_vma=False)
```
